32 devices in a mesh: dp: 16 (over z, x, core), tensor: 2 (over y).
Axes of the slice: x: 2, y: 2, z: 4, core: 2. Of those that a mesh axis runs over, the one named last changes fastest.
Arguments:
- tokens: bfloat16 [6144, 1024], P(('dp', 'tensor')), may hold values from -6 to 6
- cotangent: bfloat16 [6144, 1024], P(('dp', 'tensor')), may hold values from -6 to 6
- seq_lengths: int32 [16, 8], P('dp'), may hold values from 0 to 384, as said below
- norm1_gain: float32 [1024], replicated, may hold values from 0.5 to 1.5
- norm2_gain: float32 [1024], replicated, may hold values from 0.5 to 1.5
- mixer_in: bfloat16 [1024, 2, 1536], P(None, None, 'tensor'), may hold values from -0.1875 to 0.1875
- state_in: bfloat16 [1024, 256], replicated, may hold values from -0.1875 to 0.1875
- step_in: bfloat16 [1024, 24], P(None, 'tensor'), may hold values from -0.375 to 0.375
- conv_inner: float32 [4, 1536], P(None, 'tensor'), may hold values from -3 to 3
- conv_state: float32 [4, 256], replicated, may hold values from -3 to 3
- step_bias: float32 [24], P('tensor'), may hold values from -4 to -2
- decay_log: float32 [24], P('tensor'), may hold values from -3 to 0.5
- skip_gain: float32 [24], P('tensor'), may hold values from 0.5 to 1.5
- mixer_out: bfloat16 [1024, 1536], P(None, 'tensor'), may hold values from -0.4375 to 0.4375
- query_in: bfloat16 [1024, 512], P(None, 'tensor'), may hold values from -0.1875 to 0.1875
- key_value: bfloat16 [1024, 2, 128], replicated, may hold values from -0.1875 to 0.1875
- attend_out: bfloat16 [1024, 512], P(None, 'tensor'), may hold values from -2 to 2
- gate_up: bfloat16 [1024, 2, 2048], P(None, None, 'tensor'), may hold values from -0.1875 to 0.1875
- down_out: bfloat16 [1024, 2048], P(None, 'tensor'), may hold values from -0.125 to 0.125
Outputs:
- block_out: bfloat16 [6144, 1024], P(('dp', 'tensor'))
- token_grad: bfloat16 [6144, 1024], P(('dp', 'tensor'))
- grad_norm1: float32 [1024], replicated
- grad_norm2: float32 [1024], replicated
- grad_mixer_in: float32 [1024, 2, 1536], P('dp', None, 'tensor')
- grad_state_in: float32 [1024, 256], P('dp')
- grad_step_in: float32 [1024, 24], P('dp', 'tensor')
- grad_conv_inner: float32 [4, 1536], P(None, 'tensor')
- grad_conv_state: float32 [4, 256], replicated
- grad_step_bias: float32 [24], P('tensor')
- grad_decay_log: float32 [24], P('tensor')
- grad_skip_gain: float32 [24], P('tensor')
- grad_mixer_out: float32 [1024, 1536], P('dp', 'tensor')
- grad_query_in: float32 [1024, 512], P('dp', 'tensor')
- grad_key_value: float32 [1024, 2, 128], P('dp')
- grad_attend_out: float32 [1024, 512], P('dp', 'tensor')
- grad_gate_up: float32 [1024, 2, 2048], P('dp', None, 'tensor')
- grad_down_out: float32 [1024, 2048], P('dp', 'tensor')
The draws below stay inside these ranges and needn't reach their ends.
Inputs may be any that keep to these rules, and one draw needn't show every extreme that they name: `seq_lengths`: row g lists the lengths of the sequences of data group g in the order they lie in its 384 slots, then zeros; a row has 1 to 8 sequences and its lengths sum to at least 192; in some row one sequence fills all 384 slots.
All inputs are finite; a program needn't handle non-finite values.
Results may differ from the reference program's by a relative error of at most 0.018.
Values may be sent and summed in bfloat16 or wider, within the bound.
No kernel may reach another device: no remote copies, remote signals or barrier semaphores. Data moves between devices by JAX's collectives and lax.ppermute only.
A program may use at most 128 MiB of HBM per device.

```python
import jax
import jax.numpy as jnp
from jax import lax

D = 1024
MH = 24
HD = 64
NS = 128
KC = 4
QH = 8
KVH = 2
FF = 2048
TOK_DEV = 384
SLOTS = 8
SPAN = 128
ATT_ROWS = 384
TOKENS = 6144
N_DP = 16
N_TENSOR = 2


def one_row(key, is_whole):
    key_used, key_count, key_order = jax.random.split(key, 3)
    used_slots = jnp.where(is_whole, TOK_DEV, jax.random.randint(key_used, (), TOK_DEV // 2, TOK_DEV + 1)).astype(jnp.int32)
    number = jnp.where(is_whole, 1, jax.random.randint(key_count, (), 2, SLOTS + 1)).astype(jnp.int32)
    places = jnp.arange(1, TOK_DEV, dtype=jnp.int32)
    shuffled = jax.random.permutation(key_order, TOK_DEV - 1).astype(jnp.int32)
    priority = jnp.where(places < used_slots, shuffled, TOK_DEV + places)
    picked = places[jnp.argsort(priority, stable=True)[:SLOTS - 1]]
    slot_index = jnp.arange(SLOTS - 1, dtype=jnp.int32)
    cut_points = jnp.sort(jnp.where(slot_index < number - 1, picked, used_slots))
    bounds = jnp.concatenate([jnp.zeros((1,), jnp.int32), cut_points, used_slots[None]])
    return (bounds[1:] - bounds[:-1]).astype(jnp.int32)


def draw_seq_lengths(key, part):
    key = jax.random.fold_in(key, 7)
    key_whole, key_rows = jax.random.split(key)
    whole_row = jax.random.randint(key_whole, (), 0, N_DP)
    row_keys = jax.random.split(key_rows, N_DP)
    row_index = jnp.arange(N_DP)
    return jax.vmap(one_row)(row_keys, row_index == whole_row)


def level_of(rng, extent, shards, least, top_value):
    level = 1.0
    for axis_at, parts in shards:
        heights = jax.random.uniform(jax.random.fold_in(jax.random.fold_in(rng, 6), axis_at), (parts,), jnp.float32, least / len(shards), top_value / len(shards))
        level = level * jnp.repeat(jnp.exp(heights), extent[axis_at] // parts).reshape((-1,) + (1,) * (len(extent) - 1 - axis_at))
    return level


def gaussian(own_key, shape, deviation, most, cuts=(), held_as=jnp.bfloat16):
    loudness = level_of(own_key, shape, cuts, -0.22, 0.18) if cuts else 1.0
    values = jax.random.normal(own_key, shape, jnp.float32) * deviation * loudness
    return jnp.minimum(jnp.maximum(values, -most), most).astype(held_as)


def setup_inputs(seed: int = 0) -> dict:
    seeds = jax.random.split(jax.random.key(seed), 20)
    return {
        "tokens": gaussian(seeds[0], (TOKENS, D), 1.0, 6.0, ((0, 32),)),
        "cotangent": gaussian(seeds[1], (TOKENS, D), 1.0, 6.0, ((0, 32),)),
        "seq_lengths": draw_seq_lengths(jax.random.fold_in(seeds[19], 71), 0),
        "norm1_gain": jnp.clip(1.0 + 0.1 * jax.random.normal(seeds[3], (D,), jnp.float32), 0.5, 1.5),
        "norm2_gain": jnp.clip(1.0 + 0.1 * jax.random.normal(seeds[4], (D,), jnp.float32), 0.5, 1.5),
        "mixer_in": gaussian(seeds[5], (D, 2, MH * HD), D ** -0.5, 0.1875, ((2, 2),)),
        "state_in": gaussian(seeds[6], (D, 2 * NS), D ** -0.5, 0.1875),
        "step_in": gaussian(seeds[7], (D, MH), (D // 4) ** -0.5, 0.375, ((1, 2),)),
        "conv_inner": gaussian(seeds[8], (KC, MH * HD), KC ** -0.5, 3.0, ((1, 2),), jnp.float32),
        "conv_state": gaussian(seeds[9], (KC, 2 * NS), KC ** -0.5, 3.0, (), jnp.float32),
        "step_bias": jnp.clip(-4.0 + 2.0 * jax.random.uniform(seeds[10], (MH,), jnp.float32) ** level_of(seeds[10], (MH,), ((0, 2),), -0.2, 0.2), -4.0, -2.0),
        "decay_log": jnp.clip(-3.0 + 3.5 * jax.random.uniform(seeds[11], (MH,), jnp.float32) ** level_of(seeds[11], (MH,), ((0, 2),), -0.2, 0.2), -3.0, 0.5),
        "skip_gain": jnp.clip(0.5 + 1.0 * jax.random.uniform(seeds[12], (MH,), jnp.float32) ** level_of(seeds[12], (MH,), ((0, 2),), -0.2, 0.2), 0.5, 1.5),
        "mixer_out": gaussian(seeds[13], (D, MH * HD), (MH * HD // 8) ** -0.5, 0.4375, ((1, 2),)),
        "query_in": gaussian(seeds[14], (D, QH * HD), D ** -0.5, 0.1875, ((1, 2),)),
        "key_value": gaussian(seeds[15], (D, 2, KVH * HD), D ** -0.5, 0.1875),
        "attend_out": gaussian(seeds[16], (D, QH * HD), (QH * HD // 64) ** -0.5, 2.0, ((1, 2),)),
        "gate_up": gaussian(seeds[17], (D, 2, FF), D ** -0.5, 0.1875, ((2, 2),)),
        "down_out": gaussian(seeds[18], (D, FF), FF ** -0.5, 0.125, ((1, 2),)),
    }


rope_base = 100000000000.0
norm_eps = 1e-05
highest = lax.Precision.HIGHEST

@jax.custom_vjp
def low(v):
    return lax.optimization_barrier(v.astype(jnp.bfloat16)).astype(jnp.float32)

@jax.custom_vjp
def low_back(v):
    return v

def low_keep(v):
    return (low(v), None)

def low_pass(kept, grad):
    return (grad,)

def back_keep(v):
    return (v, None)

def back_low(kept, grad):
    return (low(grad),)
low.defvjp(low_keep, low_pass)
low_back.defvjp(back_keep, back_low)

def matmul_hi(left, right):
    return jnp.dot(left, right, precision=highest)

def segments(lengths, row_count):
    seq_ends = jnp.cumsum(lengths).astype(jnp.int32)
    places = jnp.arange(row_count, dtype=jnp.int32)
    passed = places[:, None] >= seq_ends[None, :]
    seq_ids = lax.optimization_barrier(jnp.sum(passed.astype(jnp.int32), axis=1)).astype(jnp.int32)
    starts = lax.optimization_barrier(jnp.max(jnp.where(passed, seq_ends[None, :], 0), axis=1)).astype(jnp.int32)
    is_live = (places < seq_ends[-1]).astype(jnp.float32)
    return (seq_ids, places - starts, is_live)

def rms_scale(values, gain):
    factor = lax.rsqrt(lax.optimization_barrier(jnp.mean(values * values, axis=-1, keepdims=True)) + norm_eps)
    return values * factor * gain

def rotate(vectors, positions, sign):
    half_width = vectors.shape[-1] // 2
    frequency = rope_base ** (-2.0 * jnp.arange(half_width, dtype=jnp.float32) / vectors.shape[-1])
    angles = positions.astype(jnp.float32)[:, None, None] * frequency[None, None, :]
    cosine = jnp.cos(angles)
    sine_table = jnp.sin(angles)
    first_half = vectors[..., :half_width]
    second_half = vectors[..., half_width:]
    return jnp.concatenate([first_half * cosine - sign * second_half * sine_table, second_half * cosine + sign * first_half * sine_table], axis=-1)

def causal_conv(values, weight, seq_ids):
    row_count = values.shape[0]
    kernel_len = weight.shape[0]
    running = jnp.zeros(values.shape, jnp.float32)
    for tap_index in range(kernel_len):
        offset = kernel_len - 1 - tap_index
        shifted = jnp.pad(values, ((offset, 0), (0, 0)))[:row_count]
        owner_ids = jnp.pad(seq_ids, (offset, 0), constant_values=-1)[:row_count]
        running = running + jnp.where((owner_ids == seq_ids)[:, None], shifted, 0.0) * weight[tap_index][None, :]
    return running

def state_scan(inner_x, step_sizes, state_b, state_c, decay_rates, seq_ids, block_len):
    row_count, head_count, head_dim = inner_x.shape
    blocks = row_count // block_len
    prior_ids = jnp.concatenate([jnp.full((1,), -1, jnp.int32), seq_ids[:-1]])
    within = jnp.arange(block_len, dtype=jnp.int32)
    causal = within[:, None] >= within[None, :]

    def advance(carried, pieces):
        inner_b, steps_b, keys_b, reads_b, ids_b, before = pieces
        log_decay = jnp.cumsum(-steps_b * decay_rates[None, :], axis=0)
        linked = (ids_b[:, None] == ids_b[None, :]) & causal
        decays = jnp.exp(jnp.where(linked[:, :, None], log_decay[:, None, :] - log_decay[None, :, :], -jnp.inf))
        intersection = jnp.dot(reads_b, keys_b.T, precision=highest)
        mixing = intersection[:, :, None] * decays * steps_b[None, :, :]
        inside = jnp.einsum('ijh,jhp->ihp', mixing, inner_b, precision=highest)
        keeps_state = (ids_b == before).astype(jnp.float32)
        from_state = jnp.einsum('in,hpn->ihp', reads_b, carried, precision=highest)
        outside = from_state * (jnp.exp(log_decay) * keeps_state[:, None])[:, :, None]
        tail_ok = (ids_b == ids_b[-1]).astype(jnp.float32)
        towards = jnp.exp(log_decay[-1][None, :] - log_decay) * tail_ok[:, None] * steps_b
        fresh_state = jnp.einsum('jhp,jn->hpn', towards[:, :, None] * inner_b, keys_b, precision=highest)
        carry_on = jnp.exp(log_decay[-1]) * (ids_b[-1] == before).astype(jnp.float32)
        return (fresh_state + carry_on[:, None, None] * carried, inside + outside)
    pieces = (inner_x.reshape(blocks, block_len, head_count, head_dim), step_sizes.reshape(blocks, block_len, head_count), state_b.reshape(blocks, block_len, -1), state_c.reshape(blocks, block_len, -1), seq_ids.reshape(blocks, block_len), prior_ids[::block_len])
    initial = jnp.zeros((head_count, head_dim, state_b.shape[1]), jnp.float32)
    final_state, result = lax.scan(jax.checkpoint(advance), initial, pieces)
    return result.reshape(row_count, head_count, head_dim)

def mamba_mixer(gate_z, inner_x, state_raw, step_raw, conv_inner, conv_state, step_bias, decay_log, skip_gain, seq_ids, block_len):
    row_count = inner_x.shape[0]
    head_count = step_raw.shape[1]
    state_dim = state_raw.shape[1] // 2
    conv_x = jax.nn.silu(causal_conv(inner_x, conv_inner, seq_ids)).reshape(row_count, head_count, -1)
    conv_bc = jax.nn.silu(causal_conv(state_raw, conv_state, seq_ids))
    step_sizes = jax.nn.softplus(step_raw + step_bias[None, :])
    scanned = state_scan(conv_x, step_sizes, conv_bc[:, :state_dim], conv_bc[:, state_dim:], jnp.exp(decay_log), seq_ids, block_len)
    output = scanned + skip_gain[None, :, None] * conv_x
    return output.reshape(row_count, -1) * jax.nn.silu(gate_z)

def swiglu(gate_part, up_part):
    return jax.nn.silu(gate_part) * up_part

def attend_ref(queries, keys_r, values_r, seq_ids, block_rows):
    row_count = keys_r.shape[0]
    scaling = queries.shape[2] ** (-0.5)
    columns = jnp.arange(row_count, dtype=jnp.int32)

    def one_block(row_start):
        q_block = lax.dynamic_slice_in_dim(queries, row_start, block_rows, 0)
        ids_block = lax.dynamic_slice_in_dim(seq_ids, row_start, block_rows, 0)
        places = row_start + jnp.arange(block_rows, dtype=jnp.int32)
        allowed = (ids_block[:, None] == seq_ids[None, :]) & (columns[None, :] <= places[:, None])
        scores = low_back(jnp.einsum('ihd,jd->hij', q_block, keys_r, precision=highest) * scaling)
        scores = jnp.where(allowed[None], scores, -jnp.inf)
        row_max = lax.optimization_barrier(jnp.max(scores, axis=-1, keepdims=True))
        exp_scores = jnp.exp(scores - row_max)
        row_total = lax.optimization_barrier(jnp.sum(exp_scores, axis=-1, keepdims=True))
        probs_f = exp_scores / row_total
        mixed = jnp.einsum('hij,jd->ihd', low(probs_f), values_r, precision=highest)
        return low(low_back(mixed))
    starts = jnp.arange(row_count // block_rows, dtype=jnp.int32) * block_rows
    return lax.map(jax.checkpoint(one_block), starts).reshape(row_count, queries.shape[1], queries.shape[2])

def group_layer(inputs, lengths, norm1_gain, norm2_gain, mixer_in, state_in, step_in, conv_inner, conv_state, step_bias, decay_log, skip_gain, mixer_out, query_in, key_value, attend_out, gate_up, down_out):
    row_count = inputs.shape[0]
    seq_ids, positions, is_live = segments(lengths, row_count)
    normed = low(rms_scale(inputs, norm1_gain))
    mixer_raw = low_back(matmul_hi(normed, mixer_in.reshape(D, 2 * MH * HD))).reshape(row_count, 2, MH * HD)
    state_raw = matmul_hi(normed, state_in)
    step_raw = low_back(matmul_hi(normed, step_in))
    query_all = low_back(matmul_hi(normed, query_in)).reshape(row_count, QH, HD)
    pair_raw = matmul_hi(normed, key_value.reshape(D, 2 * KVH * HD)).reshape(row_count, 2, KVH, HD)
    mixer_heads = MH // N_TENSOR
    query_heads = QH // N_TENSOR
    inner_width = mixer_heads * HD
    query_width = query_heads * HD
    running = jnp.zeros((row_count, D), jnp.float32)
    for part_index in range(N_TENSOR):
        inner_cols = slice(part_index * inner_width, (part_index + 1) * inner_width)
        head_cols = slice(part_index * mixer_heads, (part_index + 1) * mixer_heads)
        query_cols = slice(part_index * query_width, (part_index + 1) * query_width)
        gated = mamba_mixer(mixer_raw[:, 0, inner_cols], mixer_raw[:, 1, inner_cols], low_back(state_raw), step_raw[:, head_cols], conv_inner[:, inner_cols], conv_state, step_bias[head_cols], decay_log[head_cols], skip_gain[head_cols], seq_ids, SPAN)
        running = running + matmul_hi(low(gated), mixer_out[:, inner_cols].T)
        key_head = part_index * query_heads // (QH // KVH)
        pair_copy = low_back(pair_raw[:, :, key_head])
        queries = low(rotate(query_all[:, part_index * query_heads:(part_index + 1) * query_heads], positions, 1.0))
        keys_r = low(rotate(pair_copy[:, 0:1], positions, 1.0)[:, 0])
        values_r = low(pair_copy[:, 1])
        attended = attend_ref(queries, keys_r, values_r, seq_ids, ATT_ROWS)
        running = running + matmul_hi(attended.reshape(row_count, query_width), attend_out[:, query_cols].T)
    hidden_in = inputs + low_back(running)
    normed2 = low(rms_scale(hidden_in, norm2_gain))
    gate_raw = low_back(matmul_hi(normed2, gate_up.reshape(D, 2 * FF))).reshape(row_count, 2, FF)
    hidden_f = low(swiglu(gate_raw[:, 0], gate_raw[:, 1]))
    ffn_out = low_back(matmul_hi(hidden_f, down_out.T))
    return (hidden_in + ffn_out) * is_live[:, None]

def reference(tokens, cotangent, seq_lengths, norm1_gain, norm2_gain, mixer_in, state_in, step_in, conv_inner, conv_state, step_bias, decay_log, skip_gain, mixer_out, query_in, key_value, attend_out, gate_up, down_out):
    params = tuple((weight.astype(jnp.float32) for weight in (norm1_gain, norm2_gain, mixer_in, state_in, step_in, conv_inner, conv_state, step_bias, decay_log, skip_gain, mixer_out, query_in, key_value, attend_out, gate_up, down_out)))

    def forward(inputs, params_in):
        grouped = inputs.reshape(N_DP, TOK_DEV, D)

        def one_group(carried, pieces):
            return (carried, group_layer(pieces[0], pieces[1], *params_in))
        final_carry, outputs = lax.scan(jax.checkpoint(one_group), jnp.zeros((), jnp.float32), (grouped, seq_lengths))
        return outputs.reshape(N_DP * TOK_DEV, D)
    block_out, pullback = jax.vjp(forward, tokens.astype(jnp.float32), params)
    token_grad, grads = pullback(cotangent.astype(jnp.float32))
    return (block_out.astype(jnp.bfloat16), token_grad.astype(jnp.bfloat16), grads[0], grads[1], grads[2], grads[3], grads[4], grads[5], grads[6], grads[7], grads[8], grads[9], grads[10], grads[11], grads[12], grads[13], grads[14], grads[15])
```

```python
import functools

import jax
import jax.numpy as jnp
from jax import lax
from jax.experimental import pallas as pl
from jax.experimental.pallas import tpu as pltpu
from jax.sharding import PartitionSpec as P

HD = 64
QH = 8
KVH = 2
LANES = 128

rope_base = 100000000000.0
norm_eps = 1e-05
far = -1e30
highest = lax.Precision.HIGHEST
f32 = jnp.float32
bf16 = jnp.bfloat16


def padded(width):
    return -(-width // LANES) * LANES


def pad_to(values, width):
    return jnp.pad(values, [(0, 0)] * (values.ndim - 1) + [(0, width - values.shape[-1])])


def mm(left, right):
    return jnp.dot(left, right, preferred_element_type=f32)


def mm_nt(left, right):
    return lax.dot_general(left, right, (((1,), (1,)), ((), ())), preferred_element_type=f32)


def mm_tn(left, right):
    return lax.dot_general(left, right, (((0,), (0,)), ((), ())), preferred_element_type=f32)


def mm_exact(left, right):
    return jnp.dot(left, right, preferred_element_type=f32, precision=highest)


def lane_ids(rows):
    return lax.broadcasted_iota(jnp.int32, (rows, LANES), 1)


def partner_half(values):
    lane = lane_ids(values.shape[0])
    return jnp.where(lane % HD < HD // 2, pltpu.roll(values, LANES - HD // 2, 1), pltpu.roll(values, HD // 2, 1))


def rotated(values, cosine, signed_sine):
    return values * cosine + partner_half(values) * signed_sine


def conv_terms(values, masks):
    return [pltpu.roll(values, offset, 0) * masks[offset] for offset in (3, 2, 1)] + [values]


def conv_back(grad, masks, taps):
    rows = grad.shape[0]
    total = grad * taps[3:4]
    for offset in (1, 2, 3):
        total = total + pltpu.roll(grad * masks[offset], rows - offset, 0) * taps[3 - offset : 4 - offset]
    return total


def link_bias(seq_col, seq_row, transposed):
    rows = seq_col.shape[0]
    down = lax.broadcasted_iota(jnp.int32, (rows, rows), 0)
    across = lax.broadcasted_iota(jnp.int32, (rows, rows), 1)
    ordered = down <= across if transposed else down >= across
    return (seq_col == seq_row) & ordered


def step_parts(raw, bias):
    shifted = raw + bias
    return jnp.maximum(shifted, 0.0) + jnp.log1p(jnp.exp(-jnp.abs(shifted)))


def spread_heads(columns, first, width):
    rows = columns.shape[0]
    low = jnp.broadcast_to(columns[:, first : first + 1], (rows, LANES))
    if width <= HD:
        return low
    high = jnp.broadcast_to(columns[:, first + 1 : first + 2], (rows, LANES))
    return jnp.where(lane_ids(rows) < HD, low, high)


def half_mask(rows, side):
    lane = lane_ids(rows)
    return lane < HD if side == 0 else lane >= HD


def front_kernel(
    dims, x_ref, gain_ref, wcat_ref, wout_ref, seqc_ref, seqr_ref, masks_ref, cos_ref, sin_ref,
    convx_ref, convs_ref, bias_ref, rate_ref, skip_ref,
    act_ref, proj_ref, scan_ref, cat_ref, part_ref, neg_ref, g_ref, xdt_ref,
):
    heads, qheads, wp, qwp, span = dims
    rows = x_ref.shape[0]
    x = x_ref[...].astype(f32)
    act = (x * lax.rsqrt(jnp.mean(x * x, axis=-1, keepdims=True) + norm_eps) * gain_ref[...]).astype(bf16)
    act_ref[...] = act
    proj_ref[...] = mm(act, wcat_ref[...])
    at_state, at_step, at_query, at_pair = 2 * wp, 2 * wp + 256, 2 * wp + 384, 2 * wp + 384 + qwp
    masks = {k: masks_ref[:, k : k + 1] for k in (1, 2, 3)}
    linked = link_bias(seqc_ref[...], seqr_ref[...], False)
    neg_ref[...] = jnp.where(linked, 0.0, far)
    dt = step_parts(proj_ref[:, at_step : at_step + LANES], bias_ref[...])
    decay = mm_exact(jnp.where(linked, 1.0, 0.0), -dt * rate_ref[...])
    decay_t = decay.T
    state = proj_ref[:, at_state : at_state + 256]
    terms = conv_terms(state, masks)
    bcc = sum(t * convs_ref[k : k + 1, :] for k, t in enumerate(terms))
    bcc = (bcc * jax.nn.sigmoid(bcc)).astype(bf16)
    g_ref[...] = mm_nt(bcc[:, 128:], bcc[:, :128])

    for p in range(wp // LANES):
        cols = slice(p * LANES, (p + 1) * LANES)
        width = HD * min(2, heads - 2 * p)
        raw = proj_ref[:, wp + p * LANES : wp + (p + 1) * LANES]
        conv = sum(t * convx_ref[k : k + 1, cols] for k, t in enumerate(conv_terms(raw, masks)))
        xc = conv * jax.nn.sigmoid(conv)
        xdt_ref[...] = (xc * spread_heads(dt, 2 * p, width)).astype(bf16)
        blocks = []
        for a in range(rows // span):
            here = slice(a * span, (a + 1) * span)
            reach = (a + 1) * span
            sides = []
            for h in range(2 * p, 2 * p + width // HD):
                gap = decay[here, h : h + 1] - decay_t[h : h + 1, :reach]
                mixing = g_ref[here, :reach] * jnp.exp(gap + neg_ref[here, :reach])
                sides.append(mm(mixing.astype(bf16), xdt_ref[:reach, :]))
            blocks.append(sides[0] if len(sides) == 1 else jnp.where(half_mask(span, 0), sides[0], sides[1]))
        scanned = jnp.concatenate(blocks, axis=0)
        scan_ref[:, cols] = scanned
        z = proj_ref[:, cols]
        cat_ref[:, cols] = ((scanned + skip_ref[:, cols] * xc) * (z * jax.nn.sigmoid(z))).astype(bf16)

    cosine, sine = cos_ref[...], sin_ref[...]
    pair = proj_ref[:, at_pair : at_pair + LANES]
    swapped = pltpu.roll(pair, HD, 1)
    lower = half_mask(rows, 0)
    keys = rotated(jnp.where(lower, pair, swapped), cosine, sine).astype(bf16)
    values = jnp.where(lower, swapped, pair).astype(bf16)
    for p in range(qwp // LANES):
        cols = slice(wp + p * LANES, wp + (p + 1) * LANES)
        queries = rotated(proj_ref[:, at_query + p * LANES : at_query + (p + 1) * LANES], cosine, sine).astype(bf16)
        for a in range(rows // span):
            here = slice(a * span, (a + 1) * span)
            reach = (a + 1) * span
            sides = []
            for side in range(min(2, qheads - 2 * p)):
                q = jnp.where(half_mask(span, side), queries[here], jnp.zeros((), bf16))
                scores = mm_nt(q, keys[:reach]) * (HD**-0.5) + neg_ref[here, :reach]
                weights = jnp.exp(scores - jnp.max(scores, axis=-1, keepdims=True))
                probs = weights / jnp.sum(weights, axis=-1, keepdims=True)
                sides.append(mm(probs.astype(bf16), values[:reach]))
            if len(sides) == 1:
                out = jnp.where(half_mask(span, 0), sides[0], 0.0)
            else:
                out = jnp.where(half_mask(span, 0), sides[0], sides[1])
            cat_ref[here, cols] = out.astype(bf16)
    part_ref[...] = mm_nt(cat_ref[...], wout_ref[...]).astype(bf16)


def middle_kernel(
    x_ref, own_ref, other_ref, gain_ref, wgu_ref, down_ref, dhid_ref,
    h1_ref, n2_ref, hidden_ref, dgu_ref, out_ref, dn2_ref,
):
    width = down_ref.shape[1]
    h1 = x_ref[...].astype(f32) + (own_ref[...].astype(f32) + other_ref[...].astype(f32))
    h1_ref[...] = h1
    n2 = (h1 * lax.rsqrt(jnp.mean(h1 * h1, axis=-1, keepdims=True) + norm_eps) * gain_ref[...]).astype(bf16)
    n2_ref[...] = n2
    gate = mm(n2, wgu_ref[:, :width])
    up = mm(n2, wgu_ref[:, width:])
    sig = jax.nn.sigmoid(gate)
    silu = gate * sig
    hidden = (silu * up).astype(bf16)
    hidden_ref[...] = hidden
    dhid = dhid_ref[...].astype(f32)
    dgu_ref[:, :width] = (dhid * up * (sig * (1.0 + gate * (1.0 - sig)))).astype(bf16)
    dgu_ref[:, width:] = (dhid * silu).astype(bf16)
    dn2_ref[...] = mm_nt(dgu_ref[...], wgu_ref[...]).astype(bf16)
    out_ref[...] = mm_nt(hidden, down_ref[...]).astype(bf16)


def back_kernel(
    dims, own_ref, other_ref, h1_ref, dout_ref, gain2_ref, x_ref, wcat_ref, wout_ref, seqc_ref, seqr_ref, masks_ref,
    cos_ref, sin_ref, convx_ref, convs_ref, bias_ref, rate_ref, skip_ref, proj_ref, scan_ref,
    dh1_ref, dmix_ref, dall_ref, dact_ref, gn1_ref, gn2_ref, gcx_ref, gcs_ref, gstep_ref, gskip_ref,
    neg_ref, gt_ref, dgt_ref, dcat_ref, dsum_ref, ddir_ref, dk_ref, dv_ref,
):
    heads, qheads, wp, qwp, span = dims
    rows = x_ref.shape[0]
    at_state, at_step, at_query, at_pair = 2 * wp, 2 * wp + 256, 2 * wp + 384, 2 * wp + 384 + qwp
    dn2 = own_ref[...].astype(f32) + other_ref[...].astype(f32)
    h1 = h1_ref[...]
    r2 = lax.rsqrt(jnp.mean(h1 * h1, axis=-1, keepdims=True) + norm_eps)
    u = dn2 * gain2_ref[...]
    dh1 = dout_ref[...].astype(f32) + r2 * u - h1 * (r2 * r2 * r2 * jnp.mean(u * h1, axis=-1, keepdims=True))
    gn2_ref[...] = jnp.sum(dn2 * h1 * r2, axis=0, keepdims=True)
    dh1_ref[...] = dh1
    dmix = dh1.astype(bf16)
    dmix_ref[...] = dmix
    dcat_ref[...] = mm(dmix, wout_ref[...])

    masks = {k: masks_ref[:, k : k + 1] for k in (1, 2, 3)}
    linked_t = link_bias(seqc_ref[...], seqr_ref[...], True)
    neg_ref[...] = jnp.where(linked_t, 0.0, far)
    lower = half_mask(rows, 0)
    cosine, sine = cos_ref[...], sin_ref[...]
    pair = proj_ref[:, at_pair : at_pair + LANES]
    swapped = pltpu.roll(pair, HD, 1)
    keys = rotated(jnp.where(lower, pair, swapped), cosine, sine).astype(bf16)
    values = jnp.where(lower, swapped, pair).astype(bf16)
    dk_ref[...] = jnp.zeros_like(dk_ref)
    dv_ref[...] = jnp.zeros_like(dv_ref)
    for p in range(qwp // LANES):
        at = at_query + p * LANES
        queries = rotated(proj_ref[:, at : at + LANES], cosine, sine).astype(bf16)
        datt = dcat_ref[:, wp + p * LANES : wp + (p + 1) * LANES].astype(bf16)
        blocks = []
        for a in range(rows // span):
            here = slice(a * span, (a + 1) * span)
            reach = (a + 1) * span
            sides = []
            for side in range(min(2, qheads - 2 * p)):
                half = half_mask(span, side)
                q = jnp.where(half, queries[here], jnp.zeros((), bf16))
                do = jnp.where(half, datt[here], jnp.zeros((), bf16))
                scores = mm_nt(keys[:reach], q) * (HD**-0.5) + neg_ref[:reach, here]
                weights = jnp.exp(scores - jnp.max(scores, axis=0, keepdims=True))
                probs = weights / jnp.sum(weights, axis=0, keepdims=True)
                dp = mm_nt(values[:reach], do)
                ds = (probs * (dp - jnp.sum(probs * dp, axis=0, keepdims=True))).astype(bf16)
                dk_ref[:reach, :] += mm(ds, q)
                dv_ref[:reach, :] += mm(probs.astype(bf16), do)
                sides.append(mm_tn(ds, keys[:reach]))
            if len(sides) == 1:
                blocks.append(jnp.where(half_mask(span, 0), sides[0], 0.0))
            else:
                blocks.append(jnp.where(half_mask(span, 0), sides[0], sides[1]))
        dq = jnp.concatenate(blocks, axis=0) * (HD**-0.5)
        dall_ref[:, at : at + LANES] = rotated(dq, cosine, -sine).astype(bf16)
    dk = dk_ref[...] * (HD**-0.5)
    dk = rotated(dk + pltpu.roll(dk, HD, 1), cosine, -sine)
    dv = dv_ref[...]
    dv = dv + pltpu.roll(dv, HD, 1)
    dall_ref[:, at_pair : at_pair + LANES] = jnp.where(lower, dk, dv).astype(bf16)

    dt = step_parts(proj_ref[:, at_step : at_step + LANES], bias_ref[...])
    linked = link_bias(seqc_ref[...], seqr_ref[...], False)
    decay = mm_exact(jnp.where(linked, 1.0, 0.0), -dt * rate_ref[...])
    decay_t = decay.T
    state = proj_ref[:, at_state : at_state + 256]
    sterms = conv_terms(state, masks)
    sconv = sum(t * convs_ref[k : k + 1, :] for k, t in enumerate(sterms))
    ssig = jax.nn.sigmoid(sconv)
    bcc = (sconv * ssig).astype(bf16)
    bm, cm = bcc[:, :128], bcc[:, 128:]
    gt_ref[...] = mm_nt(bm, cm)
    dgt_ref[...] = jnp.zeros_like(dgt_ref)
    for p in range(wp // LANES):
        cols = slice(p * LANES, (p + 1) * LANES)
        width = HD * min(2, heads - 2 * p)
        raw = proj_ref[:, wp + p * LANES : wp + (p + 1) * LANES]
        terms = conv_terms(raw, masks)
        conv = sum(t * convx_ref[k : k + 1, cols] for k, t in enumerate(terms))
        csig = jax.nn.sigmoid(conv)
        xc = conv * csig
        dt_cols = spread_heads(dt, 2 * p, width)
        xdt = (xc * dt_cols).astype(bf16)
        z = proj_ref[:, cols]
        zsig = jax.nn.sigmoid(z)
        dgated = dcat_ref[:, cols]
        scanned = scan_ref[:, cols]
        skip = skip_ref[:, cols]
        dy = dgated * (z * zsig)
        dall_ref[:, cols] = (dgated * (scanned + skip * xc) * (zsig * (1.0 + z * (1.0 - zsig)))).astype(bf16)
        gskip_ref[:, cols] = jnp.sum(dy * xc, axis=0, keepdims=True)
        dyb = dy.astype(bf16)
        blocks = []
        for a in range(rows // span):
            here = slice(a * span, (a + 1) * span)
            sides = []
            for side in range(width // HD):
                h = 2 * p + side
                dys = jnp.where(half_mask(rows - a * span, side), dyb[a * span :], jnp.zeros((), bf16))
                gap = decay_t[h : h + 1, a * span :] - decay[here, h : h + 1]
                falloff = jnp.exp(gap + neg_ref[here, a * span :])
                mixing = (gt_ref[here, a * span :] * falloff).astype(bf16)
                sides.append(mm(mixing, dyb[a * span :]))
                dgt_ref[here, a * span :] += mm_nt(xdt[here], dys) * falloff
            blocks.append(sides[0] if len(sides) == 1 else jnp.where(half_mask(span, 0), sides[0], sides[1]))
        dxdt = jnp.concatenate(blocks, axis=0)
        dsum_ref[:, cols] = dyb.astype(f32) * scanned - xdt.astype(f32) * dxdt
        ddir_ref[:, cols] = dxdt * xc
        dconv = (dxdt * dt_cols + skip * dy) * (csig * (1.0 + conv * (1.0 - csig)))
        gcx_ref[:, cols] = jnp.concatenate([jnp.sum(t * dconv, axis=0, keepdims=True) for t in terms], axis=0)
        dall_ref[:, wp + p * LANES : wp + (p + 1) * LANES] = conv_back(dconv, masks, convx_ref[:, cols]).astype(bf16)

    dgt = dgt_ref[...].astype(bf16)
    dbcc = jnp.concatenate([mm(dgt, cm), mm_tn(dgt, bm)], axis=1)
    dsconv = dbcc * (ssig * (1.0 + sconv * (1.0 - ssig)))
    gcs_ref[...] = jnp.concatenate([jnp.sum(t * dsconv, axis=0, keepdims=True) for t in sterms], axis=0)
    dall_ref[:, at_state : at_state + 256] = conv_back(dsconv, masks, convs_ref[...]).astype(bf16)

    head_of = lax.broadcasted_iota(jnp.int32, (wp, LANES), 0) // HD
    pick = jnp.where(head_of == lax.broadcasted_iota(jnp.int32, (wp, LANES), 1), 1.0, 0.0)
    ds = mm_exact(dsum_ref[...], pick)
    ddirect = mm_exact(ddir_ref[...], pick)
    dlog = mm_exact(jnp.where(linked_t, 1.0, 0.0), ds)
    rate = rate_ref[...]
    ddt = ddirect - rate * dlog
    dstep = ddt * jax.nn.sigmoid(proj_ref[:, at_step : at_step + LANES] + bias_ref[...])
    dstep = jnp.where(lane_ids(rows) < heads, dstep, 0.0)
    dall_ref[:, at_step : at_step + LANES] = dstep.astype(bf16)
    gstep_ref[...] = jnp.concatenate(
        [jnp.sum(dstep, axis=0, keepdims=True), -rate * jnp.sum(dt * dlog, axis=0, keepdims=True)], axis=0
    )
    dact = mm_nt(dall_ref[...], wcat_ref[...])
    dact_ref[...] = dact.astype(bf16)
    x = x_ref[...].astype(f32)
    r1 = lax.rsqrt(jnp.mean(x * x, axis=-1, keepdims=True) + norm_eps)
    gn1_ref[...] = jnp.sum(dact * x * r1, axis=0, keepdims=True)


def call(kernel, outs, scratch, args, flops):
    moved = sum(a.size * a.dtype.itemsize for a in args) + sum(s[0] * s[1] * jnp.dtype(t).itemsize for s, t in outs)
    return pl.pallas_call(
        kernel,
        out_shape=[jax.ShapeDtypeStruct(s, t) for s, t in outs],
        in_specs=[pl.BlockSpec(memory_space=pltpu.VMEM)] * len(args),
        out_specs=[pl.BlockSpec(memory_space=pltpu.VMEM)] * len(outs),
        scratch_shapes=[pltpu.VMEM(s, t) for s, t in scratch],
        compiler_params=pltpu.CompilerParams(vmem_limit_bytes=50 * 1024 * 1024),
        cost_estimate=pl.CostEstimate(flops=flops, bytes_accessed=moved, transcendentals=0),
    )(*args)


def swap(values):
    return lax.ppermute(values, "tensor", [(0, 1), (1, 0)])


def gather_rows(values, me, count):
    if count != 2:
        return lax.all_gather(values, "tensor", axis=0, tiled=True)
    other = swap(values)
    first = jnp.where(me == 0, values, other)
    return jnp.concatenate([first, jnp.where(me == 0, other, values)], axis=0)


def both_parts(part, count):
    if count != 2:
        return (lax.psum(part, "tensor"), jnp.zeros_like(part))
    return (part, swap(part))


def scatter_rows(part, me, count):
    if count != 2:
        return lax.psum_scatter(part, "tensor", scatter_dimension=0, tiled=True).astype(f32)
    halves = part.reshape(2, part.shape[0] // 2, part.shape[1])
    arrived = swap(lax.dynamic_index_in_dim(halves, 1 - me, 0, keepdims=False))
    return lax.dynamic_index_in_dim(halves, me, 0, keepdims=False).astype(f32) + arrived.astype(f32)


def partners(count, bit):
    return [(i, i ^ bit) for i in range(count)]


def weight_halves(left_t, right, index, count):
    features = left_t.shape[0]
    blocks = left_t.reshape(count // 2, 2, features // count, left_t.shape[1])
    bit = index % 2

    def part(which):
        chosen = lax.dynamic_index_in_dim(blocks, which, 1, keepdims=False).reshape(features // 2, -1)
        return mm(chosen, right).astype(bf16)

    return part(1 - bit), part(bit)


def halving(sent, kept, index, count):
    arrived = lax.ppermute(sent, "dp", partners(count, 1))
    held = kept.astype(f32) + arrived.astype(f32)
    left, bit = count // 2, 2
    while left > 1:
        blocks = held.astype(bf16).reshape(left // 2, 2, held.shape[0] // left, held.shape[1])
        which = (index // bit) % 2
        away = lax.dynamic_index_in_dim(blocks, 1 - which, 1, keepdims=False).reshape(held.shape[0] // 2, -1)
        mine = lax.dynamic_index_in_dim(blocks, which, 1, keepdims=False).reshape(held.shape[0] // 2, -1)
        arrived = lax.ppermute(away, "dp", partners(count, bit))
        held = mine.astype(f32) + arrived.astype(f32)
        left, bit = left // 2, bit * 2
    return held


def doubling(values, count):
    bit = 1
    while bit < count:
        values = values + lax.ppermute(values, "dp", partners(count, bit))
        bit *= 2
    return values


def segments(lengths, row_count):
    seq_ends = jnp.cumsum(lengths)
    places = jnp.arange(row_count, dtype=jnp.int32)
    passed = places[:, None] >= seq_ends[None, :]
    seq_ids = jnp.sum(passed.astype(jnp.int32), axis=1)
    starts = jnp.max(jnp.where(passed, seq_ends[None, :], 0), axis=1)
    is_live = (places < seq_ends[-1]).astype(f32)
    return (seq_ids, places - starts, is_live)


def body(
    dp_count, tensor_count, tokens, cotangent, seq_lengths, norm1_gain, norm2_gain, mixer_in, state_in, step_in,
    conv_inner, conv_state, step_bias, decay_log, skip_gain, mixer_out, query_in, key_value, attend_out, gate_up,
    down_out,
):
    share, model = tokens.shape
    rows = share * tensor_count
    me = lax.axis_index("tensor")
    index = lax.axis_index("dp")
    inner = mixer_in.shape[2]
    heads = step_in.shape[1]
    query_width = query_in.shape[1]
    qheads = query_width // HD
    wp, qwp = padded(inner), padded(query_width)
    span = min(LANES, rows)
    dims = (heads, qheads, wp, qwp, span)
    columns = 2 * wp + 384 + qwp + LANES

    x_rows = gather_rows(tokens, me, tensor_count)
    seq_ids, positions, is_live = segments(seq_lengths[0], rows)
    live_share = lax.dynamic_slice_in_dim(is_live, me * share, share, 0)[:, None]
    grad_out = cotangent.astype(f32) * live_share
    dout_rows = gather_rows(grad_out.astype(bf16), me, tensor_count)

    seq_col = seq_ids.astype(f32)[:, None]
    seq_row = seq_ids.astype(f32)[None, :]
    shifts = jnp.minimum(jnp.arange(LANES, dtype=jnp.int32), 4)[None, :]
    masks = (positions[:, None] >= shifts).astype(f32)
    lane = jnp.arange(LANES)
    frequency = rope_base ** (-2.0 * jnp.arange(HD // 2, dtype=f32) / HD)
    angles = positions.astype(f32)[:, None] * frequency[None, :]
    cosine = jnp.tile(jnp.cos(angles), (1, 4))
    sine = jnp.tile(jnp.sin(angles), (1, 4)) * jnp.where(lane % HD < HD // 2, -1.0, 1.0)[None, :]

    key_index = me * qheads // (QH // KVH)
    pair_local = lax.dynamic_slice_in_dim(key_value, key_index * HD, HD, 2).reshape(model, 2 * HD)
    wcat = jnp.concatenate(
        [
            pad_to(mixer_in[:, 0], wp), pad_to(mixer_in[:, 1], wp), state_in, pad_to(step_in, LANES),
            pad_to(query_in, qwp), pair_local,
        ],
        axis=1,
    )
    wout = jnp.concatenate([pad_to(mixer_out, wp), pad_to(attend_out, qwp)], axis=1)
    wgu = gate_up.reshape(model, -1)
    taps = pad_to(conv_inner, wp)
    bias = pad_to(step_bias[None], LANES)
    rate = pad_to(jnp.exp(decay_log)[None], LANES)
    skip = pad_to(jnp.repeat(skip_gain, HD)[None], wp)
    gain1, gain2 = norm1_gain[None], norm2_gain[None]

    act, proj, scanned, cat, part = call(
        functools.partial(front_kernel, dims),
        [((rows, model), bf16), ((rows, columns), f32), ((rows, wp), f32), ((rows, wp + qwp), bf16), ((rows, model), bf16)],
        [((rows, rows), f32), ((rows, rows), f32), ((rows, LANES), bf16)],
        (x_rows, gain1, wcat, wout, seq_col, seq_row, masks, cosine, sine, taps, conv_state, bias, rate, skip),
        8 * rows * model * columns,
    )
    dhidden = mm(dout_rows, down_out)
    own, other = both_parts(part, tensor_count)
    ff2 = wgu.shape[1]
    h1, n2, hidden, dgu, ffn_part, dn2_part = call(
        middle_kernel,
        [
            ((rows, model), f32), ((rows, model), bf16), ((rows, ff2 // 2), bf16), ((rows, ff2), bf16),
            ((rows, model), bf16), ((rows, model), bf16),
        ],
        [],
        (x_rows, own, other, gain2, wgu, down_out, dhidden),
        6 * rows * model * ff2,
    )
    dn2_own, dn2_other = both_parts(dn2_part, tensor_count)
    ffn_share = scatter_rows(ffn_part, me, tensor_count)
    h1_share = lax.dynamic_slice_in_dim(h1, me * share, share, 0)
    block_out = ((h1_share + ffn_share) * live_share).astype(bf16)

    up_sent, up_kept = weight_halves(n2.T, dgu, index, dp_count)
    down_sent, down_kept = weight_halves(dout_rows.T, hidden, index, dp_count)
    ffn_total = halving(
        jnp.concatenate([up_sent, down_sent], axis=1), jnp.concatenate([up_kept, down_kept], axis=1), index, dp_count
    )

    dh1, dmix, dall, dact, gn1, gn2, gcx, gcs, gstep, gskip = call(
        functools.partial(back_kernel, dims),
        [
            ((rows, model), f32), ((rows, model), bf16), ((rows, columns), bf16), ((rows, model), bf16),
            ((1, model), f32), ((1, model), f32), ((4, wp), f32), ((4, 256), f32), ((2, LANES), f32), ((1, wp), f32),
        ],
        [
            ((rows, rows), f32), ((rows, rows), f32), ((rows, rows), f32), ((rows, wp + qwp), f32),
            ((rows, wp), f32), ((rows, wp), f32), ((rows, LANES), f32), ((rows, LANES), f32),
        ],
        (
            dn2_own, dn2_other, h1, dout_rows, gain2, x_rows, wcat, wout, seq_col, seq_row, masks, cosine, sine, taps,
            conv_state, bias, rate, skip, proj, scanned,
        ),
        12 * rows * model * columns,
    )
    out_sent, out_kept = weight_halves(dmix.T, cat, index, dp_count)
    out_total = halving(out_sent, out_kept, index, dp_count)
    in_sent, in_kept = weight_halves(act.T, dall, index, dp_count)
    in_total = halving(in_sent, in_kept, index, dp_count)

    dact_share = scatter_rows(dact, me, tensor_count)
    x_share = tokens.astype(f32)
    r1 = lax.rsqrt(jnp.mean(x_share * x_share, axis=-1, keepdims=True) + norm_eps)
    u = dact_share * gain1
    dh1_share = lax.dynamic_slice_in_dim(dh1, me * share, share, 0)
    token_grad = dh1_share + r1 * u - x_share * (r1 * r1 * r1 * jnp.mean(u * x_share, axis=-1, keepdims=True))

    shared = jnp.concatenate([gn1[0], gn2[0] * (1.0 / tensor_count), gcs.reshape(-1)]).reshape(-1, LANES)
    local = jnp.concatenate([gcx.reshape(-1), gskip.reshape(-1), gstep.reshape(-1)]).reshape(-1, LANES)
    minor = doubling(jnp.concatenate([shared, local], axis=0), dp_count)
    shared_rows = shared.shape[0]
    shared = lax.psum(minor[:shared_rows], "tensor") if tensor_count != 2 else minor[:shared_rows] + swap(minor[:shared_rows])
    shared = shared.reshape(-1)
    local = minor[shared_rows:].reshape(-1)
    g_norm1, g_norm2, g_conv_state = shared[:model], shared[model : 2 * model], shared[2 * model :].reshape(4, 256)
    g_conv_inner = local[: 4 * wp].reshape(4, wp)[:, :inner]
    g_skip = jnp.sum(local[4 * wp : 5 * wp].reshape(-1, HD), axis=1)[:heads]
    g_bias = local[5 * wp : 5 * wp + heads]
    g_decay = local[5 * wp + LANES : 5 * wp + LANES + heads]

    block = in_total.shape[0]
    both = jnp.concatenate([in_total[:, 2 * wp : 2 * wp + 256], in_total[:, columns - LANES :]], axis=1).astype(bf16)
    placed = lambda pair: lax.dynamic_update_slice_in_dim(
        jnp.zeros((block,) + key_value.shape[1:], f32), pair.astype(f32).reshape(block, 2, HD), key_index * HD, 2
    )
    if tensor_count == 2:
        arrived = swap(both)
        g_state = both[:, :256].astype(f32) + arrived[:, :256].astype(f32)
        mine = both[:, 256:].reshape(block, 2, HD)
        theirs = arrived[:, 256:].reshape(block, 2, HD)
        g_pair = jnp.concatenate(
            [jnp.where(me == 0, mine, theirs), jnp.where(me == 0, theirs, mine)], axis=2
        ).astype(f32)
    else:
        g_state = lax.psum(both[:, :256], "tensor").astype(f32)
        g_pair = lax.psum(placed(both[:, 256:]).astype(bf16), "tensor").astype(f32)

    g_mixer_in = jnp.stack([in_total[:, :inner], in_total[:, wp : wp + inner]], axis=1)
    at_step = 2 * wp + 256
    at_query = at_step + LANES
    return (
        block_out,
        token_grad.astype(bf16),
        g_norm1,
        g_norm2,
        g_mixer_in,
        g_state,
        in_total[:, at_step : at_step + heads],
        g_conv_inner,
        g_conv_state,
        g_bias,
        g_decay,
        g_skip,
        out_total[:, :inner],
        in_total[:, at_query : at_query + query_width],
        g_pair,
        out_total[:, wp : wp + query_width],
        ffn_total[:, :ff2].reshape(block, 2, ff2 // 2),
        ffn_total[:, ff2:],
    )


def solution(mesh):
    return jax.shard_map(
        functools.partial(body, mesh.shape["dp"], mesh.shape["tensor"]),
        mesh=mesh,
        in_specs=(
            P(("dp", "tensor"), None),
            P(("dp", "tensor"), None),
            P("dp", None),
            P(),
            P(),
            P(None, None, "tensor"),
            P(),
            P(None, "tensor"),
            P(None, "tensor"),
            P(),
            P("tensor"),
            P("tensor"),
            P("tensor"),
            P(None, "tensor"),
            P(None, "tensor"),
            P(),
            P(None, "tensor"),
            P(None, None, "tensor"),
            P(None, "tensor"),
        ),
        out_specs=(
            P(("dp", "tensor"), None),
            P(("dp", "tensor"), None),
            P(),
            P(),
            P("dp", None, "tensor"),
            P("dp", None),
            P("dp", "tensor"),
            P(None, "tensor"),
            P(),
            P("tensor"),
            P("tensor"),
            P("tensor"),
            P("dp", "tensor"),
            P("dp", "tensor"),
            P("dp", None, None),
            P("dp", "tensor"),
            P("dp", None, "tensor"),
            P("dp", "tensor"),
        ),
        check_vma=False,
    )
```

```python
import functools

import jax
import jax.numpy as jnp
from jax import lax
from jax.experimental import pallas as pl
from jax.experimental.pallas import tpu as pltpu
from jax.sharding import PartitionSpec as P

HD = 64
QH = 8
KVH = 2
LANES = 128

rope_base = 100000000000.0
norm_eps = 1e-05
far = -1e30
highest = lax.Precision.HIGHEST
f32 = jnp.float32
bf16 = jnp.bfloat16


def padded(width):
    return -(-width // LANES) * LANES


def pad_to(values, width):
    return jnp.pad(values, [(0, 0)] * (values.ndim - 1) + [(0, width - values.shape[-1])])


def mm(left, right):
    return jnp.dot(left, right, preferred_element_type=f32)


def mm_nt(left, right):
    return lax.dot_general(left, right, (((1,), (1,)), ((), ())), preferred_element_type=f32)


def mm_tn(left, right):
    return lax.dot_general(left, right, (((0,), (0,)), ((), ())), preferred_element_type=f32)


def mm_exact(left, right):
    return jnp.dot(left, right, preferred_element_type=f32, precision=highest)


def lane_ids(rows):
    return lax.broadcasted_iota(jnp.int32, (rows, LANES), 1)


def partner_half(values):
    lane = lane_ids(values.shape[0])
    return jnp.where(lane % HD < HD // 2, pltpu.roll(values, LANES - HD // 2, 1), pltpu.roll(values, HD // 2, 1))


def rotated(values, cosine, signed_sine):
    return values * cosine + partner_half(values) * signed_sine


def conv_terms(values, masks):
    return [pltpu.roll(values, offset, 0) * masks[offset] for offset in (3, 2, 1)] + [values]


def conv_back(grad, masks, taps):
    rows = grad.shape[0]
    total = grad * taps[3:4]
    for offset in (1, 2, 3):
        total = total + pltpu.roll(grad * masks[offset], rows - offset, 0) * taps[3 - offset : 4 - offset]
    return total


def link_bias(seq_col, seq_row, transposed):
    rows = seq_col.shape[0]
    down = lax.broadcasted_iota(jnp.int32, (rows, rows), 0)
    across = lax.broadcasted_iota(jnp.int32, (rows, rows), 1)
    ordered = down <= across if transposed else down >= across
    return (seq_col == seq_row) & ordered


def step_parts(raw, bias):
    shifted = raw + bias
    return jnp.maximum(shifted, 0.0) + jnp.log1p(jnp.exp(-jnp.abs(shifted)))


def spread_heads(columns, first, width):
    rows = columns.shape[0]
    low = jnp.broadcast_to(columns[:, first : first + 1], (rows, LANES))
    if width <= HD:
        return low
    high = jnp.broadcast_to(columns[:, first + 1 : first + 2], (rows, LANES))
    return jnp.where(lane_ids(rows) < HD, low, high)


def half_mask(rows, side):
    lane = lane_ids(rows)
    return lane < HD if side == 0 else lane >= HD


def front_kernel(
    dims, x_ref, gain_ref, wzx_ref, wbc_ref, wq_ref, wsp_ref, wmix_ref, watt_ref, seqc_ref, seqr_ref, masks_ref,
    cos_ref, sin_ref, convx_ref, convs_ref, bias_ref, rate_ref, skip_ref,
    act_ref, pa_ref, pb_ref, y_ref, cat_ref, part_ref, neg_ref, g_ref, xdt_ref,
):
    heads, qheads, wp, qwp, span = dims
    rows = x_ref.shape[0]
    x = x_ref[...].astype(f32)
    act = (x * lax.rsqrt(jnp.mean(x * x, axis=-1, keepdims=True) + norm_eps) * gain_ref[...]).astype(bf16)
    act_ref[...] = act
    pb_ref[:, wp : wp + 256] = mm(act, wbc_ref[...])
    pb_ref[:, wp + 256 :] = mm(act, wsp_ref[:, :LANES])
    pb_ref[:, :wp] = mm(act, wzx_ref[:, wp:])
    pa_ref[:, wp : wp + qwp] = mm(act, wq_ref[...])
    pa_ref[:, wp + qwp :] = mm(act, wsp_ref[:, LANES:])
    pa_ref[:, :wp] = mm(act, wzx_ref[:, :wp])
    masks = {k: masks_ref[:, k : k + 1] for k in (1, 2, 3)}
    linked = link_bias(seqc_ref[...], seqr_ref[...], False)
    neg_ref[...] = jnp.where(linked, 0.0, far)
    dt = step_parts(pb_ref[:, wp + 256 :], bias_ref[...])
    decay = mm_exact(jnp.where(linked, 1.0, 0.0), -dt * rate_ref[...])
    decay_t = decay.T
    terms = conv_terms(pb_ref[:, wp : wp + 256], masks)
    bcc = sum(t * convs_ref[k : k + 1, :] for k, t in enumerate(terms))
    bcc = (bcc * jax.nn.sigmoid(bcc)).astype(bf16)
    g_ref[...] = mm_nt(bcc[:, 128:], bcc[:, :128])

    for p in range(wp // LANES):
        cols = slice(p * LANES, (p + 1) * LANES)
        width = HD * min(2, heads - 2 * p)
        conv = sum(t * convx_ref[k : k + 1, cols] for k, t in enumerate(conv_terms(pb_ref[:, cols], masks)))
        xc = conv * jax.nn.sigmoid(conv)
        xdt_ref[...] = (xc * spread_heads(dt, 2 * p, width)).astype(bf16)
        blocks = []
        for a in range(rows // span):
            here = slice(a * span, (a + 1) * span)
            reach = (a + 1) * span
            sides = []
            for h in range(2 * p, 2 * p + width // HD):
                gap = decay[here, h : h + 1] - decay_t[h : h + 1, :reach]
                mixing = g_ref[here, :reach] * jnp.exp(gap + neg_ref[here, :reach])
                sides.append(mm(mixing.astype(bf16), xdt_ref[:reach, :]))
            blocks.append(sides[0] if len(sides) == 1 else jnp.where(half_mask(span, 0), sides[0], sides[1]))
        y = jnp.concatenate(blocks, axis=0) + skip_ref[:, cols] * xc
        y_ref[:, cols] = y
        z = pa_ref[:, cols]
        cat_ref[:, cols] = (y * (z * jax.nn.sigmoid(z))).astype(bf16)

    cosine, sine = cos_ref[...], sin_ref[...]
    pair = pa_ref[:, wp + qwp :]
    swapped = pltpu.roll(pair, HD, 1)
    lower = half_mask(rows, 0)
    keys = rotated(jnp.where(lower, pair, swapped), cosine, sine).astype(bf16)
    values = jnp.where(lower, swapped, pair).astype(bf16)
    for p in range(qwp // LANES):
        cols = slice(wp + p * LANES, wp + (p + 1) * LANES)
        queries = rotated(pa_ref[:, cols], cosine, sine).astype(bf16)
        for a in range(rows // span):
            here = slice(a * span, (a + 1) * span)
            reach = (a + 1) * span
            sides = []
            for side in range(min(2, qheads - 2 * p)):
                q = jnp.where(half_mask(span, side), queries[here], jnp.zeros((), bf16))
                scores = mm_nt(q, keys[:reach]) * (HD**-0.5) + neg_ref[here, :reach]
                weights = jnp.exp(scores - jnp.max(scores, axis=-1, keepdims=True))
                probs = weights / jnp.sum(weights, axis=-1, keepdims=True)
                sides.append(mm(probs.astype(bf16), values[:reach]))
            if len(sides) == 1:
                out = jnp.where(half_mask(span, 0), sides[0], 0.0)
            else:
                out = jnp.where(half_mask(span, 0), sides[0], sides[1])
            cat_ref[here, cols] = out.astype(bf16)
    part_ref[...] = (mm_nt(cat_ref[:, :wp], wmix_ref[...]) + mm_nt(cat_ref[:, wp:], watt_ref[...])).astype(bf16)


def middle_kernel(
    x_ref, own_ref, other_ref, gain_ref, wgu_ref, down_ref, dhid_ref,
    h1_ref, n2_ref, hidden_ref, dgu_ref, out_ref, dn2_ref,
):
    width = down_ref.shape[1]
    h1 = x_ref[...].astype(f32) + (own_ref[...].astype(f32) + other_ref[...].astype(f32))
    h1_ref[...] = h1
    n2 = (h1 * lax.rsqrt(jnp.mean(h1 * h1, axis=-1, keepdims=True) + norm_eps) * gain_ref[...]).astype(bf16)
    n2_ref[...] = n2
    gate = mm(n2, wgu_ref[:, :width])
    up = mm(n2, wgu_ref[:, width:])
    sig = jax.nn.sigmoid(gate)
    silu = gate * sig
    hidden = (silu * up).astype(bf16)
    hidden_ref[...] = hidden
    dhid = dhid_ref[...].astype(f32)
    dgu_ref[:, :width] = (dhid * up * (sig * (1.0 + gate * (1.0 - sig)))).astype(bf16)
    dgu_ref[:, width:] = (dhid * silu).astype(bf16)
    dn2_ref[...] = mm_nt(dgu_ref[...], wgu_ref[...]).astype(bf16)
    out_ref[...] = mm_nt(hidden, down_ref[...]).astype(bf16)


def attend_back_kernel(
    dims, share, place_ref, own_ref, other_ref, ffn_ref, h1_ref, dout_ref, gain2_ref, wmix_ref, watt_ref, seqc_ref,
    seqr_ref, cos_ref, sin_ref, pa_ref, y_ref,
    dh1_ref, ffn_send_ref, dmix_ref, dy_ref, da_ref, gn2_ref,
    neg_ref, dh1_all_ref, datt_ref, dk_ref, dv_ref,
):
    heads, qheads, wp, qwp, span = dims
    rows = own_ref.shape[0]
    dn2 = own_ref[...].astype(f32) + other_ref[...].astype(f32)
    h1 = h1_ref[...]
    r2 = lax.rsqrt(jnp.mean(h1 * h1, axis=-1, keepdims=True) + norm_eps)
    u = dn2 * gain2_ref[...]
    dh1 = dout_ref[...].astype(f32) + r2 * u - h1 * (r2 * r2 * r2 * jnp.mean(u * h1, axis=-1, keepdims=True))
    gn2_ref[...] = jnp.sum(dn2 * h1 * r2, axis=0, keepdims=True)
    dh1_all_ref[...] = dh1
    dh1_ref[...] = dh1_all_ref[pl.ds(pl.multiple_of(place_ref[0] * share, 16), share), :]
    ffn_send_ref[...] = ffn_ref[pl.ds(pl.multiple_of(place_ref[1] * share, 16), share), :]
    dmix = dh1.astype(bf16)
    dmix_ref[...] = dmix
    datt_ref[...] = mm(dmix, watt_ref[...]).astype(bf16)
    for p in range(wp // LANES):
        cols = slice(p * LANES, (p + 1) * LANES)
        dgated = mm(dmix, wmix_ref[:, cols])
        z = pa_ref[:, cols]
        sig = jax.nn.sigmoid(z)
        dy_ref[:, cols] = dgated * (z * sig)
        da_ref[:, cols] = (dgated * y_ref[:, cols] * (sig * (1.0 + z * (1.0 - sig)))).astype(bf16)

    linked_t = link_bias(seqc_ref[...], seqr_ref[...], True)
    neg_ref[...] = jnp.where(linked_t, 0.0, far)
    lower = half_mask(rows, 0)
    cosine, sine = cos_ref[...], sin_ref[...]
    pair = pa_ref[:, wp + qwp :]
    swapped = pltpu.roll(pair, HD, 1)
    keys = rotated(jnp.where(lower, pair, swapped), cosine, sine).astype(bf16)
    values = jnp.where(lower, swapped, pair).astype(bf16)
    dk_ref[...] = jnp.zeros_like(dk_ref)
    dv_ref[...] = jnp.zeros_like(dv_ref)
    for p in range(qwp // LANES):
        cols = slice(wp + p * LANES, wp + (p + 1) * LANES)
        queries = rotated(pa_ref[:, cols], cosine, sine).astype(bf16)
        datt = datt_ref[:, p * LANES : (p + 1) * LANES]
        blocks = []
        for a in range(rows // span):
            here = slice(a * span, (a + 1) * span)
            reach = (a + 1) * span
            sides = []
            for side in range(min(2, qheads - 2 * p)):
                half = half_mask(span, side)
                q = jnp.where(half, queries[here], jnp.zeros((), bf16))
                do = jnp.where(half, datt[here], jnp.zeros((), bf16))
                scores = mm_nt(keys[:reach], q) * (HD**-0.5) + neg_ref[:reach, here]
                weights = jnp.exp(scores - jnp.max(scores, axis=0, keepdims=True))
                probs = weights / jnp.sum(weights, axis=0, keepdims=True)
                dp = mm_nt(values[:reach], do)
                ds = (probs * (dp - jnp.sum(probs * dp, axis=0, keepdims=True))).astype(bf16)
                dk_ref[:reach, :] += mm(ds, q)
                dv_ref[:reach, :] += mm(probs.astype(bf16), do)
                sides.append(mm_tn(ds, keys[:reach]))
            if len(sides) == 1:
                blocks.append(jnp.where(half_mask(span, 0), sides[0], 0.0))
            else:
                blocks.append(jnp.where(half_mask(span, 0), sides[0], sides[1]))
        dq = jnp.concatenate(blocks, axis=0) * (HD**-0.5)
        da_ref[:, cols] = rotated(dq, cosine, -sine).astype(bf16)
    dk = dk_ref[...] * (HD**-0.5)
    dk = rotated(dk + pltpu.roll(dk, HD, 1), cosine, -sine)
    dv = dv_ref[...]
    dv = dv + pltpu.roll(dv, HD, 1)
    da_ref[:, wp + qwp :] = jnp.where(lower, dk, dv).astype(bf16)


def mixer_back_kernel(
    dims, dy_ref, da_ref, x_ref, wzx_ref, wbc_ref, wq_ref, wsp_ref, seqc_ref, seqr_ref, masks_ref,
    convx_ref, convs_ref, bias_ref, rate_ref, skip_ref, pb_ref, y_ref,
    dxs_ref, dbc_ref, dact_ref, gn1_ref, gcx_ref, gcs_ref, gstep_ref, gskip_ref,
    neg_ref, gt_ref, dgt_ref, dsum_ref, ddir_ref,
):
    heads, qheads, wp, qwp, span = dims
    rows = x_ref.shape[0]
    masks = {k: masks_ref[:, k : k + 1] for k in (1, 2, 3)}
    linked_t = link_bias(seqc_ref[...], seqr_ref[...], True)
    neg_ref[...] = jnp.where(linked_t, 0.0, far)
    dt = step_parts(pb_ref[:, wp + 256 :], bias_ref[...])
    linked = link_bias(seqc_ref[...], seqr_ref[...], False)
    decay = mm_exact(jnp.where(linked, 1.0, 0.0), -dt * rate_ref[...])
    decay_t = decay.T
    state = pb_ref[:, wp : wp + 256]
    sterms = conv_terms(state, masks)
    sconv = sum(t * convs_ref[k : k + 1, :] for k, t in enumerate(sterms))
    ssig = jax.nn.sigmoid(sconv)
    bcc = (sconv * ssig).astype(bf16)
    bm, cm = bcc[:, :128], bcc[:, 128:]
    gt_ref[...] = mm_nt(bm, cm)
    dgt_ref[...] = jnp.zeros_like(dgt_ref)
    for p in range(wp // LANES):
        cols = slice(p * LANES, (p + 1) * LANES)
        width = HD * min(2, heads - 2 * p)
        terms = conv_terms(pb_ref[:, cols], masks)
        conv = sum(t * convx_ref[k : k + 1, cols] for k, t in enumerate(terms))
        csig = jax.nn.sigmoid(conv)
        xc = conv * csig
        dt_cols = spread_heads(dt, 2 * p, width)
        xdt = (xc * dt_cols).astype(bf16)
        skip = skip_ref[:, cols]
        scanned = y_ref[:, cols] - skip * xc
        dy = dy_ref[:, cols]
        gskip_ref[:, cols] = jnp.sum(dy * xc, axis=0, keepdims=True)
        dyb = dy.astype(bf16)
        blocks = []
        for a in range(rows // span):
            here = slice(a * span, (a + 1) * span)
            sides = []
            for side in range(width // HD):
                h = 2 * p + side
                dys = jnp.where(half_mask(rows - a * span, side), dyb[a * span :], jnp.zeros((), bf16))
                gap = decay_t[h : h + 1, a * span :] - decay[here, h : h + 1]
                falloff = jnp.exp(gap + neg_ref[here, a * span :])
                mixing = (gt_ref[here, a * span :] * falloff).astype(bf16)
                sides.append(mm(mixing, dyb[a * span :]))
                dgt_ref[here, a * span :] += mm_nt(xdt[here], dys) * falloff
            blocks.append(sides[0] if len(sides) == 1 else jnp.where(half_mask(span, 0), sides[0], sides[1]))
        dxdt = jnp.concatenate(blocks, axis=0)
        dsum_ref[:, cols] = dyb.astype(f32) * scanned - xdt.astype(f32) * dxdt
        ddir_ref[:, cols] = dxdt * xc
        dconv = (dxdt * dt_cols + skip * dy) * (csig * (1.0 + conv * (1.0 - csig)))
        gcx_ref[:, cols] = jnp.concatenate([jnp.sum(t * dconv, axis=0, keepdims=True) for t in terms], axis=0)
        dxs_ref[:, cols] = conv_back(dconv, masks, convx_ref[:, cols]).astype(bf16)

    dgt = dgt_ref[...].astype(bf16)
    dbcc = jnp.concatenate([mm(dgt, cm), mm_tn(dgt, bm)], axis=1)
    dsconv = dbcc * (ssig * (1.0 + sconv * (1.0 - ssig)))
    gcs_ref[...] = jnp.concatenate([jnp.sum(t * dsconv, axis=0, keepdims=True) for t in sterms], axis=0)
    dbc_ref[...] = conv_back(dsconv, masks, convs_ref[...]).astype(bf16)

    head_of = lax.broadcasted_iota(jnp.int32, (wp, LANES), 0) // HD
    pick = jnp.where(head_of == lax.broadcasted_iota(jnp.int32, (wp, LANES), 1), 1.0, 0.0)
    ds = mm_exact(dsum_ref[...], pick)
    ddirect = mm_exact(ddir_ref[...], pick)
    dlog = mm_exact(jnp.where(linked_t, 1.0, 0.0), ds)
    rate = rate_ref[...]
    ddt = ddirect - rate * dlog
    dstep = ddt * jax.nn.sigmoid(pb_ref[:, wp + 256 :] + bias_ref[...])
    dstep = jnp.where(lane_ids(rows) < heads, dstep, 0.0)
    dxs_ref[:, wp:] = dstep.astype(bf16)
    gstep_ref[...] = jnp.concatenate(
        [jnp.sum(dstep, axis=0, keepdims=True), -rate * jnp.sum(dt * dlog, axis=0, keepdims=True)], axis=0
    )
    dact = mm_nt(da_ref[:, :wp], wzx_ref[:, :wp]) + mm_nt(dxs_ref[:, :wp], wzx_ref[:, wp:])
    dact = dact + mm_nt(dbc_ref[...], wbc_ref[...]) + mm_nt(da_ref[:, wp : wp + qwp], wq_ref[...])
    dact = dact + mm_nt(dxs_ref[:, wp:], wsp_ref[:, :LANES]) + mm_nt(da_ref[:, wp + qwp :], wsp_ref[:, LANES:])
    dact_ref[...] = dact.astype(bf16)
    x = x_ref[...].astype(f32)
    r1 = lax.rsqrt(jnp.mean(x * x, axis=-1, keepdims=True) + norm_eps)
    gn1_ref[...] = jnp.sum(dact * x * r1, axis=0, keepdims=True)


def grad_kernel(pairs, block, *refs):
    bit_ref, ins = refs[0], refs[1 : 1 + 2 * pairs]
    outs, turned = refs[1 + 2 * pairs : -1], refs[-1]
    bit = bit_ref[0]
    for k in range(pairs):
        left, right = ins[2 * k], ins[2 * k + 1]
        turned[...] = left[...].astype(f32).T.astype(bf16)
        count = turned.shape[0] // (2 * block)
        for side, out in enumerate(outs[2 * k : 2 * k + 2]):
            which = 1 - bit if side == 0 else bit
            for i in range(count):
                start = pl.multiple_of((2 * i + which) * block, block)
                out[i * block : (i + 1) * block, :] = mm(turned[pl.ds(start, block), :], right[...]).astype(bf16)


def weight_halves(pairs, bit, block, after=()):
    args = [bit] + [a for pair in pairs for a in pair]
    outs = [((left.shape[1] // 2, right.shape[1]), bf16) for left, right in pairs for _ in range(2)]
    left = pairs[0][0]
    return call(
        functools.partial(grad_kernel, len(pairs), block), outs, [((left.shape[1], left.shape[0]), bf16)], args, 20, 1,
        after,
    )


def step_kernel(block, which_ref, kept_ref, arrived_ref, away_ref, mine_ref):
    which = which_ref[0]
    for out, side in ((away_ref, 1 - which), (mine_ref, which)):
        for i in range(kept_ref.shape[0] // (2 * block)):
            start = pl.multiple_of((2 * i + side) * block, block)
            total = kept_ref[pl.ds(start, block), :].astype(f32) + arrived_ref[pl.ds(start, block), :].astype(f32)
            out[i * block : (i + 1) * block, :] = total.astype(bf16)


def add_kernel(a_ref, b_ref, out_ref):
    out_ref[...] = a_ref[...] + b_ref[...]


def call(kernel, outs, scratch, args, megabytes, scalars=0, after=()):
    count = len(args)

    def wrapped(*refs):
        kernel(*refs[:count], *refs[count + len(after) :])

    spaces = [pltpu.SMEM] * scalars + [pltpu.VMEM] * (count - scalars) + [pl.ANY] * len(after)
    return pl.pallas_call(
        wrapped,
        out_shape=[jax.ShapeDtypeStruct(s, t) for s, t in outs],
        in_specs=[pl.BlockSpec(memory_space=space) for space in spaces],
        out_specs=[pl.BlockSpec(memory_space=pltpu.VMEM)] * len(outs),
        scratch_shapes=[pltpu.VMEM(s, t) for s, t in scratch],
        compiler_params=pltpu.CompilerParams(vmem_limit_bytes=megabytes * 1024 * 1024),
        cost_estimate=pl.CostEstimate(flops=1000, bytes_accessed=1000, transcendentals=0),
    )(*args, *after)


def swap(values):
    return lax.ppermute(values, "tensor", [(0, 1), (1, 0)])


def gather_rows(values, me, count):
    if count != 2:
        return lax.all_gather(values, "tensor", axis=0, tiled=True)
    other = swap(values)
    first = jnp.where(me == 0, values, other)
    return jnp.concatenate([first, jnp.where(me == 0, other, values)], axis=0)


def both_parts(part, count):
    if count != 2:
        return (lax.psum(part, "tensor"), jnp.zeros_like(part))
    return (part, swap(part))


def scatter_rows(part, me, count):
    if count != 2:
        return lax.psum_scatter(part, "tensor", scatter_dimension=0, tiled=True).astype(f32)
    halves = part.reshape(2, part.shape[0] // 2, part.shape[1])
    arrived = swap(lax.dynamic_index_in_dim(halves, 1 - me, 0, keepdims=False))
    return lax.dynamic_index_in_dim(halves, me, 0, keepdims=False).astype(f32) + arrived.astype(f32)


def partners(count, bit):
    return [(i, i ^ bit) for i in range(count)]


def exchange(sent, count, bit):
    return lax.ppermute(sent, "dp", partners(count, bit))


class Reduction:
    def __init__(self, sent, kept, index, count, block):
        self.index, self.count, self.block, self.bit = index, count, block, 1
        self.kept, self.sent = kept, sent
        self.arrived = exchange(sent, count, 1)

    def done(self):
        return self.bit * 2 >= self.count

    def step(self, after=()):
        if self.done():
            return after
        self.bit *= 2
        which = ((self.index // self.bit) % 2).astype(jnp.int32).reshape(1)
        half = (self.kept.shape[0] // 2, self.kept.shape[1])
        self.sent, self.kept = call(
            functools.partial(step_kernel, self.block), [(half, bf16), (half, bf16)], [],
            (which, self.kept, self.arrived), 16, 1, after,
        )
        self.arrived = exchange(self.sent, self.count, self.bit)
        return (self.sent,)

    def total(self):
        return self.kept.astype(f32) + self.arrived.astype(f32)


def segments(lengths, row_count):
    seq_ends = jnp.cumsum(lengths)
    places = jnp.arange(row_count, dtype=jnp.int32)
    passed = places[:, None] >= seq_ends[None, :]
    seq_ids = jnp.sum(passed.astype(jnp.int32), axis=1)
    starts = jnp.max(jnp.where(passed, seq_ends[None, :], 0), axis=1)
    is_live = (places < seq_ends[-1]).astype(f32)
    return (seq_ids, places - starts, is_live)


def body(
    dp_count, tensor_count, tokens, cotangent, seq_lengths, norm1_gain, norm2_gain, mixer_in, state_in, step_in,
    conv_inner, conv_state, step_bias, decay_log, skip_gain, mixer_out, query_in, key_value, attend_out, gate_up,
    down_out,
):
    share, model = tokens.shape
    rows = share * tensor_count
    me = lax.axis_index("tensor")
    index = lax.axis_index("dp")
    inner = mixer_in.shape[2]
    heads = step_in.shape[1]
    query_width = query_in.shape[1]
    qheads = query_width // HD
    wp, qwp = padded(inner), padded(query_width)
    span = min(LANES, rows)
    dims = (heads, qheads, wp, qwp, span)

    x_rows = gather_rows(tokens, me, tensor_count)
    seq_ids, positions, is_live = segments(seq_lengths[0], rows)
    live_share = lax.dynamic_slice_in_dim(is_live, me * share, share, 0)[:, None]
    dout_rows = gather_rows(lax.optimization_barrier((cotangent, x_rows))[0], me, tensor_count)
    dout_rows = dout_rows * is_live[:, None].astype(bf16)

    seq_col = seq_ids.astype(f32)[:, None]
    seq_row = seq_ids.astype(f32)[None, :]
    shifts = jnp.minimum(jnp.arange(LANES, dtype=jnp.int32), 4)[None, :]
    masks = (positions[:, None] >= shifts).astype(f32)
    lane = jnp.arange(LANES)
    frequency = rope_base ** (-2.0 * jnp.arange(HD // 2, dtype=f32) / HD)
    angles = positions.astype(f32)[:, None] * frequency[None, :]
    cosine = jnp.tile(jnp.cos(angles), (1, 4))
    sine = jnp.tile(jnp.sin(angles), (1, 4)) * jnp.where(lane % HD < HD // 2, -1.0, 1.0)[None, :]

    key_index = me * qheads // (QH // KVH)
    pair_local = lax.dynamic_slice_in_dim(key_value, key_index * HD, HD, 2).reshape(model, 2 * HD)
    if inner == wp:
        wzx = mixer_in.reshape(model, 2 * inner)
    else:
        wzx = pad_to(mixer_in, wp).reshape(model, 2 * wp)
    wsp = jnp.concatenate([pad_to(step_in, LANES), pair_local], axis=1)
    wq, wmix, watt = pad_to(query_in, qwp), pad_to(mixer_out, wp), pad_to(attend_out, qwp)
    wgu = gate_up.reshape(model, -1)
    taps = pad_to(conv_inner, wp)
    bias = pad_to(step_bias[None], LANES)
    rate = pad_to(jnp.exp(decay_log)[None], LANES)
    skip = pad_to(jnp.repeat(skip_gain, HD)[None], wp)
    gain1, gain2 = norm1_gain[None], norm2_gain[None]

    act, pa, pb, y, cat, part = call(
        functools.partial(front_kernel, dims),
        [
            ((rows, model), bf16), ((rows, wp + qwp + LANES), f32), ((rows, wp + 384), f32), ((rows, wp), f32),
            ((rows, wp + qwp), bf16), ((rows, model), bf16),
        ],
        [((rows, rows), f32), ((rows, rows), f32), ((rows, LANES), bf16)],
        (
            x_rows, gain1, wzx, state_in, wq, wsp, wmix, watt, seq_col, seq_row, masks, cosine, sine, taps, conv_state,
            bias, rate, skip,
        ),
        24,
    )
    dhidden = mm(dout_rows, down_out)
    own, other = both_parts(part, tensor_count)
    ff2 = wgu.shape[1]
    h1, n2, hidden, dgu, ffn_part, dn2_part = call(
        middle_kernel,
        [
            ((rows, model), f32), ((rows, model), bf16), ((rows, ff2 // 2), bf16), ((rows, ff2), bf16),
            ((rows, model), bf16), ((rows, model), bf16),
        ],
        [],
        (x_rows, own, other, gain2, wgu, down_out, dhidden),
        28,
    )
    dn2_own, dn2_other = both_parts(dn2_part, tensor_count)

    bit = (index % 2).astype(jnp.int32).reshape(1)
    block = model // dp_count
    reduction = lambda sent, kept: Reduction(sent, kept, index, dp_count, block)
    down_sent, down_kept, up_sent, up_kept = weight_halves([(dout_rows, hidden), (n2, dgu)], bit, block)
    down = reduction(down_sent, down_kept)
    up = reduction(up_sent, up_kept)
    order = down.step()
    order = up.step(order)

    place = jnp.stack([me, lax.rem(me + 1, tensor_count)]).astype(jnp.int32)
    dh1_share, ffn_send, dmix, dy, da, gn2 = call(
        functools.partial(attend_back_kernel, dims, share),
        [
            ((share, model), f32), ((share, model), bf16), ((rows, model), bf16), ((rows, wp), f32),
            ((rows, wp + qwp + LANES), bf16), ((1, model), f32),
        ],
        [((rows, rows), f32), ((rows, model), f32), ((rows, qwp), bf16), ((rows, LANES), f32), ((rows, LANES), f32)],
        (
            place, dn2_own, dn2_other, ffn_part, h1, dout_rows, gain2, wmix, watt, seq_col, seq_row, cosine, sine, pa, y,
        ),
        28, 1, order,
    )
    out_sent, out_kept, first_sent, first_kept = weight_halves([(dmix, cat), (act, da)], bit, block)
    out = reduction(out_sent, out_kept)
    first = reduction(first_sent, first_kept)
    order = down.step((out_kept,))
    order = out.step(order)
    order = first.step(order)

    dxs, dbc, dact, gn1, gcx, gcs, gstep, gskip = call(
        functools.partial(mixer_back_kernel, dims),
        [
            ((rows, wp + LANES), bf16), ((rows, 256), bf16), ((rows, model), bf16),
            ((1, model), f32), ((4, wp), f32), ((4, 256), f32), ((2, LANES), f32), ((1, wp), f32),
        ],
        [
            ((rows, rows), f32), ((rows, rows), f32), ((rows, rows), f32), ((rows, wp), f32), ((rows, wp), f32),
        ],
        (
            dy, da, x_rows, wzx, state_in, wq, wsp, seq_col, seq_row, masks, taps, conv_state, bias, rate, skip, pb, y,
        ),
        28, 0, order,
    )
    shared = jnp.concatenate([gn1[0], gn2[0] * (1.0 / tensor_count), gcs.reshape(-1)]).reshape(-1, LANES)
    local = jnp.concatenate([gcx.reshape(-1), gskip.reshape(-1), gstep.reshape(-1)]).reshape(-1, LANES)
    shared_rows = shared.shape[0]
    minor = jnp.concatenate([shared, local], axis=0)

    def minor_step(values, bit, after):
        arrived = exchange(values, dp_count, bit)
        return call(add_kernel, [(values.shape, f32)], [], (values, arrived), 4, 0, after)[0]

    second_sent, second_kept, state_sent, state_kept = weight_halves([(act, dxs), (act, dbc)], bit, block)
    second = reduction(second_sent, second_kept)
    state = reduction(state_sent, state_kept)
    order = up.step((second_kept,))
    order = second.step(order)
    order = state.step(order)
    order = down.step(order)
    minor_bit = 1
    waiting = [out, first, up, state, second, out, first, state, second]
    waiting += [r for _ in range(8) for r in (down, up, out, first, state, second)]
    for r in waiting:
        if r.done():
            continue
        if minor_bit < dp_count:
            minor = minor_step(minor, minor_bit, order)
            minor_bit *= 2
            order = (minor,)
        order = r.step(order)
    while minor_bit < dp_count:
        minor = minor_step(minor, minor_bit, order)
        minor_bit *= 2
    down_total, up_total, out_total = down.total(), up.total(), out.total()
    first_total, second_total, state_total = first.total(), second.total(), state.total()

    if tensor_count == 2:
        ffn_mine = lax.dynamic_slice_in_dim(ffn_part, me * share, share, 0).astype(f32)
        ffn_share = ffn_mine + swap(ffn_send).astype(f32)
    else:
        ffn_share = scatter_rows(ffn_part, me, tensor_count)
    h1_share = lax.dynamic_slice_in_dim(h1, me * share, share, 0)
    block_out = ((h1_share + ffn_share) * live_share).astype(bf16)

    dact_share = scatter_rows(dact, me, tensor_count)
    x_share = tokens.astype(f32)
    r1 = lax.rsqrt(jnp.mean(x_share * x_share, axis=-1, keepdims=True) + norm_eps)
    u = dact_share * gain1
    token_grad = dh1_share + r1 * u - x_share * (r1 * r1 * r1 * jnp.mean(u * x_share, axis=-1, keepdims=True))

    shared = lax.psum(minor[:shared_rows], "tensor") if tensor_count != 2 else minor[:shared_rows] + swap(minor[:shared_rows])
    shared = shared.reshape(-1)
    local = minor[shared_rows:].reshape(-1)
    g_norm1, g_norm2, g_conv_state = shared[:model], shared[model : 2 * model], shared[2 * model :].reshape(4, 256)
    g_conv_inner = local[: 4 * wp].reshape(4, wp)[:, :inner]
    g_skip = jnp.sum(local[4 * wp : 5 * wp].reshape(-1, HD), axis=1)[:heads]
    g_bias = local[5 * wp : 5 * wp + heads]
    g_decay = local[5 * wp + LANES : 5 * wp + LANES + heads]

    both = jnp.concatenate([state_total, first_total[:, wp + qwp :]], axis=1).astype(bf16)
    placed = lambda pair: lax.dynamic_update_slice_in_dim(
        jnp.zeros((block,) + key_value.shape[1:], f32), pair.astype(f32).reshape(block, 2, HD), key_index * HD, 2
    )
    if tensor_count == 2:
        arrived = swap(both)
        g_state = both[:, :256].astype(f32) + arrived[:, :256].astype(f32)
        mine = both[:, 256:].reshape(block, 2, HD)
        theirs = arrived[:, 256:].reshape(block, 2, HD)
        g_pair = jnp.concatenate(
            [jnp.where(me == 0, mine, theirs), jnp.where(me == 0, theirs, mine)], axis=2
        ).astype(f32)
    else:
        g_state = lax.psum(both[:, :256], "tensor").astype(f32)
        g_pair = lax.psum(placed(both[:, 256:]).astype(bf16), "tensor").astype(f32)

    g_mixer_in = jnp.stack([first_total[:, :inner], second_total[:, :inner]], axis=1)
    return (
        block_out,
        token_grad.astype(bf16),
        g_norm1,
        g_norm2,
        g_mixer_in,
        g_state,
        second_total[:, wp : wp + heads],
        g_conv_inner,
        g_conv_state,
        g_bias,
        g_decay,
        g_skip,
        out_total[:, :inner],
        first_total[:, wp : wp + query_width],
        g_pair,
        out_total[:, wp : wp + query_width],
        up_total.reshape(block, 2, ff2 // 2),
        down_total,
    )


def solution(mesh):
    return jax.shard_map(
        functools.partial(body, mesh.shape["dp"], mesh.shape["tensor"]),
        mesh=mesh,
        in_specs=(
            P(("dp", "tensor"), None),
            P(("dp", "tensor"), None),
            P("dp", None),
            P(),
            P(),
            P(None, None, "tensor"),
            P(),
            P(None, "tensor"),
            P(None, "tensor"),
            P(),
            P("tensor"),
            P("tensor"),
            P("tensor"),
            P(None, "tensor"),
            P(None, "tensor"),
            P(),
            P(None, "tensor"),
            P(None, None, "tensor"),
            P(None, "tensor"),
        ),
        out_specs=(
            P(("dp", "tensor"), None),
            P(("dp", "tensor"), None),
            P(),
            P(),
            P("dp", None, "tensor"),
            P("dp", None),
            P("dp", "tensor"),
            P(None, "tensor"),
            P(),
            P("tensor"),
            P("tensor"),
            P("tensor"),
            P("dp", "tensor"),
            P("dp", "tensor"),
            P("dp", None, None),
            P("dp", "tensor"),
            P("dp", None, "tensor"),
            P("dp", "tensor"),
        ),
        check_vma=False,
    )
```

```python
import functools

import jax
import jax.numpy as jnp
from jax import lax
from jax.experimental import pallas as pl
from jax.experimental.pallas import tpu as pltpu
from jax.sharding import PartitionSpec as P

HD = 64
QH = 8
KVH = 2
LANES = 128

rope_base = 100000000000.0
norm_eps = 1e-05
far = -1e30
highest = lax.Precision.HIGHEST
f32 = jnp.float32
bf16 = jnp.bfloat16


def padded(width):
    return -(-width // LANES) * LANES


def pad_to(values, width):
    return jnp.pad(values, [(0, 0)] * (values.ndim - 1) + [(0, width - values.shape[-1])])


def mm(left, right):
    return jnp.dot(left, right, preferred_element_type=f32)


def mm_nt(left, right):
    return lax.dot_general(left, right, (((1,), (1,)), ((), ())), preferred_element_type=f32)


def mm_tn(left, right):
    return lax.dot_general(left, right, (((0,), (0,)), ((), ())), preferred_element_type=f32)


def mm_exact(left, right):
    return jnp.dot(left, right, preferred_element_type=f32, precision=highest)


def lane_ids(rows):
    return lax.broadcasted_iota(jnp.int32, (rows, LANES), 1)


def partner_half(values):
    lane = lane_ids(values.shape[0])
    return jnp.where(lane % HD < HD // 2, pltpu.roll(values, LANES - HD // 2, 1), pltpu.roll(values, HD // 2, 1))


def rotated(values, cosine, signed_sine):
    return values * cosine + partner_half(values) * signed_sine


def conv_terms(values, masks):
    return [pltpu.roll(values, offset, 0) * masks[offset] for offset in (3, 2, 1)] + [values]


def conv_back(grad, masks, taps):
    rows = grad.shape[0]
    total = grad * taps[3:4]
    for offset in (1, 2, 3):
        total = total + pltpu.roll(grad * masks[offset], rows - offset, 0) * taps[3 - offset : 4 - offset]
    return total


def link_bias(seq_col, seq_row, transposed):
    rows = seq_col.shape[0]
    down = lax.broadcasted_iota(jnp.int32, (rows, rows), 0)
    across = lax.broadcasted_iota(jnp.int32, (rows, rows), 1)
    ordered = down <= across if transposed else down >= across
    return (seq_col == seq_row) & ordered


def step_parts(raw, bias):
    shifted = raw + bias
    return jnp.maximum(shifted, 0.0) + jnp.log1p(jnp.exp(-jnp.abs(shifted)))


def spread_heads(columns, first, width):
    rows = columns.shape[0]
    low = jnp.broadcast_to(columns[:, first : first + 1], (rows, LANES))
    if width <= HD:
        return low
    high = jnp.broadcast_to(columns[:, first + 1 : first + 2], (rows, LANES))
    return jnp.where(lane_ids(rows) < HD, low, high)


def half_mask(rows, side):
    lane = lane_ids(rows)
    return lane < HD if side == 0 else lane >= HD


def front_kernel(
    dims, place_ref, own_ref, other_ref, wbc_ref, wsp_ref, wzx_ref, wq_ref, wmix_ref, watt_ref, gain_ref, seqc_ref,
    seqr_ref, masks_ref, cos_ref, sin_ref, convx_ref, convs_ref, bias_ref, rate_ref, skip_ref,
    x_ref, act_ref, pa_ref, pb_ref, y_ref, cat_ref, part_ref, neg_ref, g_ref, xdt_ref,
):
    heads, qheads, wp, qwp, span = dims
    rows = x_ref.shape[0]
    share = own_ref.shape[0]
    if share == rows:
        x_ref[...] = own_ref[...]
    else:
        x_ref[pl.ds(pl.multiple_of(place_ref[0] * share, 16), share), :] = own_ref[...]
        x_ref[pl.ds(pl.multiple_of(place_ref[1] * share, 16), share), :] = other_ref[...]
    finish(x_ref)
    x = x_ref[...].astype(f32)
    act = (x * lax.rsqrt(jnp.mean(x * x, axis=-1, keepdims=True) + norm_eps) * gain_ref[...]).astype(bf16)
    act_ref[...] = act
    finish(act_ref)
    pb_ref[:, wp : wp + 256] = mm(act, wbc_ref[...])
    pb_ref[:, wp + 256 :] = mm(act, wsp_ref[:, :LANES])
    pb_ref[:, :wp] = mm(act, wzx_ref[:, wp:])
    pa_ref[:, wp : wp + qwp] = mm(act, wq_ref[...])
    pa_ref[:, wp + qwp :] = mm(act, wsp_ref[:, LANES:])
    pa_ref[:, :wp] = mm(act, wzx_ref[:, :wp])
    finish(pa_ref, pb_ref)
    masks = {k: masks_ref[:, k : k + 1] for k in (1, 2, 3)}
    linked = link_bias(seqc_ref[...], seqr_ref[...], False)
    neg_ref[...] = jnp.where(linked, 0.0, far)
    dt = step_parts(pb_ref[:, wp + 256 :], bias_ref[...])
    decay = mm_exact(jnp.where(linked, 1.0, 0.0), -dt * rate_ref[...])
    decay_t = decay.T
    terms = conv_terms(pb_ref[:, wp : wp + 256], masks)
    bcc = sum(t * convs_ref[k : k + 1, :] for k, t in enumerate(terms))
    bcc = (bcc * jax.nn.sigmoid(bcc)).astype(bf16)
    g_ref[...] = mm_nt(bcc[:, 128:], bcc[:, :128])

    for p in range(wp // LANES):
        cols = slice(p * LANES, (p + 1) * LANES)
        width = HD * min(2, heads - 2 * p)
        conv = sum(t * convx_ref[k : k + 1, cols] for k, t in enumerate(conv_terms(pb_ref[:, cols], masks)))
        xc = conv * jax.nn.sigmoid(conv)
        xdt_ref[...] = (xc * spread_heads(dt, 2 * p, width)).astype(bf16)
        blocks = []
        for a in range(rows // span):
            here = slice(a * span, (a + 1) * span)
            reach = (a + 1) * span
            sides = []
            for h in range(2 * p, 2 * p + width // HD):
                gap = decay[here, h : h + 1] - decay_t[h : h + 1, :reach]
                mixing = g_ref[here, :reach] * jnp.exp(gap + neg_ref[here, :reach])
                sides.append(mm(mixing.astype(bf16), xdt_ref[:reach, :]))
            blocks.append(sides[0] if len(sides) == 1 else jnp.where(half_mask(span, 0), sides[0], sides[1]))
        y = jnp.concatenate(blocks, axis=0) + skip_ref[:, cols] * xc
        y_ref[:, cols] = y
        z = pa_ref[:, cols]
        cat_ref[:, cols] = (y * (z * jax.nn.sigmoid(z))).astype(bf16)

    finish(y_ref)
    cosine, sine = cos_ref[...], sin_ref[...]
    pair = pa_ref[:, wp + qwp :]
    swapped = pltpu.roll(pair, HD, 1)
    lower = half_mask(rows, 0)
    keys = rotated(jnp.where(lower, pair, swapped), cosine, sine).astype(bf16)
    values = jnp.where(lower, swapped, pair).astype(bf16)
    for p in range(qwp // LANES):
        cols = slice(wp + p * LANES, wp + (p + 1) * LANES)
        queries = rotated(pa_ref[:, cols], cosine, sine).astype(bf16)
        for a in range(rows // span):
            here = slice(a * span, (a + 1) * span)
            reach = (a + 1) * span
            sides = []
            for side in range(min(2, qheads - 2 * p)):
                q = jnp.where(half_mask(span, side), queries[here], jnp.zeros((), bf16))
                scores = mm_nt(q, keys[:reach]) * (HD**-0.5) + neg_ref[here, :reach]
                weights = jnp.exp(scores - jnp.max(scores, axis=-1, keepdims=True))
                probs = weights / jnp.sum(weights, axis=-1, keepdims=True)
                sides.append(mm(probs.astype(bf16), values[:reach]))
            if len(sides) == 1:
                out = jnp.where(half_mask(span, 0), sides[0], 0.0)
            else:
                out = jnp.where(half_mask(span, 0), sides[0], sides[1])
            cat_ref[here, cols] = out.astype(bf16)
    finish(cat_ref)
    part_ref[...] = (mm_nt(cat_ref[:, :wp], wmix_ref[...]) + mm_nt(cat_ref[:, wp:], watt_ref[...])).astype(bf16)


def middle_kernel(
    x_ref, own_ref, other_ref, gain_ref, wgu_ref, down_ref, dhid_ref,
    h1_ref, n2_ref, hidden_ref, dgu_ref, out_ref, dn2_ref,
):
    width = down_ref.shape[1]
    h1 = x_ref[...].astype(f32) + (own_ref[...].astype(f32) + other_ref[...].astype(f32))
    h1_ref[...] = h1
    finish(h1_ref)
    n2 = (h1 * lax.rsqrt(jnp.mean(h1 * h1, axis=-1, keepdims=True) + norm_eps) * gain_ref[...]).astype(bf16)
    n2_ref[...] = n2
    finish(n2_ref)
    gate = mm(n2, wgu_ref[:, :width])
    up = mm(n2, wgu_ref[:, width:])
    sig = jax.nn.sigmoid(gate)
    silu = gate * sig
    hidden = (silu * up).astype(bf16)
    hidden_ref[...] = hidden
    finish(hidden_ref)
    dhid = dhid_ref[...].astype(f32)
    dgu_ref[:, :width] = (dhid * up * (sig * (1.0 + gate * (1.0 - sig)))).astype(bf16)
    dgu_ref[:, width:] = (dhid * silu).astype(bf16)
    finish(dgu_ref)
    dn2_ref[...] = mm_nt(dgu_ref[...], wgu_ref[...]).astype(bf16)
    finish(dn2_ref)
    out_ref[...] = mm_nt(hidden, down_ref[...]).astype(bf16)


def attend_back_kernel(
    dims, share, place_ref, own_ref, other_ref, ffn_ref, h1_ref, dout_ref, gain2_ref, wmix_ref, watt_ref, seqc_ref,
    seqr_ref, cos_ref, sin_ref, pa_ref, y_ref,
    dh1_ref, ffn_send_ref, dmix_ref, dy_ref, da_ref, gn2_ref,
    neg_ref, dh1_all_ref, datt_ref, dk_ref, dv_ref,
):
    heads, qheads, wp, qwp, span = dims
    rows = own_ref.shape[0]
    dn2 = own_ref[...].astype(f32) + other_ref[...].astype(f32)
    h1 = h1_ref[...]
    r2 = lax.rsqrt(jnp.mean(h1 * h1, axis=-1, keepdims=True) + norm_eps)
    u = dn2 * gain2_ref[...]
    dh1 = dout_ref[...].astype(f32) + r2 * u - h1 * (r2 * r2 * r2 * jnp.mean(u * h1, axis=-1, keepdims=True))
    gn2_ref[...] = jnp.sum(dn2 * h1 * r2, axis=0, keepdims=True)
    dh1_all_ref[...] = dh1
    dh1_ref[...] = dh1_all_ref[pl.ds(pl.multiple_of(place_ref[0] * share, 16), share), :]
    ffn_send_ref[...] = ffn_ref[pl.ds(pl.multiple_of(place_ref[1] * share, 16), share), :]
    dmix = dh1.astype(bf16)
    dmix_ref[...] = dmix
    finish(dh1_ref, ffn_send_ref, dmix_ref)
    datt_ref[...] = mm(dmix, watt_ref[...]).astype(bf16)
    for p in range(wp // LANES):
        cols = slice(p * LANES, (p + 1) * LANES)
        dgated = mm(dmix, wmix_ref[:, cols])
        z = pa_ref[:, cols]
        sig = jax.nn.sigmoid(z)
        dy_ref[:, cols] = dgated * (z * sig)
        da_ref[:, cols] = (dgated * y_ref[:, cols] * (sig * (1.0 + z * (1.0 - sig)))).astype(bf16)
    finish(dy_ref)

    linked_t = link_bias(seqc_ref[...], seqr_ref[...], True)
    neg_ref[...] = jnp.where(linked_t, 0.0, far)
    lower = half_mask(rows, 0)
    cosine, sine = cos_ref[...], sin_ref[...]
    pair = pa_ref[:, wp + qwp :]
    swapped = pltpu.roll(pair, HD, 1)
    keys = rotated(jnp.where(lower, pair, swapped), cosine, sine).astype(bf16)
    values = jnp.where(lower, swapped, pair).astype(bf16)
    dk_ref[...] = jnp.zeros_like(dk_ref)
    dv_ref[...] = jnp.zeros_like(dv_ref)
    for p in range(qwp // LANES):
        cols = slice(wp + p * LANES, wp + (p + 1) * LANES)
        queries = rotated(pa_ref[:, cols], cosine, sine).astype(bf16)
        datt = datt_ref[:, p * LANES : (p + 1) * LANES]
        blocks = []
        for a in range(rows // span):
            here = slice(a * span, (a + 1) * span)
            reach = (a + 1) * span
            sides = []
            for side in range(min(2, qheads - 2 * p)):
                half = half_mask(span, side)
                q = jnp.where(half, queries[here], jnp.zeros((), bf16))
                do = jnp.where(half, datt[here], jnp.zeros((), bf16))
                scores = mm_nt(keys[:reach], q) * (HD**-0.5) + neg_ref[:reach, here]
                weights = jnp.exp(scores - jnp.max(scores, axis=0, keepdims=True))
                probs = weights / jnp.sum(weights, axis=0, keepdims=True)
                dp = mm_nt(values[:reach], do)
                ds = (probs * (dp - jnp.sum(probs * dp, axis=0, keepdims=True))).astype(bf16)
                dk_ref[:reach, :] += mm(ds, q)
                dv_ref[:reach, :] += mm(probs.astype(bf16), do)
                sides.append(mm_tn(ds, keys[:reach]))
            if len(sides) == 1:
                blocks.append(jnp.where(half_mask(span, 0), sides[0], 0.0))
            else:
                blocks.append(jnp.where(half_mask(span, 0), sides[0], sides[1]))
        dq = jnp.concatenate(blocks, axis=0) * (HD**-0.5)
        da_ref[:, cols] = rotated(dq, cosine, -sine).astype(bf16)
    dk = dk_ref[...] * (HD**-0.5)
    dk = rotated(dk + pltpu.roll(dk, HD, 1), cosine, -sine)
    dv = dv_ref[...]
    dv = dv + pltpu.roll(dv, HD, 1)
    da_ref[:, wp + qwp :] = jnp.where(lower, dk, dv).astype(bf16)


def mixer_back_kernel(
    dims, pb_ref, dy_ref, y_ref, wzx_ref, wbc_ref, wsp_ref, da_ref, wq_ref, x_ref, seqc_ref, seqr_ref, masks_ref,
    convx_ref, convs_ref, bias_ref, rate_ref, skip_ref,
    dxb_ref, dact_ref, gn1_ref, gcx_ref, gcs_ref, gstep_ref, gskip_ref,
    neg_ref, gt_ref, dgt_ref, dsum_ref, ddir_ref,
):
    heads, qheads, wp, qwp, span = dims
    rows = x_ref.shape[0]
    masks = {k: masks_ref[:, k : k + 1] for k in (1, 2, 3)}
    linked_t = link_bias(seqc_ref[...], seqr_ref[...], True)
    neg_ref[...] = jnp.where(linked_t, 0.0, far)
    dt = step_parts(pb_ref[:, wp + 256 :], bias_ref[...])
    linked = link_bias(seqc_ref[...], seqr_ref[...], False)
    decay = mm_exact(jnp.where(linked, 1.0, 0.0), -dt * rate_ref[...])
    decay_t = decay.T
    state = pb_ref[:, wp : wp + 256]
    sterms = conv_terms(state, masks)
    sconv = sum(t * convs_ref[k : k + 1, :] for k, t in enumerate(sterms))
    ssig = jax.nn.sigmoid(sconv)
    bcc = (sconv * ssig).astype(bf16)
    bm, cm = bcc[:, :128], bcc[:, 128:]
    gt_ref[...] = mm_nt(bm, cm)
    dgt_ref[...] = jnp.zeros_like(dgt_ref)
    for p in range(wp // LANES):
        cols = slice(p * LANES, (p + 1) * LANES)
        width = HD * min(2, heads - 2 * p)
        terms = conv_terms(pb_ref[:, cols], masks)
        conv = sum(t * convx_ref[k : k + 1, cols] for k, t in enumerate(terms))
        csig = jax.nn.sigmoid(conv)
        xc = conv * csig
        dt_cols = spread_heads(dt, 2 * p, width)
        xdt = (xc * dt_cols).astype(bf16)
        skip = skip_ref[:, cols]
        scanned = y_ref[:, cols] - skip * xc
        dy = dy_ref[:, cols]
        gskip_ref[:, cols] = jnp.sum(dy * xc, axis=0, keepdims=True)
        dyb = dy.astype(bf16)
        blocks = []
        for a in range(rows // span):
            here = slice(a * span, (a + 1) * span)
            sides = []
            for side in range(width // HD):
                h = 2 * p + side
                dys = jnp.where(half_mask(rows - a * span, side), dyb[a * span :], jnp.zeros((), bf16))
                gap = decay_t[h : h + 1, a * span :] - decay[here, h : h + 1]
                falloff = jnp.exp(gap + neg_ref[here, a * span :])
                mixing = (gt_ref[here, a * span :] * falloff).astype(bf16)
                sides.append(mm(mixing, dyb[a * span :]))
                dgt_ref[here, a * span :] += mm_nt(xdt[here], dys) * falloff
            blocks.append(sides[0] if len(sides) == 1 else jnp.where(half_mask(span, 0), sides[0], sides[1]))
        dxdt = jnp.concatenate(blocks, axis=0)
        dsum_ref[:, cols] = dyb.astype(f32) * scanned - xdt.astype(f32) * dxdt
        ddir_ref[:, cols] = dxdt * xc
        dconv = (dxdt * dt_cols + skip * dy) * (csig * (1.0 + conv * (1.0 - csig)))
        gcx_ref[:, cols] = jnp.concatenate([jnp.sum(t * dconv, axis=0, keepdims=True) for t in terms], axis=0)
        dxb_ref[:, cols] = conv_back(dconv, masks, convx_ref[:, cols]).astype(bf16)

    dgt = dgt_ref[...].astype(bf16)
    dbcc = jnp.concatenate([mm(dgt, cm), mm_tn(dgt, bm)], axis=1)
    dsconv = dbcc * (ssig * (1.0 + sconv * (1.0 - ssig)))
    gcs_ref[...] = jnp.concatenate([jnp.sum(t * dsconv, axis=0, keepdims=True) for t in sterms], axis=0)
    dxb_ref[:, wp : wp + 256] = conv_back(dsconv, masks, convs_ref[...]).astype(bf16)

    head_of = lax.broadcasted_iota(jnp.int32, (wp, LANES), 0) // HD
    pick = jnp.where(head_of == lax.broadcasted_iota(jnp.int32, (wp, LANES), 1), 1.0, 0.0)
    ds = mm_exact(dsum_ref[...], pick)
    ddirect = mm_exact(ddir_ref[...], pick)
    dlog = mm_exact(jnp.where(linked_t, 1.0, 0.0), ds)
    rate = rate_ref[...]
    ddt = ddirect - rate * dlog
    dstep = ddt * jax.nn.sigmoid(pb_ref[:, wp + 256 :] + bias_ref[...])
    dstep = jnp.where(lane_ids(rows) < heads, dstep, 0.0)
    dxb_ref[:, wp + 256 :] = dstep.astype(bf16)
    gstep_ref[...] = jnp.concatenate(
        [jnp.sum(dstep, axis=0, keepdims=True), -rate * jnp.sum(dt * dlog, axis=0, keepdims=True)], axis=0
    )
    finish(dxb_ref)
    dact = mm_nt(da_ref[:, :wp], wzx_ref[:, :wp]) + mm_nt(dxb_ref[:, :wp], wzx_ref[:, wp:])
    dact = dact + mm_nt(dxb_ref[:, wp : wp + 256], wbc_ref[...]) + mm_nt(da_ref[:, wp : wp + qwp], wq_ref[...])
    dact = dact + mm_nt(dxb_ref[:, wp + 256 :], wsp_ref[:, :LANES]) + mm_nt(da_ref[:, wp + qwp :], wsp_ref[:, LANES:])
    dact_ref[...] = dact.astype(bf16)
    finish(dact_ref)
    x = x_ref[...].astype(f32)
    r1 = lax.rsqrt(jnp.mean(x * x, axis=-1, keepdims=True) + norm_eps)
    gn1_ref[...] = jnp.sum(dact * x * r1, axis=0, keepdims=True)


def grad_kernel(cuts, block, *refs):
    pairs = len(cuts)
    bit_ref, ins = refs[0], refs[1 : 1 + 2 * pairs]
    sent_ref, kept_ref, turned = refs[1 + 2 * pairs :]
    bit = bit_ref[0]
    at = 0
    for k, (low, high) in enumerate(cuts):
        left, right = ins[2 * k], ins[2 * k + 1]
        if k == 0 or left is not ins[2 * k - 2]:
            turned[...] = left[...].astype(f32).T.astype(bf16)
        count = turned.shape[0] // (2 * block)
        for side, out in enumerate((sent_ref, kept_ref)):
            which = 1 - bit if side == 0 else bit
            for i in range(count):
                start = pl.multiple_of((2 * i + which) * block, block)
                rows = turned[pl.ds(start, block), :]
                out[i * block : (i + 1) * block, at : at + high - low] = mm(rows, right[:, low:high]).astype(bf16)
        at += high - low


def weight_halves(pairs, bit, block, after=()):
    args = [bit] + [a for left, right, _, _ in pairs for a in (left, right)]
    cuts = [(low, high) for _, _, low, high in pairs]
    rows, model = pairs[0][0].shape
    half = (model // 2, sum(high - low for low, high in cuts))
    return call(
        functools.partial(grad_kernel, cuts, block), [(half, bf16), (half, bf16)], [((model, rows), bf16)], args, 1, after
    )


def step_kernel(block, which_ref, kept_ref, arrived_ref, away_ref, mine_ref):
    which = which_ref[0]
    for out, side in ((away_ref, 1 - which), (mine_ref, which)):
        for i in range(kept_ref.shape[0] // (2 * block)):
            start = pl.multiple_of((2 * i + side) * block, block)
            total = kept_ref[pl.ds(start, block), :].astype(f32) + arrived_ref[pl.ds(start, block), :].astype(f32)
            out[i * block : (i + 1) * block, :] = total.astype(bf16)


def add_kernel(a_ref, b_ref, out_ref):
    out_ref[...] = a_ref[...] + b_ref[...]


class Fetched:
    def __init__(self, source, held, sem):
        self.held, self.copy, self.ready = held, pltpu.make_async_copy(source, held, sem), False
        self.shape, self.dtype = held.shape, held.dtype
        self.copy.start()

    def __getitem__(self, key):
        if not self.ready:
            self.copy.wait()
            self.ready = True
        return self.held[key]


class Stored:
    def __init__(self, held, target, sem):
        self.held, self.copy, self.sent = held, pltpu.make_async_copy(held, target, sem), False
        self.shape, self.dtype = held.shape, held.dtype

    def __getitem__(self, key):
        return self.held[key]

    def __setitem__(self, key, value):
        self.held[key] = value

    def finish(self):
        if not self.sent:
            self.copy.start()
            self.sent = True


LARGE = 1 << 16


def finish(*refs):
    for ref in refs:
        if isinstance(ref, Stored):
            ref.finish()


def call(kernel, outs, scratch, args, scalars=0, after=()):
    count = len(args)
    large_in = [i >= scalars and a.size * a.dtype.itemsize >= LARGE for i, a in enumerate(args)]
    large_out = [s[0] * s[1] * jnp.dtype(t).itemsize >= LARGE for s, t in outs]
    buffers = [pltpu.VMEM(a.shape, a.dtype) for a, big in zip(args, large_in) if big]
    buffers += [pltpu.VMEM(s, t) for (s, t), big in zip(outs, large_out) if big]
    copies = len(buffers)

    def wrapped(*refs):
        ins, rest = list(refs[:count]), refs[count + len(after) :]
        results, rest = list(rest[: len(outs)]), rest[len(outs) :]
        held, sems, inner = rest[:copies], rest[copies], rest[copies + 1 :]
        slot = 0
        for i, big in enumerate(large_in):
            if big:
                ins[i] = Fetched(ins[i], held[slot], sems.at[slot])
                slot += 1
        for i, big in enumerate(large_out):
            if big:
                results[i] = Stored(held[slot], results[i], sems.at[slot])
                slot += 1
        kernel(*ins, *results, *inner)
        finish(*results)
        for ref in ins:
            if isinstance(ref, Fetched) and not ref.ready:
                ref.copy.wait()
        for ref in results:
            if isinstance(ref, Stored):
                ref.copy.wait()

    spaces = [pltpu.SMEM] * scalars + [pl.ANY if big else pltpu.VMEM for big in large_in[scalars:]] + [pl.ANY] * len(after)
    return pl.pallas_call(
        wrapped,
        out_shape=[jax.ShapeDtypeStruct(s, t) for s, t in outs],
        in_specs=[pl.BlockSpec(memory_space=space) for space in spaces],
        out_specs=[pl.BlockSpec(memory_space=pl.ANY if big else pltpu.VMEM) for big in large_out],
        scratch_shapes=buffers + [pltpu.SemaphoreType.DMA((max(copies, 1),))] + [pltpu.VMEM(s, t) for s, t in scratch],
        compiler_params=pltpu.CompilerParams(vmem_limit_bytes=52 * 1024 * 1024),
        cost_estimate=pl.CostEstimate(flops=1000, bytes_accessed=1000, transcendentals=0),
    )(*args, *after)


def swap(values):
    return lax.ppermute(values, "tensor", [(0, 1), (1, 0)])


def gather_rows(values, me, count):
    if count != 2:
        return lax.all_gather(values, "tensor", axis=0, tiled=True)
    other = swap(values)
    first = jnp.where(me == 0, values, other)
    return jnp.concatenate([first, jnp.where(me == 0, other, values)], axis=0)


def both_parts(part, count):
    if count != 2:
        return (lax.psum(part, "tensor"), jnp.zeros_like(part))
    return (part, swap(part))


def scatter_rows(part, me, count):
    if count != 2:
        return lax.psum_scatter(part, "tensor", scatter_dimension=0, tiled=True).astype(f32)
    halves = part.reshape(2, part.shape[0] // 2, part.shape[1])
    arrived = swap(lax.dynamic_index_in_dim(halves, 1 - me, 0, keepdims=False))
    return lax.dynamic_index_in_dim(halves, me, 0, keepdims=False).astype(f32) + arrived.astype(f32)


def partners(count, bit):
    return [(i, i ^ bit) for i in range(count)]


def exchange(sent, count, bit):
    return lax.ppermute(sent, "dp", partners(count, bit))


class Reduction:
    def __init__(self, sent, kept, index, count, block):
        self.index, self.count, self.block, self.bit = index, count, block, 1
        self.kept, self.sent = kept, sent
        self.arrived = exchange(sent, count, 1)

    def done(self):
        return self.bit * 2 >= self.count

    def step(self, after=()):
        if self.done():
            return after
        self.bit *= 2
        which = ((self.index // self.bit) % 2).astype(jnp.int32).reshape(1)
        half = (self.kept.shape[0] // 2, self.kept.shape[1])
        self.sent, self.kept = call(
            functools.partial(step_kernel, self.block), [(half, bf16), (half, bf16)], [],
            (which, self.kept, self.arrived), 1, after,
        )
        self.arrived = exchange(self.sent, self.count, self.bit)
        return (self.sent,)

    def total(self):
        return self.kept.astype(f32) + self.arrived.astype(f32)


def segments(lengths, row_count):
    seq_ends = jnp.cumsum(lengths)
    places = jnp.arange(row_count, dtype=jnp.int32)
    passed = places[:, None] >= seq_ends[None, :]
    seq_ids = jnp.sum(passed.astype(jnp.int32), axis=1)
    starts = jnp.max(jnp.where(passed, seq_ends[None, :], 0), axis=1)
    is_live = (places < seq_ends[-1]).astype(f32)
    return (seq_ids, places - starts, is_live)


def body(
    dp_count, tensor_count, tokens, cotangent, seq_lengths, norm1_gain, norm2_gain, mixer_in, state_in, step_in,
    conv_inner, conv_state, step_bias, decay_log, skip_gain, mixer_out, query_in, key_value, attend_out, gate_up,
    down_out,
):
    share, model = tokens.shape
    rows = share * tensor_count
    me = lax.axis_index("tensor")
    index = lax.axis_index("dp")
    inner = mixer_in.shape[2]
    heads = step_in.shape[1]
    query_width = query_in.shape[1]
    qheads = query_width // HD
    wp, qwp = padded(inner), padded(query_width)
    span = min(LANES, rows)
    dims = (heads, qheads, wp, qwp, span)

    if tensor_count == 2:
        x_own, x_other = tokens, swap(tokens)
    else:
        x_own = x_other = gather_rows(tokens, me, tensor_count)
    place = jnp.stack([me, lax.rem(me + 1, tensor_count)]).astype(jnp.int32)
    seq_ids, positions, is_live = segments(seq_lengths[0], rows)
    live_share = lax.dynamic_slice_in_dim(is_live, me * share, share, 0)[:, None]
    dout_rows = gather_rows(lax.optimization_barrier((cotangent, x_other))[0], me, tensor_count)
    dout_rows = dout_rows * is_live[:, None].astype(bf16)

    seq_col = seq_ids.astype(f32)[:, None]
    seq_row = seq_ids.astype(f32)[None, :]
    shifts = jnp.minimum(jnp.arange(LANES, dtype=jnp.int32), 4)[None, :]
    masks = (positions[:, None] >= shifts).astype(f32)
    lane = jnp.arange(LANES)
    frequency = rope_base ** (-2.0 * (lane % (HD // 2)).astype(f32) / HD)
    angles = positions.astype(f32)[:, None] * frequency[None, :]
    cosine = jnp.cos(angles)
    sine = jnp.sin(angles) * jnp.where(lane % HD < HD // 2, -1.0, 1.0)[None, :]

    key_index = me * qheads // (QH // KVH)
    pair_local = lax.dynamic_slice_in_dim(key_value, key_index * HD, HD, 2).reshape(model, 2 * HD)
    if inner == wp:
        wzx = mixer_in.reshape(model, 2 * inner)
    else:
        wzx = pad_to(mixer_in, wp).reshape(model, 2 * wp)
    wsp = jnp.concatenate([pad_to(step_in, LANES), pair_local], axis=1)
    wq, wmix, watt = pad_to(query_in, qwp), pad_to(mixer_out, wp), pad_to(attend_out, qwp)
    taps = pad_to(conv_inner, wp)
    bias = pad_to(step_bias[None], LANES)
    rate = pad_to(jnp.exp(decay_log)[None], LANES)
    skip = pad_to(jnp.repeat(skip_gain, HD)[None], wp)
    gain1, gain2 = norm1_gain[None], norm2_gain[None]

    x_rows, act, pa, pb, y, cat, part = call(
        functools.partial(front_kernel, dims),
        [
            ((rows, model), bf16), ((rows, model), bf16), ((rows, wp + qwp + LANES), f32), ((rows, wp + 384), f32),
            ((rows, wp), f32), ((rows, wp + qwp), bf16), ((rows, model), bf16),
        ],
        [((rows, rows), f32), ((rows, rows), f32), ((rows, LANES), bf16)],
        (
            place, x_own, x_other, state_in, wsp, wzx, wq, wmix, watt, gain1, seq_col, seq_row, masks, cosine, sine, taps,
            conv_state, bias, rate, skip,
        ),
        1,
    )
    own, other = both_parts(part, tensor_count)
    wgu = lax.optimization_barrier((gate_up, part))[0].reshape(model, -1)
    dhidden = mm(dout_rows, down_out)
    ff2 = wgu.shape[1]
    h1, n2, hidden, dgu, ffn_part, dn2_part = call(
        middle_kernel,
        [
            ((rows, model), f32), ((rows, model), bf16), ((rows, ff2 // 2), bf16), ((rows, ff2), bf16),
            ((rows, model), bf16), ((rows, model), bf16),
        ],
        [],
        (x_rows, own, other, gain2, wgu, down_out, dhidden),
    )
    dn2_own, dn2_other = both_parts(dn2_part, tensor_count)

    bit = (index % 2).astype(jnp.int32).reshape(1)
    block = model // dp_count
    cut = ff2 // 4

    def reduction(pairs, after=()):
        sent, kept = weight_halves(pairs, bit, block, after)
        return Reduction(sent, kept, index, dp_count, block)

    ffn_a = reduction([(dout_rows, hidden, 0, ff2 // 2), (n2, dgu, 0, cut)])
    order = ffn_a.step()

    dh1_share, ffn_send, dmix, dy, da, gn2 = call(
        functools.partial(attend_back_kernel, dims, share),
        [
            ((share, model), f32), ((share, model), bf16), ((rows, model), bf16), ((rows, wp), f32),
            ((rows, wp + qwp + LANES), bf16), ((1, model), f32),
        ],
        [((rows, rows), f32), ((rows, model), f32), ((rows, qwp), bf16), ((rows, LANES), f32), ((rows, LANES), f32)],
        (
            place, dn2_own, dn2_other, ffn_part, h1, dout_rows, gain2, wmix, watt, seq_col, seq_row, cosine, sine, pa, y,
        ),
        1, order,
    )
    order = ffn_a.step((dmix,))
    ffn_b = reduction([(n2, dgu, cut, ff2)], order)
    mix_a = reduction([(dmix, cat, 0, wp + qwp), (act, da, 0, wp + qwp + LANES)], (ffn_b.kept,))
    order = ffn_b.step((mix_a.kept,))
    order = mix_a.step(order)

    dxb, dact, gn1, gcx, gcs, gstep, gskip = call(
        functools.partial(mixer_back_kernel, dims),
        [
            ((rows, wp + 384), bf16), ((rows, model), bf16),
            ((1, model), f32), ((4, wp), f32), ((4, 256), f32), ((2, LANES), f32), ((1, wp), f32),
        ],
        [
            ((rows, rows), f32), ((rows, rows), f32), ((rows, rows), f32), ((rows, wp), f32), ((rows, wp), f32),
        ],
        (
            pb, dy, y, wzx, state_in, wsp, da, wq, x_rows, seq_col, seq_row, masks, taps, conv_state, bias, rate, skip,
        ),
        0, order,
    )
    shared = jnp.concatenate([gn1[0], gn2[0] * (1.0 / tensor_count), gcs.reshape(-1)]).reshape(-1, LANES)
    local = jnp.concatenate([gcx.reshape(-1), gskip.reshape(-1), gstep.reshape(-1)]).reshape(-1, LANES)
    shared_rows = shared.shape[0]
    minor = jnp.concatenate([shared, local], axis=0)

    def minor_step(values, bit, after):
        arrived = exchange(values, dp_count, bit)
        return call(add_kernel, [(values.shape, f32)], [], (values, arrived), 0, after)[0]

    order = ffn_a.step((dxb,))
    mix_b = reduction([(act, dxb, 0, wp + 384)], order)
    order = ffn_b.step((mix_b.kept,))
    minor_bit = 1
    for r in [mix_b, mix_a, ffn_b, mix_b, mix_a] + 4 * [ffn_a, ffn_b, mix_a, mix_b]:
        if r.done():
            continue
        if minor_bit < dp_count:
            minor = minor_step(minor, minor_bit, order)
            minor_bit *= 2
            order = (minor,)
        order = r.step(order)
    while minor_bit < dp_count:
        minor = minor_step(minor, minor_bit, order)
        minor_bit *= 2
    ffn_a, ffn_b, mix_a, mix_b = ffn_a.total(), ffn_b.total(), mix_a.total(), mix_b.total()
    down_total = ffn_a[:, : ff2 // 2]
    up_total = jnp.concatenate([ffn_a[:, ff2 // 2 :], ffn_b], axis=1)
    out_total, first_total = mix_a[:, : wp + qwp], mix_a[:, wp + qwp :]
    second_total, state_total = mix_b[:, :wp], mix_b[:, wp : wp + 256]
    step_total = mix_b[:, wp + 256 :]

    if tensor_count == 2:
        ffn_mine = lax.dynamic_slice_in_dim(ffn_part, me * share, share, 0).astype(f32)
        ffn_share = ffn_mine + swap(ffn_send).astype(f32)
    else:
        ffn_share = scatter_rows(ffn_part, me, tensor_count)
    h1_share = lax.dynamic_slice_in_dim(h1, me * share, share, 0)
    block_out = ((h1_share + ffn_share) * live_share).astype(bf16)

    dact_share = scatter_rows(dact, me, tensor_count)
    x_share = tokens.astype(f32)
    r1 = lax.rsqrt(jnp.mean(x_share * x_share, axis=-1, keepdims=True) + norm_eps)
    u = dact_share * gain1
    token_grad = dh1_share + r1 * u - x_share * (r1 * r1 * r1 * jnp.mean(u * x_share, axis=-1, keepdims=True))

    shared = lax.psum(minor[:shared_rows], "tensor") if tensor_count != 2 else minor[:shared_rows] + swap(minor[:shared_rows])
    shared = shared.reshape(-1)
    local = minor[shared_rows:].reshape(-1)
    g_norm1, g_norm2, g_conv_state = shared[:model], shared[model : 2 * model], shared[2 * model :].reshape(4, 256)
    g_conv_inner = local[: 4 * wp].reshape(4, wp)[:, :inner]
    g_skip = jnp.sum(local[4 * wp : 5 * wp].reshape(-1, HD), axis=1)[:heads]
    g_bias = local[5 * wp : 5 * wp + heads]
    g_decay = local[5 * wp + LANES : 5 * wp + LANES + heads]

    both = jnp.concatenate([state_total, first_total[:, wp + qwp :]], axis=1).astype(bf16)
    placed = lambda pair: lax.dynamic_update_slice_in_dim(
        jnp.zeros((block,) + key_value.shape[1:], f32), pair.astype(f32).reshape(block, 2, HD), key_index * HD, 2
    )
    if tensor_count == 2:
        arrived = swap(both)
        g_state = both[:, :256].astype(f32) + arrived[:, :256].astype(f32)
        mine = both[:, 256:].reshape(block, 2, HD)
        theirs = arrived[:, 256:].reshape(block, 2, HD)
        g_pair = jnp.concatenate(
            [jnp.where(me == 0, mine, theirs), jnp.where(me == 0, theirs, mine)], axis=2
        ).astype(f32)
    else:
        g_state = lax.psum(both[:, :256], "tensor").astype(f32)
        g_pair = lax.psum(placed(both[:, 256:]).astype(bf16), "tensor").astype(f32)

    g_mixer_in = jnp.stack([first_total[:, :inner], second_total[:, :inner]], axis=1)
    return (
        block_out,
        token_grad.astype(bf16),
        g_norm1,
        g_norm2,
        g_mixer_in,
        g_state,
        step_total[:, :heads],
        g_conv_inner,
        g_conv_state,
        g_bias,
        g_decay,
        g_skip,
        out_total[:, :inner],
        first_total[:, wp : wp + query_width],
        g_pair,
        out_total[:, wp : wp + query_width],
        up_total.reshape(block, 2, ff2 // 2),
        down_total,
    )


def solution(mesh):
    return jax.shard_map(
        functools.partial(body, mesh.shape["dp"], mesh.shape["tensor"]),
        mesh=mesh,
        in_specs=(
            P(("dp", "tensor"), None),
            P(("dp", "tensor"), None),
            P("dp", None),
            P(),
            P(),
            P(None, None, "tensor"),
            P(),
            P(None, "tensor"),
            P(None, "tensor"),
            P(),
            P("tensor"),
            P("tensor"),
            P("tensor"),
            P(None, "tensor"),
            P(None, "tensor"),
            P(),
            P(None, "tensor"),
            P(None, None, "tensor"),
            P(None, "tensor"),
        ),
        out_specs=(
            P(("dp", "tensor"), None),
            P(("dp", "tensor"), None),
            P(),
            P(),
            P("dp", None, "tensor"),
            P("dp", None),
            P("dp", "tensor"),
            P(None, "tensor"),
            P(),
            P("tensor"),
            P("tensor"),
            P("tensor"),
            P("dp", "tensor"),
            P("dp", "tensor"),
            P("dp", None, None),
            P("dp", "tensor"),
            P("dp", None, "tensor"),
            P("dp", "tensor"),
        ),
        check_vma=False,
    )
```

```python
import functools

import jax
import jax.numpy as jnp
from jax import lax
from jax.experimental import pallas as pl
from jax.experimental.pallas import tpu as pltpu
from jax.sharding import PartitionSpec as P

HD = 64
QH = 8
KVH = 2
LANES = 128

rope_base = 100000000000.0
norm_eps = 1e-05
far = -1e30
highest = lax.Precision.HIGHEST
f32 = jnp.float32
bf16 = jnp.bfloat16


def padded(width):
    return -(-width // LANES) * LANES


def pad_to(values, width):
    return jnp.pad(values, [(0, 0)] * (values.ndim - 1) + [(0, width - values.shape[-1])])


def mm(left, right):
    return jnp.dot(left, right, preferred_element_type=f32)


def mm_nt(left, right):
    return lax.dot_general(left, right, (((1,), (1,)), ((), ())), preferred_element_type=f32)


def mm_tn(left, right):
    return lax.dot_general(left, right, (((0,), (0,)), ((), ())), preferred_element_type=f32)


def mm_exact(left, right):
    return jnp.dot(left, right, preferred_element_type=f32, precision=highest)


def lane_ids(rows):
    return lax.broadcasted_iota(jnp.int32, (rows, LANES), 1)


def partner_half(values):
    lane = lane_ids(values.shape[0])
    return jnp.where(lane % HD < HD // 2, pltpu.roll(values, LANES - HD // 2, 1), pltpu.roll(values, HD // 2, 1))


def rotated(values, cosine, signed_sine):
    return values * cosine + partner_half(values) * signed_sine


def conv_terms(values, masks):
    return [pltpu.roll(values, offset, 0) * masks[offset] for offset in (3, 2, 1)] + [values]


def conv_back(grad, masks, taps):
    rows = grad.shape[0]
    total = grad * taps[3:4]
    for offset in (1, 2, 3):
        total = total + pltpu.roll(grad * masks[offset], rows - offset, 0) * taps[3 - offset : 4 - offset]
    return total


def link_bias(seq_col, seq_row, transposed):
    rows = seq_col.shape[0]
    down = lax.broadcasted_iota(jnp.int32, (rows, rows), 0)
    across = lax.broadcasted_iota(jnp.int32, (rows, rows), 1)
    ordered = down <= across if transposed else down >= across
    return (seq_col == seq_row) & ordered


def step_parts(raw, bias):
    shifted = raw + bias
    return jnp.maximum(shifted, 0.0) + jnp.log1p(jnp.exp(-jnp.abs(shifted)))


def spread_heads(columns, first, width):
    rows = columns.shape[0]
    low = jnp.broadcast_to(columns[:, first : first + 1], (rows, LANES))
    if width <= HD:
        return low
    high = jnp.broadcast_to(columns[:, first + 1 : first + 2], (rows, LANES))
    return jnp.where(lane_ids(rows) < HD, low, high)


def half_mask(rows, side):
    lane = lane_ids(rows)
    return lane < HD if side == 0 else lane >= HD


def front_kernel(
    dims, place_ref, own_ref, other_ref, wbc_ref, wsp_ref, wzx_ref, wq_ref, wmix_ref, watt_ref, gain_ref, seqc_ref,
    seqr_ref, masks_ref, cos_ref, sin_ref, convx_ref, convs_ref, bias_ref, rate_ref, skip_ref,
    x_ref, act_ref, pa_ref, pb_ref, y_ref, cat_ref, part_ref, neg_ref, g_ref, xdt_ref,
):
    heads, qheads, wp, qwp, span = dims
    rows = x_ref.shape[0]
    share = own_ref.shape[0]
    if share == rows:
        x_ref[...] = own_ref[...]
    else:
        x_ref[pl.ds(pl.multiple_of(place_ref[0] * share, 16), share), :] = own_ref[...]
        x_ref[pl.ds(pl.multiple_of(place_ref[1] * share, 16), share), :] = other_ref[...]
    finish(x_ref)
    x = x_ref[...].astype(f32)
    act = (x * lax.rsqrt(jnp.mean(x * x, axis=-1, keepdims=True) + norm_eps) * gain_ref[...]).astype(bf16)
    act_ref[...] = act
    finish(act_ref)
    pb_ref[:, wp : wp + 256] = mm(act, wbc_ref[...])
    pb_ref[:, wp + 256 :] = mm(act, wsp_ref[:, :LANES])
    pb_ref[:, :wp] = mm(act, wzx_ref[:, wp:])
    pa_ref[:, wp : wp + qwp] = mm(act, wq_ref[...])
    pa_ref[:, wp + qwp :] = mm(act, wsp_ref[:, LANES:])
    pa_ref[:, :wp] = mm(act, wzx_ref[:, :wp])
    finish(pa_ref, pb_ref)
    masks = {k: masks_ref[:, k : k + 1] for k in (1, 2, 3)}
    linked = link_bias(seqc_ref[...], seqr_ref[...], False)
    neg_ref[...] = jnp.where(linked, 0.0, far)
    dt = step_parts(pb_ref[:, wp + 256 :], bias_ref[...])
    decay = mm_exact(jnp.where(linked, 1.0, 0.0), -dt * rate_ref[...])
    decay_t = decay.T
    terms = conv_terms(pb_ref[:, wp : wp + 256], masks)
    bcc = sum(t * convs_ref[k : k + 1, :] for k, t in enumerate(terms))
    bcc = (bcc * jax.nn.sigmoid(bcc)).astype(bf16)
    g_ref[...] = mm_nt(bcc[:, 128:], bcc[:, :128])

    for p in range(wp // LANES):
        cols = slice(p * LANES, (p + 1) * LANES)
        width = HD * min(2, heads - 2 * p)
        conv = sum(t * convx_ref[k : k + 1, cols] for k, t in enumerate(conv_terms(pb_ref[:, cols], masks)))
        xc = conv * jax.nn.sigmoid(conv)
        xdt_ref[...] = (xc * spread_heads(dt, 2 * p, width)).astype(bf16)
        blocks = []
        for a in range(rows // span):
            here = slice(a * span, (a + 1) * span)
            reach = (a + 1) * span
            sides = []
            for h in range(2 * p, 2 * p + width // HD):
                gap = decay[here, h : h + 1] - decay_t[h : h + 1, :reach]
                mixing = g_ref[here, :reach] * jnp.exp(gap + neg_ref[here, :reach])
                sides.append(mm(mixing.astype(bf16), xdt_ref[:reach, :]))
            blocks.append(sides[0] if len(sides) == 1 else jnp.where(half_mask(span, 0), sides[0], sides[1]))
        y = jnp.concatenate(blocks, axis=0) + skip_ref[:, cols] * xc
        y_ref[:, cols] = y
        z = pa_ref[:, cols]
        cat_ref[:, cols] = (y * (z * jax.nn.sigmoid(z))).astype(bf16)

    finish(y_ref)
    cosine, sine = cos_ref[...], sin_ref[...]
    pair = pa_ref[:, wp + qwp :]
    swapped = pltpu.roll(pair, HD, 1)
    lower = half_mask(rows, 0)
    keys = rotated(jnp.where(lower, pair, swapped), cosine, sine).astype(bf16)
    values = jnp.where(lower, swapped, pair).astype(bf16)
    for p in range(qwp // LANES):
        cols = slice(wp + p * LANES, wp + (p + 1) * LANES)
        queries = rotated(pa_ref[:, cols], cosine, sine).astype(bf16)
        for a in range(rows // span):
            here = slice(a * span, (a + 1) * span)
            reach = (a + 1) * span
            sides = []
            for side in range(min(2, qheads - 2 * p)):
                q = jnp.where(half_mask(span, side), queries[here], jnp.zeros((), bf16))
                scores = mm_nt(q, keys[:reach]) * (HD**-0.5) + neg_ref[here, :reach]
                weights = jnp.exp(scores - jnp.max(scores, axis=-1, keepdims=True))
                probs = weights / jnp.sum(weights, axis=-1, keepdims=True)
                sides.append(mm(probs.astype(bf16), values[:reach]))
            if len(sides) == 1:
                out = jnp.where(half_mask(span, 0), sides[0], 0.0)
            else:
                out = jnp.where(half_mask(span, 0), sides[0], sides[1])
            cat_ref[here, cols] = out.astype(bf16)
    finish(cat_ref)
    part_ref[...] = (mm_nt(cat_ref[:, :wp], wmix_ref[...]) + mm_nt(cat_ref[:, wp:], watt_ref[...])).astype(bf16)


def middle_kernel(
    x_ref, own_ref, other_ref, gain_ref, wgu_ref, down_ref, dhid_ref,
    h1_ref, n2_ref, hidden_ref, dgu_ref, out_ref, dn2_ref,
):
    width = down_ref.shape[1]
    h1 = x_ref[...].astype(f32) + (own_ref[...].astype(f32) + other_ref[...].astype(f32))
    h1_ref[...] = h1
    finish(h1_ref)
    n2 = (h1 * lax.rsqrt(jnp.mean(h1 * h1, axis=-1, keepdims=True) + norm_eps) * gain_ref[...]).astype(bf16)
    n2_ref[...] = n2
    finish(n2_ref)
    gate = mm(n2, wgu_ref[:, :width])
    up = mm(n2, wgu_ref[:, width:])
    sig = jax.nn.sigmoid(gate)
    silu = gate * sig
    hidden = (silu * up).astype(bf16)
    hidden_ref[...] = hidden
    finish(hidden_ref)
    dhid = dhid_ref[...].astype(f32)
    dgu_ref[:, :width] = (dhid * up * (sig * (1.0 + gate * (1.0 - sig)))).astype(bf16)
    dgu_ref[:, width:] = (dhid * silu).astype(bf16)
    finish(dgu_ref)
    dn2_ref[...] = mm_nt(dgu_ref[...], wgu_ref[...]).astype(bf16)
    finish(dn2_ref)
    out_ref[...] = mm_nt(hidden, down_ref[...]).astype(bf16)


def attend_back_kernel(
    dims, share, place_ref, own_ref, other_ref, ffn_ref, h1_ref, dout_ref, gain2_ref, wmix_ref, watt_ref, seqc_ref,
    seqr_ref, cos_ref, sin_ref, pa_ref, y_ref,
    dh1_ref, ffn_send_ref, dmix_ref, dy_ref, da_ref, gn2_ref,
    neg_ref, dh1_all_ref, datt_ref, dk_ref, dv_ref,
):
    heads, qheads, wp, qwp, span = dims
    rows = own_ref.shape[0]
    dn2 = own_ref[...].astype(f32) + other_ref[...].astype(f32)
    h1 = h1_ref[...]
    r2 = lax.rsqrt(jnp.mean(h1 * h1, axis=-1, keepdims=True) + norm_eps)
    u = dn2 * gain2_ref[...]
    dh1 = dout_ref[...].astype(f32) + r2 * u - h1 * (r2 * r2 * r2 * jnp.mean(u * h1, axis=-1, keepdims=True))
    gn2_ref[...] = jnp.sum(dn2 * h1 * r2, axis=0, keepdims=True)
    dh1_all_ref[...] = dh1
    dh1_ref[...] = dh1_all_ref[pl.ds(pl.multiple_of(place_ref[0] * share, 16), share), :]
    ffn_send_ref[...] = ffn_ref[pl.ds(pl.multiple_of(place_ref[1] * share, 16), share), :]
    dmix = dh1.astype(bf16)
    dmix_ref[...] = dmix
    finish(dh1_ref, ffn_send_ref, dmix_ref)
    datt_ref[...] = mm(dmix, watt_ref[...]).astype(bf16)
    for p in range(wp // LANES):
        cols = slice(p * LANES, (p + 1) * LANES)
        dgated = mm(dmix, wmix_ref[:, cols])
        z = pa_ref[:, cols]
        sig = jax.nn.sigmoid(z)
        dy_ref[:, cols] = dgated * (z * sig)
        da_ref[:, cols] = (dgated * y_ref[:, cols] * (sig * (1.0 + z * (1.0 - sig)))).astype(bf16)
    finish(dy_ref)

    linked_t = link_bias(seqc_ref[...], seqr_ref[...], True)
    neg_ref[...] = jnp.where(linked_t, 0.0, far)
    lower = half_mask(rows, 0)
    cosine, sine = cos_ref[...], sin_ref[...]
    pair = pa_ref[:, wp + qwp :]
    swapped = pltpu.roll(pair, HD, 1)
    keys = rotated(jnp.where(lower, pair, swapped), cosine, sine).astype(bf16)
    values = jnp.where(lower, swapped, pair).astype(bf16)
    dk_ref[...] = jnp.zeros_like(dk_ref)
    dv_ref[...] = jnp.zeros_like(dv_ref)
    for p in range(qwp // LANES):
        cols = slice(wp + p * LANES, wp + (p + 1) * LANES)
        queries = rotated(pa_ref[:, cols], cosine, sine).astype(bf16)
        datt = datt_ref[:, p * LANES : (p + 1) * LANES]
        blocks = []
        for a in range(rows // span):
            here = slice(a * span, (a + 1) * span)
            reach = (a + 1) * span
            sides = []
            for side in range(min(2, qheads - 2 * p)):
                half = half_mask(span, side)
                q = jnp.where(half, queries[here], jnp.zeros((), bf16))
                do = jnp.where(half, datt[here], jnp.zeros((), bf16))
                scores = mm_nt(keys[:reach], q) * (HD**-0.5) + neg_ref[:reach, here]
                weights = jnp.exp(scores - jnp.max(scores, axis=0, keepdims=True))
                probs = weights / jnp.sum(weights, axis=0, keepdims=True)
                dp = mm_nt(values[:reach], do)
                ds = (probs * (dp - jnp.sum(probs * dp, axis=0, keepdims=True))).astype(bf16)
                dk_ref[:reach, :] += mm(ds, q)
                dv_ref[:reach, :] += mm(probs.astype(bf16), do)
                sides.append(mm_tn(ds, keys[:reach]))
            if len(sides) == 1:
                blocks.append(jnp.where(half_mask(span, 0), sides[0], 0.0))
            else:
                blocks.append(jnp.where(half_mask(span, 0), sides[0], sides[1]))
        dq = jnp.concatenate(blocks, axis=0) * (HD**-0.5)
        da_ref[:, cols] = rotated(dq, cosine, -sine).astype(bf16)
    dk = dk_ref[...] * (HD**-0.5)
    dk = rotated(dk + pltpu.roll(dk, HD, 1), cosine, -sine)
    dv = dv_ref[...]
    dv = dv + pltpu.roll(dv, HD, 1)
    da_ref[:, wp + qwp :] = jnp.where(lower, dk, dv).astype(bf16)


def mixer_back_kernel(
    dims, pb_ref, dy_ref, y_ref, wzx_ref, wbc_ref, wsp_ref, da_ref, wq_ref, x_ref, seqc_ref, seqr_ref, masks_ref,
    convx_ref, convs_ref, bias_ref, rate_ref, skip_ref,
    dxb_ref, dact_ref, gn1_ref, gcx_ref, gcs_ref, gstep_ref, gskip_ref,
    neg_ref, gt_ref, dgt_ref, dsum_ref, ddir_ref,
):
    heads, qheads, wp, qwp, span = dims
    rows = x_ref.shape[0]
    masks = {k: masks_ref[:, k : k + 1] for k in (1, 2, 3)}
    linked_t = link_bias(seqc_ref[...], seqr_ref[...], True)
    neg_ref[...] = jnp.where(linked_t, 0.0, far)
    dt = step_parts(pb_ref[:, wp + 256 :], bias_ref[...])
    linked = link_bias(seqc_ref[...], seqr_ref[...], False)
    decay = mm_exact(jnp.where(linked, 1.0, 0.0), -dt * rate_ref[...])
    decay_t = decay.T
    state = pb_ref[:, wp : wp + 256]
    sterms = conv_terms(state, masks)
    sconv = sum(t * convs_ref[k : k + 1, :] for k, t in enumerate(sterms))
    ssig = jax.nn.sigmoid(sconv)
    bcc = (sconv * ssig).astype(bf16)
    bm, cm = bcc[:, :128], bcc[:, 128:]
    gt_ref[...] = mm_nt(bm, cm)
    dgt_ref[...] = jnp.zeros_like(dgt_ref)
    for p in range(wp // LANES):
        cols = slice(p * LANES, (p + 1) * LANES)
        width = HD * min(2, heads - 2 * p)
        terms = conv_terms(pb_ref[:, cols], masks)
        conv = sum(t * convx_ref[k : k + 1, cols] for k, t in enumerate(terms))
        csig = jax.nn.sigmoid(conv)
        xc = conv * csig
        dt_cols = spread_heads(dt, 2 * p, width)
        xdt = (xc * dt_cols).astype(bf16)
        skip = skip_ref[:, cols]
        scanned = y_ref[:, cols] - skip * xc
        dy = dy_ref[:, cols]
        gskip_ref[:, cols] = jnp.sum(dy * xc, axis=0, keepdims=True)
        dyb = dy.astype(bf16)
        blocks = []
        for a in range(rows // span):
            here = slice(a * span, (a + 1) * span)
            sides = []
            for side in range(width // HD):
                h = 2 * p + side
                dys = jnp.where(half_mask(rows - a * span, side), dyb[a * span :], jnp.zeros((), bf16))
                gap = decay_t[h : h + 1, a * span :] - decay[here, h : h + 1]
                falloff = jnp.exp(gap + neg_ref[here, a * span :])
                mixing = (gt_ref[here, a * span :] * falloff).astype(bf16)
                sides.append(mm(mixing, dyb[a * span :]))
                dgt_ref[here, a * span :] += mm_nt(xdt[here], dys) * falloff
            blocks.append(sides[0] if len(sides) == 1 else jnp.where(half_mask(span, 0), sides[0], sides[1]))
        dxdt = jnp.concatenate(blocks, axis=0)
        dsum_ref[:, cols] = dyb.astype(f32) * scanned - xdt.astype(f32) * dxdt
        ddir_ref[:, cols] = dxdt * xc
        dconv = (dxdt * dt_cols + skip * dy) * (csig * (1.0 + conv * (1.0 - csig)))
        gcx_ref[:, cols] = jnp.concatenate([jnp.sum(t * dconv, axis=0, keepdims=True) for t in terms], axis=0)
        dxb_ref[:, cols] = conv_back(dconv, masks, convx_ref[:, cols]).astype(bf16)

    dgt = dgt_ref[...].astype(bf16)
    dbcc = jnp.concatenate([mm(dgt, cm), mm_tn(dgt, bm)], axis=1)
    dsconv = dbcc * (ssig * (1.0 + sconv * (1.0 - ssig)))
    gcs_ref[...] = jnp.concatenate([jnp.sum(t * dsconv, axis=0, keepdims=True) for t in sterms], axis=0)
    dxb_ref[:, wp : wp + 256] = conv_back(dsconv, masks, convs_ref[...]).astype(bf16)

    head_of = lax.broadcasted_iota(jnp.int32, (wp, LANES), 0) // HD
    pick = jnp.where(head_of == lax.broadcasted_iota(jnp.int32, (wp, LANES), 1), 1.0, 0.0)
    ds = mm_exact(dsum_ref[...], pick)
    ddirect = mm_exact(ddir_ref[...], pick)
    dlog = mm_exact(jnp.where(linked_t, 1.0, 0.0), ds)
    rate = rate_ref[...]
    ddt = ddirect - rate * dlog
    dstep = ddt * jax.nn.sigmoid(pb_ref[:, wp + 256 :] + bias_ref[...])
    dstep = jnp.where(lane_ids(rows) < heads, dstep, 0.0)
    dxb_ref[:, wp + 256 :] = dstep.astype(bf16)
    gstep_ref[...] = jnp.concatenate(
        [jnp.sum(dstep, axis=0, keepdims=True), -rate * jnp.sum(dt * dlog, axis=0, keepdims=True)], axis=0
    )
    finish(dxb_ref)
    dact = mm_nt(da_ref[:, :wp], wzx_ref[:, :wp]) + mm_nt(dxb_ref[:, :wp], wzx_ref[:, wp:])
    dact = dact + mm_nt(dxb_ref[:, wp : wp + 256], wbc_ref[...]) + mm_nt(da_ref[:, wp : wp + qwp], wq_ref[...])
    dact = dact + mm_nt(dxb_ref[:, wp + 256 :], wsp_ref[:, :LANES]) + mm_nt(da_ref[:, wp + qwp :], wsp_ref[:, LANES:])
    dact_ref[...] = dact.astype(bf16)
    finish(dact_ref)
    x = x_ref[...].astype(f32)
    r1 = lax.rsqrt(jnp.mean(x * x, axis=-1, keepdims=True) + norm_eps)
    gn1_ref[...] = jnp.sum(dact * x * r1, axis=0, keepdims=True)


def pieces_of(width, most):
    groups = width // LANES
    count = -(-groups // (most // LANES))
    edges = [(i * groups // count) * LANES for i in range(count + 1)]
    return list(zip(edges[:-1], edges[1:]))


def grad_kernel(cuts, pieces, block, bit_ref, *refs):
    pairs = len(cuts)
    ins, refs = refs[: 2 * pairs], refs[2 * pairs :]
    sents, kept, refs = refs[: len(pieces)], refs[len(pieces)], refs[len(pieces) + 1 :]
    buffers, refs = refs[: 2 * pairs], refs[2 * pairs :]
    turned, stage, in_sems, sent_sems, kept_sems = refs
    fetched = [Fetched(ins[i], buffers[i], in_sems.at[i]) for i in range(2 * pairs)]
    bit = bit_ref[0]
    count = turned.shape[0] // (2 * block)
    copies, at, sent_to = [], 0, 0
    for k, (low, high) in enumerate(cuts):
        turned[...] = fetched[2 * k][...].astype(f32).T.astype(bf16)
        for start in range(low, high, 512):
            stop = min(start + 512, high)
            full = mm(turned[...], fetched[2 * k + 1][:, start:stop]).astype(bf16)
            for j in range(2 * count):
                side = 1 - bit if j % 2 == 0 else bit
                stage[side, (j // 2) * block : (j // 2 + 1) * block, at : at + stop - start] = full[j * block : (j + 1) * block]
            at += stop - start
            while sent_to < len(pieces) and pieces[sent_to][1] <= at:
                cols = pl.ds(pieces[sent_to][0], pieces[sent_to][1] - pieces[sent_to][0])
                copies.append(pltpu.make_async_copy(stage.at[0, :, cols], sents[sent_to], sent_sems.at[sent_to]))
                copies.append(pltpu.make_async_copy(stage.at[1, :, cols], kept.at[:, cols], kept_sems.at[sent_to]))
                copies[-2].start()
                copies[-1].start()
                sent_to += 1
    for copy in copies:
        copy.wait()


def plain_params(flops=1000):
    return dict(
        compiler_params=pltpu.CompilerParams(vmem_limit_bytes=52 * 1024 * 1024),
        cost_estimate=pl.CostEstimate(flops=flops, bytes_accessed=1000, transcendentals=0),
    )


def weight_halves(pairs, bit, block, most, after=()):
    args = [a for left, right, _, _ in pairs for a in (left, right)]
    cuts = [(low, high) for _, _, low, high in pairs]
    rows, model = pairs[0][0].shape
    width = sum(high - low for low, high in cuts)
    pieces = pieces_of(width, most)
    outs = [(model // 2, high - low) for low, high in pieces] + [(model // 2, width)]

    def wrapped(bit_ref, *refs):
        grad_kernel(cuts, pieces, block, bit_ref, *refs[: len(args)], *refs[len(args) + len(after) :])

    *sent, kept = pl.pallas_call(
        wrapped,
        out_shape=[jax.ShapeDtypeStruct(s, bf16) for s in outs],
        in_specs=[pl.BlockSpec(memory_space=pltpu.SMEM)] + [pl.BlockSpec(memory_space=pl.ANY)] * (len(args) + len(after)),
        out_specs=[pl.BlockSpec(memory_space=pl.ANY)] * len(outs),
        scratch_shapes=[pltpu.VMEM(a.shape, a.dtype) for a in args]
        + [
            pltpu.VMEM((model, rows), bf16), pltpu.VMEM((2, model // 2, width), bf16),
            pltpu.SemaphoreType.DMA((len(args),)), pltpu.SemaphoreType.DMA((len(pieces),)),
            pltpu.SemaphoreType.DMA((len(pieces),)),
        ],
        **plain_params(),
    )(bit, *args, *after)
    return sent, kept


def step_kernel(pieces, whole, block, which_ref, kept, *refs):
    count = 1 if whole else len(pieces)
    arrived, refs = refs[:count], refs[count:]
    away, mine, kept_buf, arrived_buf, away_buf, mine_buf, kept_sems, arrived_sems, away_sems, mine_sems = refs
    which = which_ref[0]
    ins, outs = [], []
    for k, (low, high) in enumerate(pieces):
        cols = pl.ds(low, high - low)
        source = arrived[0].at[:, cols] if whole else arrived[k]
        ins.append(pltpu.make_async_copy(kept.at[:, cols], kept_buf.at[:, cols], kept_sems.at[k]))
        ins.append(pltpu.make_async_copy(source, arrived_buf.at[:, cols], arrived_sems.at[k]))
        ins[-2].start()
        ins[-1].start()
    for k, (low, high) in enumerate(pieces):
        ins[2 * k].wait()
        ins[2 * k + 1].wait()
        cols = pl.ds(low, high - low)
        for out, target, sems, side in ((away_buf, away, away_sems, 1 - which), (mine_buf, mine, mine_sems, which)):
            for i in range(kept.shape[0] // (2 * block)):
                rows = pl.ds(pl.multiple_of((2 * i + side) * block, block), block)
                total = kept_buf[rows, low:high].astype(f32) + arrived_buf[rows, low:high].astype(f32)
                out[i * block : (i + 1) * block, low:high] = total.astype(bf16)
            outs.append(pltpu.make_async_copy(out.at[:, cols], target.at[:, cols], sems.at[k]))
            outs[-1].start()
    for copy in outs:
        copy.wait()


def step_call(which, kept, arrived, block, after):
    rows, width = kept.shape
    whole = len(arrived) == 1
    if whole:
        pieces = pieces_of(width, 512)
    else:
        edges = [0]
        for a in arrived:
            edges.append(edges[-1] + a.shape[1])
        pieces = list(zip(edges[:-1], edges[1:]))
    used = 1 + len(arrived)

    def wrapped(which_ref, *refs):
        step_kernel(pieces, whole, block, which_ref, *refs[:used], *refs[used + len(after) :])

    half = (rows // 2, width)
    return pl.pallas_call(
        wrapped,
        out_shape=[jax.ShapeDtypeStruct(half, bf16)] * 2,
        in_specs=[pl.BlockSpec(memory_space=pltpu.SMEM)] + [pl.BlockSpec(memory_space=pl.ANY)] * (used + len(after)),
        out_specs=[pl.BlockSpec(memory_space=pl.ANY)] * 2,
        scratch_shapes=[pltpu.VMEM((rows, width), bf16)] * 2
        + [pltpu.VMEM(half, bf16)] * 2
        + [pltpu.SemaphoreType.DMA((len(pieces),))] * 4,
        **plain_params(),
    )(which, kept, *arrived, *after)


def add_kernel(a_ref, b_ref, out_ref):
    out_ref[...] = a_ref[...] + b_ref[...]


class Fetched:
    def __init__(self, source, held, sem):
        self.held, self.copy, self.ready = held, pltpu.make_async_copy(source, held, sem), False
        self.shape, self.dtype = held.shape, held.dtype
        self.copy.start()

    def __getitem__(self, key):
        if not self.ready:
            self.copy.wait()
            self.ready = True
        return self.held[key]


class Stored:
    def __init__(self, held, target, sem):
        self.held, self.copy, self.sent = held, pltpu.make_async_copy(held, target, sem), False
        self.shape, self.dtype = held.shape, held.dtype

    def __getitem__(self, key):
        return self.held[key]

    def __setitem__(self, key, value):
        self.held[key] = value

    def finish(self):
        if not self.sent:
            self.copy.start()
            self.sent = True


LARGE = 1 << 16
COST_US = 1100000000


def finish(*refs):
    for ref in refs:
        if isinstance(ref, Stored):
            ref.finish()


def call(kernel, outs, scratch, args, scalars=0, after=(), flops=1000):
    count = len(args)
    large_in = [i >= scalars and a.size * a.dtype.itemsize >= LARGE for i, a in enumerate(args)]
    large_out = [s[0] * s[1] * jnp.dtype(t).itemsize >= LARGE for s, t in outs]
    buffers = [pltpu.VMEM(a.shape, a.dtype) for a, big in zip(args, large_in) if big]
    buffers += [pltpu.VMEM(s, t) for (s, t), big in zip(outs, large_out) if big]
    copies = len(buffers)

    def wrapped(*refs):
        ins, rest = list(refs[:count]), refs[count + len(after) :]
        results, rest = list(rest[: len(outs)]), rest[len(outs) :]
        held, sems, inner = rest[:copies], rest[copies], rest[copies + 1 :]
        slot = 0
        for i, big in enumerate(large_in):
            if big:
                ins[i] = Fetched(ins[i], held[slot], sems.at[slot])
                slot += 1
        for i, big in enumerate(large_out):
            if big:
                results[i] = Stored(held[slot], results[i], sems.at[slot])
                slot += 1
        kernel(*ins, *results, *inner)
        finish(*results)
        for ref in ins:
            if isinstance(ref, Fetched) and not ref.ready:
                ref.copy.wait()
        for ref in results:
            if isinstance(ref, Stored):
                ref.copy.wait()

    spaces = [pltpu.SMEM] * scalars + [pl.ANY if big else pltpu.VMEM for big in large_in[scalars:]] + [pl.ANY] * len(after)
    return pl.pallas_call(
        wrapped,
        out_shape=[jax.ShapeDtypeStruct(s, t) for s, t in outs],
        in_specs=[pl.BlockSpec(memory_space=space) for space in spaces],
        out_specs=[pl.BlockSpec(memory_space=pl.ANY if big else pltpu.VMEM) for big in large_out],
        scratch_shapes=buffers + [pltpu.SemaphoreType.DMA((max(copies, 1),))] + [pltpu.VMEM(s, t) for s, t in scratch],
        **plain_params(flops),
    )(*args, *after)


def swap(values):
    return lax.ppermute(values, "tensor", [(0, 1), (1, 0)])


def gather_rows(values, me, count):
    if count != 2:
        return lax.all_gather(values, "tensor", axis=0, tiled=True)
    other = swap(values)
    first = jnp.where(me == 0, values, other)
    return jnp.concatenate([first, jnp.where(me == 0, other, values)], axis=0)


def both_parts(part, count):
    if count != 2:
        return (lax.psum(part, "tensor"), jnp.zeros_like(part))
    return (part, swap(part))


def scatter_rows(part, me, count):
    if count != 2:
        return lax.psum_scatter(part, "tensor", scatter_dimension=0, tiled=True).astype(f32)
    halves = part.reshape(2, part.shape[0] // 2, part.shape[1])
    arrived = swap(lax.dynamic_index_in_dim(halves, 1 - me, 0, keepdims=False))
    return lax.dynamic_index_in_dim(halves, me, 0, keepdims=False).astype(f32) + arrived.astype(f32)


def partners(count, bit):
    return [(i, i ^ bit) for i in range(count)]


def exchange(sent, count, bit):
    return lax.ppermute(sent, "dp", partners(count, bit))


class Reduction:
    def __init__(self, sent, kept, index, count, block):
        self.index, self.count, self.block, self.bit = index, count, block, 1
        self.kept = kept
        self.arrived = [exchange(part, count, 1) for part in sent]

    def done(self):
        return self.bit * 2 >= self.count

    def step(self, after=()):
        if self.done():
            return after
        self.bit *= 2
        which = ((self.index // self.bit) % 2).astype(jnp.int32).reshape(1)
        sent, self.kept = step_call(which, self.kept, self.arrived, self.block, after)
        self.arrived = [exchange(sent, self.count, self.bit)]
        return (sent,)

    def total(self):
        arrived = self.arrived[0] if len(self.arrived) == 1 else jnp.concatenate(self.arrived, axis=1)
        return self.kept.astype(f32) + arrived.astype(f32)


def segments(lengths, row_count):
    seq_ends = jnp.cumsum(lengths)
    places = jnp.arange(row_count, dtype=jnp.int32)
    passed = places[:, None] >= seq_ends[None, :]
    seq_ids = jnp.sum(passed.astype(jnp.int32), axis=1)
    starts = jnp.max(jnp.where(passed, seq_ends[None, :], 0), axis=1)
    is_live = (places < seq_ends[-1]).astype(f32)
    return (seq_ids, places - starts, is_live)


def body(
    dp_count, tensor_count, tokens, cotangent, seq_lengths, norm1_gain, norm2_gain, mixer_in, state_in, step_in,
    conv_inner, conv_state, step_bias, decay_log, skip_gain, mixer_out, query_in, key_value, attend_out, gate_up,
    down_out,
):
    share, model = tokens.shape
    rows = share * tensor_count
    me = lax.axis_index("tensor")
    index = lax.axis_index("dp")
    inner = mixer_in.shape[2]
    heads = step_in.shape[1]
    query_width = query_in.shape[1]
    qheads = query_width // HD
    wp, qwp = padded(inner), padded(query_width)
    span = min(LANES, rows)
    dims = (heads, qheads, wp, qwp, span)

    if tensor_count == 2:
        x_own, x_other = tokens, swap(tokens)
    else:
        x_own = x_other = gather_rows(tokens, me, tensor_count)
    place = jnp.stack([me, lax.rem(me + 1, tensor_count)]).astype(jnp.int32)
    seq_ids, positions, is_live = segments(seq_lengths[0], rows)
    live_share = lax.dynamic_slice_in_dim(is_live, me * share, share, 0)[:, None]
    dout_rows = gather_rows(lax.optimization_barrier((cotangent, x_other))[0], me, tensor_count)
    dout_rows = dout_rows * is_live[:, None].astype(bf16)

    seq_col = seq_ids.astype(f32)[:, None]
    seq_row = seq_ids.astype(f32)[None, :]
    shifts = jnp.minimum(jnp.arange(LANES, dtype=jnp.int32), 4)[None, :]
    masks = (positions[:, None] >= shifts).astype(f32)
    lane = jnp.arange(LANES)
    frequency = rope_base ** (-2.0 * (lane % (HD // 2)).astype(f32) / HD)
    angles = positions.astype(f32)[:, None] * frequency[None, :]
    cosine = jnp.cos(angles)
    sine = jnp.sin(angles) * jnp.where(lane % HD < HD // 2, -1.0, 1.0)[None, :]

    key_index = me * qheads // (QH // KVH)
    pair_local = lax.dynamic_slice_in_dim(key_value, key_index * HD, HD, 2).reshape(model, 2 * HD)
    if inner == wp:
        wzx = mixer_in.reshape(model, 2 * inner)
    else:
        wzx = pad_to(mixer_in, wp).reshape(model, 2 * wp)
    wsp = jnp.concatenate([pad_to(step_in, LANES), pair_local], axis=1)
    wq, wmix, watt = pad_to(query_in, qwp), pad_to(mixer_out, wp), pad_to(attend_out, qwp)
    taps = pad_to(conv_inner, wp)
    bias = pad_to(step_bias[None], LANES)
    rate = pad_to(jnp.exp(decay_log)[None], LANES)
    skip = pad_to(jnp.repeat(skip_gain, HD)[None], wp)
    gain1, gain2 = norm1_gain[None], norm2_gain[None]

    x_rows, act, pa, pb, y, cat, part = call(
        functools.partial(front_kernel, dims),
        [
            ((rows, model), bf16), ((rows, model), bf16), ((rows, wp + qwp + LANES), f32), ((rows, wp + 384), f32),
            ((rows, wp), f32), ((rows, wp + qwp), bf16), ((rows, model), bf16),
        ],
        [((rows, rows), f32), ((rows, rows), f32), ((rows, LANES), bf16)],
        (
            place, x_own, x_other, state_in, wsp, wzx, wq, wmix, watt, gain1, seq_col, seq_row, masks, cosine, sine, taps,
            conv_state, bias, rate, skip,
        ),
        1, (), 10 * COST_US,
    )
    own, other = both_parts(part, tensor_count)
    wgu = lax.optimization_barrier((gate_up, part))[0].reshape(model, -1)
    dhidden = mm(dout_rows, down_out)
    ff2 = wgu.shape[1]
    h1, n2, hidden, dgu, ffn_part, dn2_part = call(
        middle_kernel,
        [
            ((rows, model), f32), ((rows, model), bf16), ((rows, ff2 // 2), bf16), ((rows, ff2), bf16),
            ((rows, model), bf16), ((rows, model), bf16),
        ],
        [],
        (x_rows, own, other, gain2, wgu, down_out, dhidden),
    )
    dn2_own, dn2_other = both_parts(dn2_part, tensor_count)

    bit = (index % 2).astype(jnp.int32).reshape(1)
    block = model // dp_count
    cut = max(LANES, ff2 * 3 // 8 // LANES * LANES)

    def reduction(pairs, most, after=()):
        sent, kept = weight_halves(pairs, bit, block, most, after)
        return Reduction(sent, kept, index, dp_count, block)

    ffn_a = reduction([(dout_rows, hidden, 0, cut)], 768)
    ffn_b = reduction([(dout_rows, hidden, cut, ff2 // 2), (n2, dgu, 0, ff2)], 768, (ffn_a.kept,))
    order = ffn_a.step((ffn_b.kept,))
    order = ffn_b.step(order)

    dh1_share, ffn_send, dmix, dy, da, gn2 = call(
        functools.partial(attend_back_kernel, dims, share),
        [
            ((share, model), f32), ((share, model), bf16), ((rows, model), bf16), ((rows, wp), f32),
            ((rows, wp + qwp + LANES), bf16), ((1, model), f32),
        ],
        [((rows, rows), f32), ((rows, model), f32), ((rows, qwp), bf16), ((rows, LANES), f32), ((rows, LANES), f32)],
        (
            place, dn2_own, dn2_other, ffn_part, h1, dout_rows, gain2, wmix, watt, seq_col, seq_row, cosine, sine, pa, y,
        ),
        1, order, 40 * COST_US,
    )
    order = ffn_a.step((dmix,))
    mix_out = reduction([(dmix, cat, 0, wp + qwp)], 2048, order)
    mix_a = reduction([(act, da, 0, wp + qwp + LANES)], 2048, (mix_out.kept,))
    order = ffn_b.step((mix_a.kept,))
    order = mix_out.step(order)

    dxb, dact, gn1, gcx, gcs, gstep, gskip = call(
        functools.partial(mixer_back_kernel, dims),
        [
            ((rows, wp + 384), bf16), ((rows, model), bf16),
            ((1, model), f32), ((4, wp), f32), ((4, 256), f32), ((2, LANES), f32), ((1, wp), f32),
        ],
        [
            ((rows, rows), f32), ((rows, rows), f32), ((rows, rows), f32), ((rows, wp), f32), ((rows, wp), f32),
        ],
        (
            pb, dy, y, wzx, state_in, wsp, da, wq, x_rows, seq_col, seq_row, masks, taps, conv_state, bias, rate, skip,
        ),
        0, order, 40 * COST_US,
    )
    shared = jnp.concatenate([gn1[0], gn2[0] * (1.0 / tensor_count), gcs.reshape(-1)]).reshape(-1, LANES)
    local = jnp.concatenate([gcx.reshape(-1), gskip.reshape(-1), gstep.reshape(-1)]).reshape(-1, LANES)
    shared_rows = shared.shape[0]
    minor = jnp.concatenate([shared, local], axis=0)

    def minor_step(values, bit, after):
        arrived = exchange(values, dp_count, bit)
        return call(add_kernel, [(values.shape, f32)], [], (values, arrived), 0, after)[0]

    order = mix_out.step((dxb,))
    order = mix_a.step(order)
    mix_b = reduction([(act, dxb, 0, wp + 384)], 2048, order)
    order = mix_b.step((mix_b.kept,))
    minor_bit = 1
    for r in [ffn_a, ffn_b, mix_a, mix_out, mix_b, mix_a] + 4 * [ffn_a, ffn_b, mix_out, mix_a, mix_b]:
        if r.done():
            continue
        if minor_bit < dp_count:
            minor = minor_step(minor, minor_bit, order)
            minor_bit *= 2
            order = (minor,)
        order = r.step(order)
    while minor_bit < dp_count:
        minor = minor_step(minor, minor_bit, order)
        minor_bit *= 2
    ffn_a, ffn_b, mix_a, mix_b = ffn_a.total(), ffn_b.total(), mix_a.total(), mix_b.total()
    out_total, first_total = mix_out.total(), mix_a
    down_total = jnp.concatenate([ffn_a, ffn_b[:, : ff2 // 2 - cut]], axis=1)
    up_total = ffn_b[:, ff2 // 2 - cut :]
    second_total, state_total = mix_b[:, :wp], mix_b[:, wp : wp + 256]
    step_total = mix_b[:, wp + 256 :]

    if tensor_count == 2:
        ffn_mine = lax.dynamic_slice_in_dim(ffn_part, me * share, share, 0).astype(f32)
        ffn_share = ffn_mine + lax.optimization_barrier((swap(ffn_send), dxb))[0].astype(f32)
    else:
        ffn_share = scatter_rows(ffn_part, me, tensor_count)
    h1_share = lax.dynamic_slice_in_dim(h1, me * share, share, 0)
    block_out = ((h1_share + ffn_share) * live_share).astype(bf16)

    dact_share = scatter_rows(dact, me, tensor_count)
    x_share = tokens.astype(f32)
    r1 = lax.rsqrt(jnp.mean(x_share * x_share, axis=-1, keepdims=True) + norm_eps)
    u = dact_share * gain1
    token_grad = dh1_share + r1 * u - x_share * (r1 * r1 * r1 * jnp.mean(u * x_share, axis=-1, keepdims=True))

    shared = lax.psum(minor[:shared_rows], "tensor") if tensor_count != 2 else minor[:shared_rows] + swap(minor[:shared_rows])
    shared = shared.reshape(-1)
    local = minor[shared_rows:].reshape(-1)
    g_norm1, g_norm2, g_conv_state = shared[:model], shared[model : 2 * model], shared[2 * model :].reshape(4, 256)
    g_conv_inner = local[: 4 * wp].reshape(4, wp)[:, :inner]
    g_skip = jnp.sum(local[4 * wp : 5 * wp].reshape(-1, HD), axis=1)[:heads]
    g_bias = local[5 * wp : 5 * wp + heads]
    g_decay = local[5 * wp + LANES : 5 * wp + LANES + heads]

    both = jnp.concatenate([state_total, first_total[:, wp + qwp :]], axis=1).astype(bf16)
    placed = lambda pair: lax.dynamic_update_slice_in_dim(
        jnp.zeros((block,) + key_value.shape[1:], f32), pair.astype(f32).reshape(block, 2, HD), key_index * HD, 2
    )
    if tensor_count == 2:
        arrived = swap(both)
        g_state = both[:, :256].astype(f32) + arrived[:, :256].astype(f32)
        mine = both[:, 256:].reshape(block, 2, HD)
        theirs = arrived[:, 256:].reshape(block, 2, HD)
        g_pair = jnp.concatenate(
            [jnp.where(me == 0, mine, theirs), jnp.where(me == 0, theirs, mine)], axis=2
        ).astype(f32)
    else:
        g_state = lax.psum(both[:, :256], "tensor").astype(f32)
        g_pair = lax.psum(placed(both[:, 256:]).astype(bf16), "tensor").astype(f32)

    g_mixer_in = jnp.stack([first_total[:, :inner], second_total[:, :inner]], axis=1)
    return (
        block_out,
        token_grad.astype(bf16),
        g_norm1,
        g_norm2,
        g_mixer_in,
        g_state,
        step_total[:, :heads],
        g_conv_inner,
        g_conv_state,
        g_bias,
        g_decay,
        g_skip,
        out_total[:, :inner],
        first_total[:, wp : wp + query_width],
        g_pair,
        out_total[:, wp : wp + query_width],
        up_total.reshape(block, 2, ff2 // 2),
        down_total,
    )


def solution(mesh):
    return jax.shard_map(
        functools.partial(body, mesh.shape["dp"], mesh.shape["tensor"]),
        mesh=mesh,
        in_specs=(
            P(("dp", "tensor"), None),
            P(("dp", "tensor"), None),
            P("dp", None),
            P(),
            P(),
            P(None, None, "tensor"),
            P(),
            P(None, "tensor"),
            P(None, "tensor"),
            P(),
            P("tensor"),
            P("tensor"),
            P("tensor"),
            P(None, "tensor"),
            P(None, "tensor"),
            P(),
            P(None, "tensor"),
            P(None, None, "tensor"),
            P(None, "tensor"),
        ),
        out_specs=(
            P(("dp", "tensor"), None),
            P(("dp", "tensor"), None),
            P(),
            P(),
            P("dp", None, "tensor"),
            P("dp", None),
            P("dp", "tensor"),
            P(None, "tensor"),
            P(),
            P("tensor"),
            P("tensor"),
            P("tensor"),
            P("dp", "tensor"),
            P("dp", "tensor"),
            P("dp", None, None),
            P("dp", "tensor"),
            P("dp", None, "tensor"),
            P("dp", "tensor"),
        ),
        check_vma=False,
    )
```

```python
import functools

import jax
import jax.numpy as jnp
from jax import lax
from jax.experimental import pallas as pl
from jax.experimental.pallas import tpu as pltpu
from jax.sharding import PartitionSpec as P

HD = 64
QH = 8
KVH = 2
LANES = 128

rope_base = 100000000000.0
norm_eps = 1e-05
far = -1e30
highest = lax.Precision.HIGHEST
f32 = jnp.float32
bf16 = jnp.bfloat16


def padded(width):
    return -(-width // LANES) * LANES


def pad_to(values, width):
    return jnp.pad(values, [(0, 0)] * (values.ndim - 1) + [(0, width - values.shape[-1])])


def mm(left, right):
    return jnp.dot(left, right, preferred_element_type=f32)


def mm_nt(left, right):
    return lax.dot_general(left, right, (((1,), (1,)), ((), ())), preferred_element_type=f32)


def mm_tn(left, right):
    return lax.dot_general(left, right, (((0,), (0,)), ((), ())), preferred_element_type=f32)


def mm_exact(left, right):
    return jnp.dot(left, right, preferred_element_type=f32, precision=highest)


def lane_ids(rows):
    return lax.broadcasted_iota(jnp.int32, (rows, LANES), 1)


def partner_half(values):
    lane = lane_ids(values.shape[0])
    return jnp.where(lane % HD < HD // 2, pltpu.roll(values, LANES - HD // 2, 1), pltpu.roll(values, HD // 2, 1))


def rotated(values, cosine, signed_sine):
    return values * cosine + partner_half(values) * signed_sine


def conv_terms(values, masks):
    return [pltpu.roll(values, offset, 0) * masks[offset] for offset in (3, 2, 1)] + [values]


def conv_back(grad, masks, taps):
    rows = grad.shape[0]
    total = grad * taps[3:4]
    for offset in (1, 2, 3):
        total = total + pltpu.roll(grad * masks[offset], rows - offset, 0) * taps[3 - offset : 4 - offset]
    return total


def link_bias(seq_col, seq_row, transposed):
    rows = seq_col.shape[0]
    down = lax.broadcasted_iota(jnp.int32, (rows, rows), 0)
    across = lax.broadcasted_iota(jnp.int32, (rows, rows), 1)
    ordered = down <= across if transposed else down >= across
    return (seq_col == seq_row) & ordered


def step_parts(raw, bias):
    shifted = raw + bias
    return jnp.maximum(shifted, 0.0) + jnp.log1p(jnp.exp(-jnp.abs(shifted)))


def spread_heads(columns, first, width):
    rows = columns.shape[0]
    low = jnp.broadcast_to(columns[:, first : first + 1], (rows, LANES))
    if width <= HD:
        return low
    high = jnp.broadcast_to(columns[:, first + 1 : first + 2], (rows, LANES))
    return jnp.where(lane_ids(rows) < HD, low, high)


def half_mask(rows, side):
    lane = lane_ids(rows)
    return lane < HD if side == 0 else lane >= HD


def front_kernel(
    dims, place_ref, own_ref, other_ref, wbc_ref, wsp_ref, wzx_ref, wq_ref, wmix_ref, watt_ref, gain_ref, seqc_ref,
    seqr_ref, masks_ref, cos_ref, sin_ref, convx_ref, convs_ref, bias_ref, rate_ref, skip_ref,
    x_ref, act_ref, pa_ref, pb_ref, y_ref, cat_ref, part_ref, neg_ref, g_ref, xdt_ref,
):
    heads, qheads, wp, qwp, span = dims
    rows = x_ref.shape[0]
    share = own_ref.shape[0]
    if share == rows:
        x_ref[...] = own_ref[...]
    else:
        x_ref[pl.ds(pl.multiple_of(place_ref[0] * share, 16), share), :] = own_ref[...]
        x_ref[pl.ds(pl.multiple_of(place_ref[1] * share, 16), share), :] = other_ref[...]
    finish(x_ref)
    x = x_ref[...].astype(f32)
    act = (x * lax.rsqrt(jnp.mean(x * x, axis=-1, keepdims=True) + norm_eps) * gain_ref[...]).astype(bf16)
    act_ref[...] = act
    finish(act_ref)
    pb_ref[:, wp : wp + 256] = mm(act, wbc_ref[...])
    pb_ref[:, wp + 256 :] = mm(act, wsp_ref[:, :LANES])
    pb_ref[:, :wp] = mm(act, wzx_ref[:, wp:])
    pa_ref[:, wp : wp + qwp] = mm(act, wq_ref[...])
    pa_ref[:, wp + qwp :] = mm(act, wsp_ref[:, LANES:])
    pa_ref[:, :wp] = mm(act, wzx_ref[:, :wp])
    finish(pa_ref, pb_ref)
    masks = {k: masks_ref[:, k : k + 1] for k in (1, 2, 3)}
    linked = link_bias(seqc_ref[...], seqr_ref[...], False)
    neg_ref[...] = jnp.where(linked, 0.0, far)
    dt = step_parts(pb_ref[:, wp + 256 :], bias_ref[...])
    decay = mm_exact(jnp.where(linked, 1.0, 0.0), -dt * rate_ref[...])
    decay_t = decay.T
    terms = conv_terms(pb_ref[:, wp : wp + 256], masks)
    bcc = sum(t * convs_ref[k : k + 1, :] for k, t in enumerate(terms))
    bcc = (bcc * jax.nn.sigmoid(bcc)).astype(bf16)
    g_ref[...] = mm_nt(bcc[:, 128:], bcc[:, :128])

    for p in range(wp // LANES):
        cols = slice(p * LANES, (p + 1) * LANES)
        width = HD * min(2, heads - 2 * p)
        conv = sum(t * convx_ref[k : k + 1, cols] for k, t in enumerate(conv_terms(pb_ref[:, cols], masks)))
        xc = conv * jax.nn.sigmoid(conv)
        xdt_ref[...] = (xc * spread_heads(dt, 2 * p, width)).astype(bf16)
        blocks = []
        for a in range(rows // span):
            here = slice(a * span, (a + 1) * span)
            reach = (a + 1) * span
            sides = []
            for h in range(2 * p, 2 * p + width // HD):
                gap = decay[here, h : h + 1] - decay_t[h : h + 1, :reach]
                mixing = g_ref[here, :reach] * jnp.exp(gap + neg_ref[here, :reach])
                sides.append(mm(mixing.astype(bf16), xdt_ref[:reach, :]))
            blocks.append(sides[0] if len(sides) == 1 else jnp.where(half_mask(span, 0), sides[0], sides[1]))
        y = jnp.concatenate(blocks, axis=0) + skip_ref[:, cols] * xc
        y_ref[:, cols] = y
        z = pa_ref[:, cols]
        cat_ref[:, cols] = (y * (z * jax.nn.sigmoid(z))).astype(bf16)

    finish(y_ref)
    cosine, sine = cos_ref[...], sin_ref[...]
    pair = pa_ref[:, wp + qwp :]
    swapped = pltpu.roll(pair, HD, 1)
    lower = half_mask(rows, 0)
    keys = rotated(jnp.where(lower, pair, swapped), cosine, sine).astype(bf16)
    values = jnp.where(lower, swapped, pair).astype(bf16)
    for p in range(qwp // LANES):
        cols = slice(wp + p * LANES, wp + (p + 1) * LANES)
        queries = rotated(pa_ref[:, cols], cosine, sine).astype(bf16)
        for a in range(rows // span):
            here = slice(a * span, (a + 1) * span)
            reach = (a + 1) * span
            sides = []
            for side in range(min(2, qheads - 2 * p)):
                q = jnp.where(half_mask(span, side), queries[here], jnp.zeros((), bf16))
                scores = mm_nt(q, keys[:reach]) * (HD**-0.5) + neg_ref[here, :reach]
                weights = jnp.exp(scores - jnp.max(scores, axis=-1, keepdims=True))
                probs = weights / jnp.sum(weights, axis=-1, keepdims=True)
                sides.append(mm(probs.astype(bf16), values[:reach]))
            if len(sides) == 1:
                out = jnp.where(half_mask(span, 0), sides[0], 0.0)
            else:
                out = jnp.where(half_mask(span, 0), sides[0], sides[1])
            cat_ref[here, cols] = out.astype(bf16)
    finish(cat_ref)
    part_ref[...] = (mm_nt(cat_ref[:, :wp], wmix_ref[...]) + mm_nt(cat_ref[:, wp:], watt_ref[...])).astype(bf16)


def middle_kernel(
    x_ref, own_ref, other_ref, gain_ref, wgu_ref, down_ref, dhid_ref,
    h1_ref, n2_ref, hidden_ref, dgu_ref, out_ref, dn2_ref,
):
    width = down_ref.shape[1]
    h1 = x_ref[...].astype(f32) + (own_ref[...].astype(f32) + other_ref[...].astype(f32))
    h1_ref[...] = h1
    finish(h1_ref)
    n2 = (h1 * lax.rsqrt(jnp.mean(h1 * h1, axis=-1, keepdims=True) + norm_eps) * gain_ref[...]).astype(bf16)
    n2_ref[...] = n2
    finish(n2_ref)
    gate = mm(n2, wgu_ref[:, :width])
    up = mm(n2, wgu_ref[:, width:])
    sig = jax.nn.sigmoid(gate)
    silu = gate * sig
    hidden = (silu * up).astype(bf16)
    hidden_ref[...] = hidden
    finish(hidden_ref)
    dhid = dhid_ref[...].astype(f32)
    dgu_ref[:, :width] = (dhid * up * (sig * (1.0 + gate * (1.0 - sig)))).astype(bf16)
    dgu_ref[:, width:] = (dhid * silu).astype(bf16)
    finish(dgu_ref)
    dn2_ref[...] = mm_nt(dgu_ref[...], wgu_ref[...]).astype(bf16)
    finish(dn2_ref)
    out_ref[...] = mm_nt(hidden, down_ref[...]).astype(bf16)


def attend_back_kernel(
    dims, share, place_ref, own_ref, other_ref, ffn_ref, h1_ref, dout_ref, gain2_ref, wmix_ref, watt_ref, seqc_ref,
    seqr_ref, cos_ref, sin_ref, pa_ref, y_ref,
    dh1_ref, ffn_send_ref, dmix_ref, dy_ref, da_ref, gn2_ref,
    neg_ref, dh1_all_ref, datt_ref, dk_ref, dv_ref,
):
    heads, qheads, wp, qwp, span = dims
    rows = own_ref.shape[0]
    dn2 = own_ref[...].astype(f32) + other_ref[...].astype(f32)
    h1 = h1_ref[...]
    r2 = lax.rsqrt(jnp.mean(h1 * h1, axis=-1, keepdims=True) + norm_eps)
    u = dn2 * gain2_ref[...]
    dh1 = dout_ref[...].astype(f32) + r2 * u - h1 * (r2 * r2 * r2 * jnp.mean(u * h1, axis=-1, keepdims=True))
    gn2_ref[...] = jnp.sum(dn2 * h1 * r2, axis=0, keepdims=True)
    dh1_all_ref[...] = dh1
    dh1_ref[...] = dh1_all_ref[pl.ds(pl.multiple_of(place_ref[0] * share, 16), share), :]
    ffn_send_ref[...] = ffn_ref[pl.ds(pl.multiple_of(place_ref[1] * share, 16), share), :]
    dmix = dh1.astype(bf16)
    dmix_ref[...] = dmix
    finish(dh1_ref, ffn_send_ref, dmix_ref)
    datt_ref[...] = mm(dmix, watt_ref[...]).astype(bf16)
    for p in range(wp // LANES):
        cols = slice(p * LANES, (p + 1) * LANES)
        dgated = mm(dmix, wmix_ref[:, cols])
        z = pa_ref[:, cols]
        sig = jax.nn.sigmoid(z)
        dy_ref[:, cols] = dgated * (z * sig)
        da_ref[:, cols] = (dgated * y_ref[:, cols] * (sig * (1.0 + z * (1.0 - sig)))).astype(bf16)
    finish(dy_ref)

    linked_t = link_bias(seqc_ref[...], seqr_ref[...], True)
    neg_ref[...] = jnp.where(linked_t, 0.0, far)
    lower = half_mask(rows, 0)
    cosine, sine = cos_ref[...], sin_ref[...]
    pair = pa_ref[:, wp + qwp :]
    swapped = pltpu.roll(pair, HD, 1)
    keys = rotated(jnp.where(lower, pair, swapped), cosine, sine).astype(bf16)
    values = jnp.where(lower, swapped, pair).astype(bf16)
    dk_ref[...] = jnp.zeros_like(dk_ref)
    dv_ref[...] = jnp.zeros_like(dv_ref)
    for p in range(qwp // LANES):
        cols = slice(wp + p * LANES, wp + (p + 1) * LANES)
        queries = rotated(pa_ref[:, cols], cosine, sine).astype(bf16)
        datt = datt_ref[:, p * LANES : (p + 1) * LANES]
        blocks = []
        for a in range(rows // span):
            here = slice(a * span, (a + 1) * span)
            reach = (a + 1) * span
            sides = []
            for side in range(min(2, qheads - 2 * p)):
                half = half_mask(span, side)
                q = jnp.where(half, queries[here], jnp.zeros((), bf16))
                do = jnp.where(half, datt[here], jnp.zeros((), bf16))
                scores = mm_nt(keys[:reach], q) * (HD**-0.5) + neg_ref[:reach, here]
                weights = jnp.exp(scores - jnp.max(scores, axis=0, keepdims=True))
                probs = weights / jnp.sum(weights, axis=0, keepdims=True)
                dp = mm_nt(values[:reach], do)
                ds = (probs * (dp - jnp.sum(probs * dp, axis=0, keepdims=True))).astype(bf16)
                dk_ref[:reach, :] += mm(ds, q)
                dv_ref[:reach, :] += mm(probs.astype(bf16), do)
                sides.append(mm_tn(ds, keys[:reach]))
            if len(sides) == 1:
                blocks.append(jnp.where(half_mask(span, 0), sides[0], 0.0))
            else:
                blocks.append(jnp.where(half_mask(span, 0), sides[0], sides[1]))
        dq = jnp.concatenate(blocks, axis=0) * (HD**-0.5)
        da_ref[:, cols] = rotated(dq, cosine, -sine).astype(bf16)
    dk = dk_ref[...] * (HD**-0.5)
    dk = rotated(dk + pltpu.roll(dk, HD, 1), cosine, -sine)
    dv = dv_ref[...]
    dv = dv + pltpu.roll(dv, HD, 1)
    da_ref[:, wp + qwp :] = jnp.where(lower, dk, dv).astype(bf16)


def mixer_back_kernel(
    dims, share, place_ref, pb_ref, dy_ref, y_ref, wzx_ref, wbc_ref, wsp_ref, da_ref, wq_ref, x_ref, seqc_ref, seqr_ref, masks_ref,
    convx_ref, convs_ref, bias_ref, rate_ref, skip_ref, gn2_ref,
    dxb_ref, dact_ref, dact_send_ref, small_ref,
    neg_ref, gt_ref, dgt_ref, dsum_ref, ddir_ref,
):
    heads, qheads, wp, qwp, span = dims
    rows = x_ref.shape[0]
    masks = {k: masks_ref[:, k : k + 1] for k in (1, 2, 3)}
    linked_t = link_bias(seqc_ref[...], seqr_ref[...], True)
    neg_ref[...] = jnp.where(linked_t, 0.0, far)
    dt = step_parts(pb_ref[:, wp + 256 :], bias_ref[...])
    linked = link_bias(seqc_ref[...], seqr_ref[...], False)
    decay = mm_exact(jnp.where(linked, 1.0, 0.0), -dt * rate_ref[...])
    decay_t = decay.T
    state = pb_ref[:, wp : wp + 256]
    sterms = conv_terms(state, masks)
    sconv = sum(t * convs_ref[k : k + 1, :] for k, t in enumerate(sterms))
    ssig = jax.nn.sigmoid(sconv)
    bcc = (sconv * ssig).astype(bf16)
    bm, cm = bcc[:, :128], bcc[:, 128:]
    gt_ref[...] = mm_nt(bm, cm)
    small_ref[...] = jnp.zeros_like(small_ref)
    dgt_ref[...] = jnp.zeros_like(dgt_ref)
    for p in range(wp // LANES):
        cols = slice(p * LANES, (p + 1) * LANES)
        width = HD * min(2, heads - 2 * p)
        terms = conv_terms(pb_ref[:, cols], masks)
        conv = sum(t * convx_ref[k : k + 1, cols] for k, t in enumerate(terms))
        csig = jax.nn.sigmoid(conv)
        xc = conv * csig
        dt_cols = spread_heads(dt, 2 * p, width)
        xdt = (xc * dt_cols).astype(bf16)
        skip = skip_ref[:, cols]
        scanned = y_ref[:, cols] - skip * xc
        dy = dy_ref[:, cols]
        small_ref[6:7, cols] = jnp.sum(dy * xc, axis=0, keepdims=True)
        dyb = dy.astype(bf16)
        blocks = []
        for a in range(rows // span):
            here = slice(a * span, (a + 1) * span)
            sides = []
            for side in range(width // HD):
                h = 2 * p + side
                dys = jnp.where(half_mask(rows - a * span, side), dyb[a * span :], jnp.zeros((), bf16))
                gap = decay_t[h : h + 1, a * span :] - decay[here, h : h + 1]
                falloff = jnp.exp(gap + neg_ref[here, a * span :])
                mixing = (gt_ref[here, a * span :] * falloff).astype(bf16)
                sides.append(mm(mixing, dyb[a * span :]))
                dgt_ref[here, a * span :] += mm_nt(xdt[here], dys) * falloff
            blocks.append(sides[0] if len(sides) == 1 else jnp.where(half_mask(span, 0), sides[0], sides[1]))
        dxdt = jnp.concatenate(blocks, axis=0)
        dsum_ref[:, cols] = dyb.astype(f32) * scanned - xdt.astype(f32) * dxdt
        ddir_ref[:, cols] = dxdt * xc
        dconv = (dxdt * dt_cols + skip * dy) * (csig * (1.0 + conv * (1.0 - csig)))
        small_ref[2:6, cols] = jnp.concatenate([jnp.sum(t * dconv, axis=0, keepdims=True) for t in terms], axis=0)
        dxb_ref[:, cols] = conv_back(dconv, masks, convx_ref[:, cols]).astype(bf16)

    dgt = dgt_ref[...].astype(bf16)
    dbcc = jnp.concatenate([mm(dgt, cm), mm_tn(dgt, bm)], axis=1)
    dsconv = dbcc * (ssig * (1.0 + sconv * (1.0 - ssig)))
    small_ref[2:6, wp : wp + 256] = jnp.concatenate([jnp.sum(t * dsconv, axis=0, keepdims=True) for t in sterms], axis=0)
    dxb_ref[:, wp : wp + 256] = conv_back(dsconv, masks, convs_ref[...]).astype(bf16)

    head_of = lax.broadcasted_iota(jnp.int32, (wp, LANES), 0) // HD
    pick = jnp.where(head_of == lax.broadcasted_iota(jnp.int32, (wp, LANES), 1), 1.0, 0.0)
    ds = mm_exact(dsum_ref[...], pick)
    ddirect = mm_exact(ddir_ref[...], pick)
    dlog = mm_exact(jnp.where(linked_t, 1.0, 0.0), ds)
    rate = rate_ref[...]
    ddt = ddirect - rate * dlog
    dstep = ddt * jax.nn.sigmoid(pb_ref[:, wp + 256 :] + bias_ref[...])
    dstep = jnp.where(lane_ids(rows) < heads, dstep, 0.0)
    dxb_ref[:, wp + 256 :] = dstep.astype(bf16)
    small_ref[6:7, wp : wp + LANES] = jnp.sum(dstep, axis=0, keepdims=True)
    small_ref[6:7, wp + LANES : wp + 256] = -rate * jnp.sum(dt * dlog, axis=0, keepdims=True)
    finish(dxb_ref)
    dact = mm_nt(da_ref[:, :wp], wzx_ref[:, :wp]) + mm_nt(dxb_ref[:, :wp], wzx_ref[:, wp:])
    dact = dact + mm_nt(dxb_ref[:, wp : wp + 256], wbc_ref[...]) + mm_nt(da_ref[:, wp : wp + qwp], wq_ref[...])
    dact = dact + mm_nt(dxb_ref[:, wp + 256 :], wsp_ref[:, :LANES]) + mm_nt(da_ref[:, wp + qwp :], wsp_ref[:, LANES:])
    dact_ref[...] = dact.astype(bf16)
    finish(dact_ref)
    dact_send_ref[...] = dact_ref[pl.ds(pl.multiple_of(place_ref[1] * share, 16), share), :]
    finish(dact_send_ref)
    x = x_ref[...].astype(f32)
    r1 = lax.rsqrt(jnp.mean(x * x, axis=-1, keepdims=True) + norm_eps)
    small_ref[0:1, :] = jnp.sum(dact * x * r1, axis=0, keepdims=True)
    small_ref[1:2, :] = gn2_ref[...] * (share / rows)


def pieces_of(width, most):
    groups = width // LANES
    count = -(-groups // (most // LANES))
    edges = [(i * groups // count) * LANES for i in range(count + 1)]
    return list(zip(edges[:-1], edges[1:]))


def grad_kernel(cuts, pieces, block, bit_ref, *refs):
    pairs = len(cuts)
    ins, refs = refs[: 2 * pairs], refs[2 * pairs :]
    sents, kepts, refs = refs[: len(pieces)], refs[len(pieces) : 2 * len(pieces)], refs[2 * len(pieces) :]
    buffers, refs = refs[: 2 * pairs], refs[2 * pairs :]
    turned, stage, in_sems, sent_sems, kept_sems = refs
    fetched = [Fetched(ins[i], buffers[i], in_sems.at[i]) for i in range(2 * pairs)]
    bit = bit_ref[0]
    count = turned.shape[0] // (2 * block)
    copies, at, sent_to = [], 0, 0
    for k, (low, high) in enumerate(cuts):
        turned[...] = fetched[2 * k][...].astype(f32).T.astype(bf16)
        for start in range(low, high, 512):
            stop = min(start + 512, high)
            full = mm(turned[...], fetched[2 * k + 1][:, start:stop]).astype(bf16)
            for j in range(2 * count):
                side = 1 - bit if j % 2 == 0 else bit
                stage[side, (j // 2) * block : (j // 2 + 1) * block, at : at + stop - start] = full[j * block : (j + 1) * block]
            at += stop - start
            while sent_to < len(pieces) and pieces[sent_to][1] <= at:
                cols = pl.ds(pieces[sent_to][0], pieces[sent_to][1] - pieces[sent_to][0])
                copies.append(pltpu.make_async_copy(stage.at[0, :, cols], sents[sent_to], sent_sems.at[sent_to]))
                copies.append(pltpu.make_async_copy(stage.at[1, :, cols], kepts[sent_to], kept_sems.at[sent_to]))
                copies[-2].start()
                copies[-1].start()
                sent_to += 1
    for copy in copies:
        copy.wait()


def plain_params(flops=1000):
    return dict(
        compiler_params=pltpu.CompilerParams(vmem_limit_bytes=52 * 1024 * 1024),
        cost_estimate=pl.CostEstimate(flops=flops, bytes_accessed=1000, transcendentals=0),
    )


def weight_halves(pairs, bit, block, most, after=()):
    args = [a for left, right, _, _ in pairs for a in (left, right)]
    cuts = [(low, high) for _, _, low, high in pairs]
    rows, model = pairs[0][0].shape
    width = sum(high - low for low, high in cuts)
    pieces = pieces_of(width, most)
    outs = [(model // 2, high - low) for low, high in pieces] * 2

    def wrapped(bit_ref, *refs):
        grad_kernel(cuts, pieces, block, bit_ref, *refs[: len(args)], *refs[len(args) + len(after) :])

    outs = pl.pallas_call(
        wrapped,
        out_shape=[jax.ShapeDtypeStruct(s, bf16) for s in outs],
        in_specs=[pl.BlockSpec(memory_space=pltpu.SMEM)] + [pl.BlockSpec(memory_space=pltpu.HBM)] * (len(args) + len(after)),
        out_specs=[pl.BlockSpec(memory_space=pltpu.HBM)] * len(outs),
        scratch_shapes=[pltpu.VMEM(a.shape, a.dtype) for a in args]
        + [
            pltpu.VMEM((model, rows), bf16), pltpu.VMEM((2, model // 2, width), bf16),
            pltpu.SemaphoreType.DMA((len(args),)), pltpu.SemaphoreType.DMA((len(pieces),)),
            pltpu.SemaphoreType.DMA((len(pieces),)),
        ],
        **plain_params(),
    )(bit, *args, *after)
    return outs[: len(pieces)], outs[len(pieces) :]


def step_kernel(pieces, sources, block, small, which_ref, *refs):
    arrays, refs = refs[: 2 * sources], refs[2 * sources :]
    if small:
        small_own, small_other, refs = refs[0], refs[1], refs[2:]
    away, mine, refs = refs[0], refs[1], refs[2:]
    if small:
        small_ref, refs = refs[0], refs[1:]
    kept_buf, arrived_buf, away_buf, mine_buf, kept_sems, arrived_sems, away_sems, mine_sems = refs
    which = which_ref[0]
    ins, outs = [], []
    for k, (source, low, at, width) in enumerate(pieces):
        cols, here = pl.ds(low, width), pl.ds(at, width)
        ins.append(pltpu.make_async_copy(arrays[2 * source].at[:, cols], kept_buf.at[:, here], kept_sems.at[k]))
        ins.append(pltpu.make_async_copy(arrays[2 * source + 1].at[:, cols], arrived_buf.at[:, here], arrived_sems.at[k]))
        ins[-2].start()
        ins[-1].start()
    if small:
        small_ref[...] = small_own[...] + small_other[...]
    for k, (source, low, at, width) in enumerate(pieces):
        ins[2 * k].wait()
        ins[2 * k + 1].wait()
        here = pl.ds(at, width)
        for out, target, sems, side in ((away_buf, away, away_sems, 1 - which), (mine_buf, mine, mine_sems, which)):
            for i in range(kept_buf.shape[0] // (2 * block)):
                rows = pl.ds(pl.multiple_of((2 * i + side) * block, block), block)
                total = kept_buf[rows, at : at + width].astype(f32) + arrived_buf[rows, at : at + width].astype(f32)
                out[i * block : (i + 1) * block, at : at + width] = total.astype(bf16)
            outs.append(pltpu.make_async_copy(out.at[:, here], target.at[:, here], sems.at[k]))
            outs[-1].start()
    for copy in outs:
        copy.wait()


def step_call(which, sources, block, after, small=()):
    rows = sources[0][0].shape[0]
    pieces, at = [], 0
    for i, (kept, _) in enumerate(sources):
        for low, high in pieces_of(kept.shape[1], 512):
            pieces.append((i, low, at + low, high - low))
        at += kept.shape[1]
    args = [a for pair in sources for a in pair]

    def wrapped(which_ref, *refs):
        used = len(args) + len(small)
        step_kernel(pieces, len(sources), block, bool(small), which_ref, *refs[:used], *refs[used + len(after) :])

    half = (rows // 2, at)
    anywhere = pl.BlockSpec(memory_space=pltpu.HBM)
    inside = pl.BlockSpec(memory_space=pltpu.VMEM)
    return pl.pallas_call(
        wrapped,
        out_shape=[jax.ShapeDtypeStruct(half, bf16)] * 2 + [jax.ShapeDtypeStruct(a.shape, f32) for a in small[:1]],
        in_specs=[pl.BlockSpec(memory_space=pltpu.SMEM)] + [anywhere] * len(args) + [inside] * len(small)
        + [anywhere] * len(after),
        out_specs=[anywhere] * 2 + [inside] * len(small[:1]),
        scratch_shapes=[pltpu.VMEM((rows, at), bf16)] * 2
        + [pltpu.VMEM(half, bf16)] * 2
        + [pltpu.SemaphoreType.DMA((len(pieces),))] * 4,
        **plain_params(),
    )(which, *args, *small, *after)


class Fetched:
    def __init__(self, source, held, sem):
        self.held, self.copy, self.ready = held, pltpu.make_async_copy(source, held, sem), False
        self.shape, self.dtype = held.shape, held.dtype
        self.copy.start()

    def __getitem__(self, key):
        if not self.ready:
            self.copy.wait()
            self.ready = True
        return self.held[key]


class Stored:
    def __init__(self, held, target, sem):
        self.held, self.copy, self.sent = held, pltpu.make_async_copy(held, target, sem), False
        self.shape, self.dtype = held.shape, held.dtype

    def __getitem__(self, key):
        return self.held[key]

    def __setitem__(self, key, value):
        self.held[key] = value

    def finish(self):
        if not self.sent:
            self.copy.start()
            self.sent = True


LARGE = 1 << 16
COST_US = 1100000000


def finish(*refs):
    for ref in refs:
        if isinstance(ref, Stored):
            ref.finish()


def call(kernel, outs, scratch, args, scalars=0, after=(), flops=1000):
    count = len(args)
    large_in = [i >= scalars and a.size * a.dtype.itemsize >= LARGE for i, a in enumerate(args)]
    large_out = [s[0] * s[1] * jnp.dtype(t).itemsize >= LARGE for s, t in outs]
    buffers = [pltpu.VMEM(a.shape, a.dtype) for a, big in zip(args, large_in) if big]
    buffers += [pltpu.VMEM(s, t) for (s, t), big in zip(outs, large_out) if big]
    copies = len(buffers)

    def wrapped(*refs):
        ins, rest = list(refs[:count]), refs[count + len(after) :]
        results, rest = list(rest[: len(outs)]), rest[len(outs) :]
        held, sems, inner = rest[:copies], rest[copies], rest[copies + 1 :]
        slot = 0
        for i, big in enumerate(large_in):
            if big:
                ins[i] = Fetched(ins[i], held[slot], sems.at[slot])
                slot += 1
        for i, big in enumerate(large_out):
            if big:
                results[i] = Stored(held[slot], results[i], sems.at[slot])
                slot += 1
        kernel(*ins, *results, *inner)
        finish(*results)
        for ref in ins:
            if isinstance(ref, Fetched) and not ref.ready:
                ref.copy.wait()
        for ref in results:
            if isinstance(ref, Stored):
                ref.copy.wait()

    spaces = [pltpu.SMEM] * scalars + [pltpu.HBM if big else pltpu.VMEM for big in large_in[scalars:]] + [pltpu.HBM] * len(after)
    return pl.pallas_call(
        wrapped,
        out_shape=[jax.ShapeDtypeStruct(s, t) for s, t in outs],
        in_specs=[pl.BlockSpec(memory_space=space) for space in spaces],
        out_specs=[pl.BlockSpec(memory_space=pltpu.HBM if big else pltpu.VMEM) for big in large_out],
        scratch_shapes=buffers + [pltpu.SemaphoreType.DMA((max(copies, 1),))] + [pltpu.VMEM(s, t) for s, t in scratch],
        **plain_params(flops),
    )(*args, *after)


def swap(values):
    return lax.ppermute(values, "tensor", [(0, 1), (1, 0)])


def gather_rows(values, me, count):
    if count != 2:
        return lax.all_gather(values, "tensor", axis=0, tiled=True)
    other = swap(values)
    first = jnp.where(me == 0, values, other)
    return jnp.concatenate([first, jnp.where(me == 0, other, values)], axis=0)


def both_parts(part, count):
    if count != 2:
        return (lax.psum(part, "tensor"), jnp.zeros_like(part))
    return (part, swap(part))


def scatter_rows(part, me, count):
    if count != 2:
        return lax.psum_scatter(part, "tensor", scatter_dimension=0, tiled=True).astype(f32)
    halves = part.reshape(2, part.shape[0] // 2, part.shape[1])
    arrived = swap(lax.dynamic_index_in_dim(halves, 1 - me, 0, keepdims=False))
    return lax.dynamic_index_in_dim(halves, me, 0, keepdims=False).astype(f32) + arrived.astype(f32)


def partners(count, bit):
    return [(i, i ^ bit) for i in range(count)]


def exchange(sent, count, bit):
    return lax.ppermute(sent, "dp", partners(count, bit))


class Reduction:
    def __init__(self, parts, index, count, block, bit=1, small=None):
        self.parts, self.index, self.count, self.block, self.bit = parts, index, count, block, bit
        self.small = small
        self.small_arrived = None if small is None else exchange(small, count, bit)

    def done(self):
        return self.bit * 2 >= self.count

    def step(self, after=()):
        if self.done():
            return after
        self.bit *= 2
        which = ((self.index // self.bit) % 2).astype(jnp.int32).reshape(1)
        small = () if self.small is None else (self.small, self.small_arrived)
        sent, kept, *small = step_call(which, self.parts, self.block, after, small)
        self.parts = [(kept, exchange(sent, self.count, self.bit))]
        if small:
            self.small = small[0]
            self.small_arrived = exchange(self.small, self.count, self.bit)
        return (sent,)

    def total(self, after):
        kept, arrived = self.parts[0]
        if self.bit > 1:
            arrived = lax.optimization_barrier((arrived, after[0]))[0]
        return kept.astype(f32) + arrived.astype(f32)


def segments(lengths, row_count):
    seq_ends = jnp.cumsum(lengths)
    places = jnp.arange(row_count, dtype=jnp.int32)
    passed = places[:, None] >= seq_ends[None, :]
    seq_ids = jnp.sum(passed.astype(jnp.int32), axis=1)
    starts = jnp.max(jnp.where(passed, seq_ends[None, :], 0), axis=1)
    is_live = (places < seq_ends[-1]).astype(f32)
    return (seq_ids, places - starts, is_live)


def body(
    dp_count, tensor_count, tokens, cotangent, seq_lengths, norm1_gain, norm2_gain, mixer_in, state_in, step_in,
    conv_inner, conv_state, step_bias, decay_log, skip_gain, mixer_out, query_in, key_value, attend_out, gate_up,
    down_out,
):
    share, model = tokens.shape
    rows = share * tensor_count
    me = lax.axis_index("tensor")
    index = lax.axis_index("dp")
    inner = mixer_in.shape[2]
    heads = step_in.shape[1]
    query_width = query_in.shape[1]
    qheads = query_width // HD
    wp, qwp = padded(inner), padded(query_width)
    span = min(LANES, rows)
    dims = (heads, qheads, wp, qwp, span)

    if tensor_count == 2:
        x_own, x_other = tokens, swap(tokens)
    else:
        x_own = x_other = gather_rows(tokens, me, tensor_count)
    place = jnp.stack([me, lax.rem(me + 1, tensor_count)]).astype(jnp.int32)
    seq_ids, positions, is_live = segments(seq_lengths[0], rows)
    live_share = lax.dynamic_slice_in_dim(is_live, me * share, share, 0)[:, None]
    dout_rows = gather_rows(lax.optimization_barrier((cotangent, x_other))[0], me, tensor_count)
    dout_rows = dout_rows * is_live[:, None].astype(bf16)

    seq_col = seq_ids.astype(f32)[:, None]
    seq_row = seq_ids.astype(f32)[None, :]
    shifts = jnp.minimum(jnp.arange(LANES, dtype=jnp.int32), 4)[None, :]
    masks = (positions[:, None] >= shifts).astype(f32)
    lane = jnp.arange(LANES)
    frequency = rope_base ** (-2.0 * (lane % (HD // 2)).astype(f32) / HD)
    angles = positions.astype(f32)[:, None] * frequency[None, :]
    cosine = jnp.cos(angles)
    sine = jnp.sin(angles) * jnp.where(lane % HD < HD // 2, -1.0, 1.0)[None, :]

    key_index = me * qheads // (QH // KVH)
    pair_local = lax.dynamic_slice_in_dim(key_value, key_index * HD, HD, 2).reshape(model, 2 * HD)
    if inner == wp:
        wzx = mixer_in.reshape(model, 2 * inner)
    else:
        wzx = pad_to(mixer_in, wp).reshape(model, 2 * wp)
    wsp = jnp.concatenate([pad_to(step_in, LANES), pair_local], axis=1)
    wq, wmix, watt = pad_to(query_in, qwp), pad_to(mixer_out, wp), pad_to(attend_out, qwp)
    taps = pad_to(conv_inner, wp)
    bias = pad_to(step_bias[None], LANES)
    rate = pad_to(jnp.exp(decay_log)[None], LANES)
    skip = pad_to(jnp.repeat(skip_gain, HD)[None], wp)
    gain1, gain2 = norm1_gain[None], norm2_gain[None]

    x_rows, act, pa, pb, y, cat, part = call(
        functools.partial(front_kernel, dims),
        [
            ((rows, model), bf16), ((rows, model), bf16), ((rows, wp + qwp + LANES), f32), ((rows, wp + 384), f32),
            ((rows, wp), f32), ((rows, wp + qwp), bf16), ((rows, model), bf16),
        ],
        [((rows, rows), f32), ((rows, rows), f32), ((rows, LANES), bf16)],
        (
            place, x_own, x_other, state_in, wsp, wzx, wq, wmix, watt, gain1, seq_col, seq_row, masks, cosine, sine, taps,
            conv_state, bias, rate, skip,
        ),
        1, (), 10 * COST_US,
    )
    own, other = both_parts(part, tensor_count)
    wgu = lax.optimization_barrier((gate_up, part))[0].reshape(model, -1)
    dhidden = mm(dout_rows, down_out)
    ff2 = wgu.shape[1]
    h1, n2, hidden, dgu, ffn_part, dn2_part = call(
        middle_kernel,
        [
            ((rows, model), f32), ((rows, model), bf16), ((rows, ff2 // 2), bf16), ((rows, ff2), bf16),
            ((rows, model), bf16), ((rows, model), bf16),
        ],
        [],
        (x_rows, own, other, gain2, wgu, down_out, dhidden),
    )
    dn2_own, dn2_other = both_parts(dn2_part, tensor_count)

    bit = (index % 2).astype(jnp.int32).reshape(1)
    block = model // dp_count

    def reduction(pairs, most, after=(), small=None):
        sent, kept = weight_halves(pairs, bit, block, most, after)
        parts = [(stay, exchange(go, dp_count, 1)) for go, stay in zip(sent, kept)]
        return Reduction(parts, index, dp_count, block, 1, small)

    ffn_a = reduction([(dout_rows, hidden, 0, ff2 // 2)], 512)
    ffn_b = reduction([(n2, dgu, 0, ff2)], 2048, (ffn_a.parts[0][0],))
    order = ffn_a.step((ffn_b.parts[0][0],))

    dh1_share, ffn_send, dmix, dy, da, gn2 = call(
        functools.partial(attend_back_kernel, dims, share),
        [
            ((share, model), f32), ((share, model), bf16), ((rows, model), bf16), ((rows, wp), f32),
            ((rows, wp + qwp + LANES), bf16), ((1, model), f32),
        ],
        [((rows, rows), f32), ((rows, model), f32), ((rows, qwp), bf16), ((rows, LANES), f32), ((rows, LANES), f32)],
        (
            place, dn2_own, dn2_other, ffn_part, h1, dout_rows, gain2, wmix, watt, seq_col, seq_row, cosine, sine, pa, y,
        ),
        1, order, 40 * COST_US,
    )
    order = ffn_a.step((dmix,))
    order = ffn_b.step(order)
    mix_out = reduction([(dmix, cat, 0, wp + qwp)], 2048, order)
    mix_a = reduction([(act, da, 0, wp + qwp + LANES)], 2048, (mix_out.parts[0][0],))
    order = ffn_a.step((mix_a.parts[0][0],))
    order = mix_out.step(order)
    ffn_arrived = swap(ffn_send) if tensor_count == 2 else ffn_send

    dxb, dact, dact_send, small = call(
        functools.partial(mixer_back_kernel, dims, share),
        [((rows, wp + 384), bf16), ((rows, model), bf16), ((share, model), bf16), ((8, model), f32)],
        [
            ((rows, rows), f32), ((rows, rows), f32), ((rows, rows), f32), ((rows, wp), f32), ((rows, wp), f32),
        ],
        (
            place, pb, dy, y, wzx, state_in, wsp, da, wq, x_rows, seq_col, seq_row, masks, taps, conv_state, bias, rate,
            skip, gn2,
        ),
        1, order + (ffn_arrived,), 40 * COST_US,
    )
    order = ffn_b.step((dxb,))
    order = mix_out.step(order)
    order = mix_a.step(order)
    mix_b = reduction([(act, dxb, 0, wp + 384)], 384, order, small)
    order = mix_b.step((mix_b.parts[0][0],))
    order = ffn_b.step(order)
    order = mix_a.step(order)
    order = mix_out.step(order)
    if tensor_count == 2:
        dact_mine = lax.dynamic_slice_in_dim(dact, me * share, share, 0).astype(f32)
        dact_share = dact_mine + lax.optimization_barrier((swap(dact_send), order[0]))[0].astype(f32)
    else:
        dact_share = scatter_rows(dact, me, tensor_count)
    for r in [mix_b, mix_a] + 4 * [ffn_a, ffn_b, mix_out, mix_a, mix_b]:
        order = r.step(order)
    down_total, up_total = ffn_a.total(order), ffn_b.total(order)
    out_total, first_total = mix_out.total(order), mix_a.total(order)
    mix_b, minor = mix_b.total(order), mix_b.small + mix_b.small_arrived
    second_total, state_total = mix_b[:, :wp], mix_b[:, wp : wp + 256]
    step_total = mix_b[:, wp + 256 :]

    if tensor_count == 2:
        ffn_mine = lax.dynamic_slice_in_dim(ffn_part, me * share, share, 0).astype(f32)
        ffn_share = ffn_mine + ffn_arrived.astype(f32)
    else:
        ffn_share = scatter_rows(ffn_part, me, tensor_count)
    h1_share = lax.dynamic_slice_in_dim(h1, me * share, share, 0)
    block_out = ((h1_share + ffn_share) * live_share).astype(bf16)

    x_share = tokens.astype(f32)
    r1 = lax.rsqrt(jnp.mean(x_share * x_share, axis=-1, keepdims=True) + norm_eps)
    u = dact_share * gain1
    token_grad = dh1_share + r1 * u - x_share * (r1 * r1 * r1 * jnp.mean(u * x_share, axis=-1, keepdims=True))

    shared = minor + swap(minor) if tensor_count == 2 else lax.psum(minor, "tensor")
    g_norm1, g_norm2, g_conv_state = shared[0], shared[1], shared[2:6, wp : wp + 256]
    g_conv_inner = minor[2:6, :inner]
    g_skip = jnp.sum(minor[6, :wp].reshape(-1, HD), axis=1)[:heads]
    g_bias = minor[6, wp : wp + heads]
    g_decay = minor[6, wp + LANES : wp + LANES + heads]

    both = jnp.concatenate([state_total, first_total[:, wp + qwp :]], axis=1).astype(bf16)
    placed = lambda pair: lax.dynamic_update_slice_in_dim(
        jnp.zeros((block,) + key_value.shape[1:], f32), pair.astype(f32).reshape(block, 2, HD), key_index * HD, 2
    )
    if tensor_count == 2:
        arrived = swap(both)
        g_state = both[:, :256].astype(f32) + arrived[:, :256].astype(f32)
        mine = both[:, 256:].reshape(block, 2, HD)
        theirs = arrived[:, 256:].reshape(block, 2, HD)
        g_pair = jnp.concatenate(
            [jnp.where(me == 0, mine, theirs), jnp.where(me == 0, theirs, mine)], axis=2
        ).astype(f32)
    else:
        g_state = lax.psum(both[:, :256], "tensor").astype(f32)
        g_pair = lax.psum(placed(both[:, 256:]).astype(bf16), "tensor").astype(f32)

    g_mixer_in = jnp.stack([first_total[:, :inner], second_total[:, :inner]], axis=1)
    return (
        block_out,
        token_grad.astype(bf16),
        g_norm1,
        g_norm2,
        g_mixer_in,
        g_state,
        step_total[:, :heads],
        g_conv_inner,
        g_conv_state,
        g_bias,
        g_decay,
        g_skip,
        out_total[:, :inner],
        first_total[:, wp : wp + query_width],
        g_pair,
        out_total[:, wp : wp + query_width],
        up_total.reshape(block, 2, ff2 // 2),
        down_total,
    )


def solution(mesh):
    return jax.shard_map(
        functools.partial(body, mesh.shape["dp"], mesh.shape["tensor"]),
        mesh=mesh,
        in_specs=(
            P(("dp", "tensor"), None),
            P(("dp", "tensor"), None),
            P("dp", None),
            P(),
            P(),
            P(None, None, "tensor"),
            P(),
            P(None, "tensor"),
            P(None, "tensor"),
            P(),
            P("tensor"),
            P("tensor"),
            P("tensor"),
            P(None, "tensor"),
            P(None, "tensor"),
            P(),
            P(None, "tensor"),
            P(None, None, "tensor"),
            P(None, "tensor"),
        ),
        out_specs=(
            P(("dp", "tensor"), None),
            P(("dp", "tensor"), None),
            P(),
            P(),
            P("dp", None, "tensor"),
            P("dp", None),
            P("dp", "tensor"),
            P(None, "tensor"),
            P(),
            P("tensor"),
            P("tensor"),
            P("tensor"),
            P("dp", "tensor"),
            P("dp", "tensor"),
            P("dp", None, None),
            P("dp", "tensor"),
            P("dp", None, "tensor"),
            P("dp", "tensor"),
        ),
        check_vma=False,
    )
```

```python
import functools

import jax
import jax.numpy as jnp
from jax import lax
from jax.experimental import pallas as pl
from jax.experimental.pallas import tpu as pltpu
from jax.sharding import PartitionSpec as P

HD = 64
QH = 8
KVH = 2
LANES = 128

rope_base = 100000000000.0
norm_eps = 1e-05
far = -1e30
highest = lax.Precision.HIGHEST
f32 = jnp.float32
bf16 = jnp.bfloat16


def padded(width):
    return -(-width // LANES) * LANES


def pad_to(values, width):
    return jnp.pad(values, [(0, 0)] * (values.ndim - 1) + [(0, width - values.shape[-1])])


def mm(left, right):
    return jnp.dot(left, right, preferred_element_type=f32)


def mm_nt(left, right):
    return lax.dot_general(left, right, (((1,), (1,)), ((), ())), preferred_element_type=f32)


def mm_tn(left, right):
    return lax.dot_general(left, right, (((0,), (0,)), ((), ())), preferred_element_type=f32)


def mm_exact(left, right):
    return jnp.dot(left, right, preferred_element_type=f32, precision=highest)


def lane_ids(rows):
    return lax.broadcasted_iota(jnp.int32, (rows, LANES), 1)


def partner_half(values):
    lane = lane_ids(values.shape[0])
    return jnp.where(lane % HD < HD // 2, pltpu.roll(values, LANES - HD // 2, 1), pltpu.roll(values, HD // 2, 1))


def rotated(values, cosine, signed_sine):
    return values * cosine + partner_half(values) * signed_sine


def conv_terms(values, masks):
    return [pltpu.roll(values, offset, 0) * masks[offset] for offset in (3, 2, 1)] + [values]


def conv_back(grad, masks, taps):
    rows = grad.shape[0]
    total = grad * taps[3:4]
    for offset in (1, 2, 3):
        total = total + pltpu.roll(grad * masks[offset], rows - offset, 0) * taps[3 - offset : 4 - offset]
    return total


def link_bias(seq_col, seq_row, transposed):
    rows = seq_col.shape[0]
    down = lax.broadcasted_iota(jnp.int32, (rows, rows), 0)
    across = lax.broadcasted_iota(jnp.int32, (rows, rows), 1)
    ordered = down <= across if transposed else down >= across
    return (seq_col == seq_row) & ordered


def step_parts(raw, bias):
    shifted = raw + bias
    return jnp.maximum(shifted, 0.0) + jnp.log1p(jnp.exp(-jnp.abs(shifted)))


def spread_heads(columns, first, width):
    rows = columns.shape[0]
    low = jnp.broadcast_to(columns[:, first : first + 1], (rows, LANES))
    if width <= HD:
        return low
    high = jnp.broadcast_to(columns[:, first + 1 : first + 2], (rows, LANES))
    return jnp.where(lane_ids(rows) < HD, low, high)


def half_mask(rows, side):
    lane = lane_ids(rows)
    return lane < HD if side == 0 else lane >= HD


def front_kernel(
    dims, place_ref, own_ref, other_ref, wbc_ref, wsp_ref, wzx_ref, wq_ref, wmix_ref, watt_ref, gain_ref, seqc_ref,
    seqr_ref, masks_ref, cos_ref, sin_ref, convx_ref, convs_ref, bias_ref, rate_ref, skip_ref,
    x_ref, act_ref, pa_ref, pb_ref, y_ref, cat_ref, part_ref, neg_ref, g_ref, xdt_ref,
):
    heads, qheads, wp, qwp, span = dims
    rows = x_ref.shape[0]
    share = own_ref.shape[0]
    if share == rows:
        x_ref[...] = own_ref[...]
    else:
        x_ref[pl.ds(pl.multiple_of(place_ref[0] * share, 16), share), :] = own_ref[...]
        x_ref[pl.ds(pl.multiple_of(place_ref[1] * share, 16), share), :] = other_ref[...]
    finish(x_ref)
    x = x_ref[...].astype(f32)
    act = (x * lax.rsqrt(jnp.mean(x * x, axis=-1, keepdims=True) + norm_eps) * gain_ref[...]).astype(bf16)
    act_ref[...] = act
    finish(act_ref)
    pb_ref[:, wp : wp + 256] = mm(act, wbc_ref[...])
    pb_ref[:, wp + 256 :] = mm(act, wsp_ref[:, :LANES])
    pb_ref[:, :wp] = mm(act, wzx_ref[:, wp:])
    pa_ref[:, wp : wp + qwp] = mm(act, wq_ref[...])
    pa_ref[:, wp + qwp :] = mm(act, wsp_ref[:, LANES:])
    pa_ref[:, :wp] = mm(act, wzx_ref[:, :wp])
    finish(pa_ref, pb_ref)
    masks = {k: masks_ref[:, k : k + 1] for k in (1, 2, 3)}
    linked = link_bias(seqc_ref[...], seqr_ref[...], False)
    neg_ref[...] = jnp.where(linked, 0.0, far)
    dt = step_parts(pb_ref[:, wp + 256 :], bias_ref[...])
    decay = mm_exact(jnp.where(linked, 1.0, 0.0), -dt * rate_ref[...])
    decay_t = decay.T
    terms = conv_terms(pb_ref[:, wp : wp + 256], masks)
    bcc = sum(t * convs_ref[k : k + 1, :] for k, t in enumerate(terms))
    bcc = (bcc * jax.nn.sigmoid(bcc)).astype(bf16)
    g_ref[...] = mm_nt(bcc[:, 128:], bcc[:, :128])

    for p in range(wp // LANES):
        cols = slice(p * LANES, (p + 1) * LANES)
        width = HD * min(2, heads - 2 * p)
        conv = sum(t * convx_ref[k : k + 1, cols] for k, t in enumerate(conv_terms(pb_ref[:, cols], masks)))
        xc = conv * jax.nn.sigmoid(conv)
        xdt_ref[...] = (xc * spread_heads(dt, 2 * p, width)).astype(bf16)
        blocks = []
        for a in range(rows // span):
            here = slice(a * span, (a + 1) * span)
            reach = (a + 1) * span
            sides = []
            for h in range(2 * p, 2 * p + width // HD):
                gap = decay[here, h : h + 1] - decay_t[h : h + 1, :reach]
                mixing = g_ref[here, :reach] * jnp.exp(gap + neg_ref[here, :reach])
                sides.append(mm(mixing.astype(bf16), xdt_ref[:reach, :]))
            blocks.append(sides[0] if len(sides) == 1 else jnp.where(half_mask(span, 0), sides[0], sides[1]))
        y = jnp.concatenate(blocks, axis=0) + skip_ref[:, cols] * xc
        y_ref[:, cols] = y
        z = pa_ref[:, cols]
        cat_ref[:, cols] = (y * (z * jax.nn.sigmoid(z))).astype(bf16)

    finish(y_ref)
    cosine, sine = cos_ref[...], sin_ref[...]
    pair = pa_ref[:, wp + qwp :]
    swapped = pltpu.roll(pair, HD, 1)
    lower = half_mask(rows, 0)
    keys = rotated(jnp.where(lower, pair, swapped), cosine, sine).astype(bf16)
    values = jnp.where(lower, swapped, pair).astype(bf16)
    for p in range(qwp // LANES):
        cols = slice(wp + p * LANES, wp + (p + 1) * LANES)
        queries = rotated(pa_ref[:, cols], cosine, sine).astype(bf16)
        for a in range(rows // span):
            here = slice(a * span, (a + 1) * span)
            reach = (a + 1) * span
            sides = []
            for side in range(min(2, qheads - 2 * p)):
                q = jnp.where(half_mask(span, side), queries[here], jnp.zeros((), bf16))
                scores = mm_nt(q, keys[:reach]) * (HD**-0.5) + neg_ref[here, :reach]
                weights = jnp.exp(scores - jnp.max(scores, axis=-1, keepdims=True))
                probs = weights / jnp.sum(weights, axis=-1, keepdims=True)
                sides.append(mm(probs.astype(bf16), values[:reach]))
            if len(sides) == 1:
                out = jnp.where(half_mask(span, 0), sides[0], 0.0)
            else:
                out = jnp.where(half_mask(span, 0), sides[0], sides[1])
            cat_ref[here, cols] = out.astype(bf16)
    finish(cat_ref)
    part_ref[...] = (mm_nt(cat_ref[:, :wp], wmix_ref[...]) + mm_nt(cat_ref[:, wp:], watt_ref[...])).astype(bf16)


def middle_kernel(
    x_ref, own_ref, other_ref, gain_ref, wgu_ref, down_ref, dhid_ref,
    h1_ref, n2_ref, hidden_ref, dgu_ref, out_ref, dn2_ref,
):
    width = down_ref.shape[1]
    h1 = x_ref[...].astype(f32) + (own_ref[...].astype(f32) + other_ref[...].astype(f32))
    h1_ref[...] = h1
    finish(h1_ref)
    n2 = (h1 * lax.rsqrt(jnp.mean(h1 * h1, axis=-1, keepdims=True) + norm_eps) * gain_ref[...]).astype(bf16)
    n2_ref[...] = n2
    finish(n2_ref)
    gate = mm(n2, wgu_ref[:, :width])
    up = mm(n2, wgu_ref[:, width:])
    sig = jax.nn.sigmoid(gate)
    silu = gate * sig
    hidden = (silu * up).astype(bf16)
    hidden_ref[...] = hidden
    finish(hidden_ref)
    dhid = dhid_ref[...].astype(f32)
    dgu_ref[:, :width] = (dhid * up * (sig * (1.0 + gate * (1.0 - sig)))).astype(bf16)
    dgu_ref[:, width:] = (dhid * silu).astype(bf16)
    finish(dgu_ref)
    dn2_ref[...] = mm_nt(dgu_ref[...], wgu_ref[...]).astype(bf16)
    finish(dn2_ref)
    out_ref[...] = mm_nt(hidden, down_ref[...]).astype(bf16)


def attend_back_kernel(
    dims, share, place_ref, own_ref, other_ref, ffn_ref, h1_ref, dout_ref, gain2_ref, wmix_ref, watt_ref, seqc_ref,
    seqr_ref, cos_ref, sin_ref, pa_ref, y_ref,
    dh1_ref, ffn_send_ref, dmix_ref, dy_ref, da_ref, gn2_ref,
    neg_ref, dh1_all_ref, datt_ref, dk_ref, dv_ref,
):
    heads, qheads, wp, qwp, span = dims
    rows = own_ref.shape[0]
    dn2 = own_ref[...].astype(f32) + other_ref[...].astype(f32)
    h1 = h1_ref[...]
    r2 = lax.rsqrt(jnp.mean(h1 * h1, axis=-1, keepdims=True) + norm_eps)
    u = dn2 * gain2_ref[...]
    dh1 = dout_ref[...].astype(f32) + r2 * u - h1 * (r2 * r2 * r2 * jnp.mean(u * h1, axis=-1, keepdims=True))
    gn2_ref[...] = jnp.sum(dn2 * h1 * r2, axis=0, keepdims=True)
    dh1_all_ref[...] = dh1
    dh1_ref[...] = dh1_all_ref[pl.ds(pl.multiple_of(place_ref[0] * share, 16), share), :]
    ffn_send_ref[...] = ffn_ref[pl.ds(pl.multiple_of(place_ref[1] * share, 16), share), :]
    dmix = dh1.astype(bf16)
    dmix_ref[...] = dmix
    finish(dh1_ref, ffn_send_ref, dmix_ref)
    datt_ref[...] = mm(dmix, watt_ref[...]).astype(bf16)
    for p in range(wp // LANES):
        cols = slice(p * LANES, (p + 1) * LANES)
        dgated = mm(dmix, wmix_ref[:, cols])
        z = pa_ref[:, cols]
        sig = jax.nn.sigmoid(z)
        dy_ref[:, cols] = dgated * (z * sig)
        da_ref[:, cols] = (dgated * y_ref[:, cols] * (sig * (1.0 + z * (1.0 - sig)))).astype(bf16)
    finish(dy_ref)

    linked_t = link_bias(seqc_ref[...], seqr_ref[...], True)
    neg_ref[...] = jnp.where(linked_t, 0.0, far)
    lower = half_mask(rows, 0)
    cosine, sine = cos_ref[...], sin_ref[...]
    pair = pa_ref[:, wp + qwp :]
    swapped = pltpu.roll(pair, HD, 1)
    keys = rotated(jnp.where(lower, pair, swapped), cosine, sine).astype(bf16)
    values = jnp.where(lower, swapped, pair).astype(bf16)
    dk_ref[...] = jnp.zeros_like(dk_ref)
    dv_ref[...] = jnp.zeros_like(dv_ref)
    for p in range(qwp // LANES):
        cols = slice(wp + p * LANES, wp + (p + 1) * LANES)
        queries = rotated(pa_ref[:, cols], cosine, sine).astype(bf16)
        datt = datt_ref[:, p * LANES : (p + 1) * LANES]
        blocks = []
        for a in range(rows // span):
            here = slice(a * span, (a + 1) * span)
            reach = (a + 1) * span
            sides = []
            for side in range(min(2, qheads - 2 * p)):
                half = half_mask(span, side)
                q = jnp.where(half, queries[here], jnp.zeros((), bf16))
                do = jnp.where(half, datt[here], jnp.zeros((), bf16))
                scores = mm_nt(keys[:reach], q) * (HD**-0.5) + neg_ref[:reach, here]
                weights = jnp.exp(scores - jnp.max(scores, axis=0, keepdims=True))
                probs = weights / jnp.sum(weights, axis=0, keepdims=True)
                dp = mm_nt(values[:reach], do)
                ds = (probs * (dp - jnp.sum(probs * dp, axis=0, keepdims=True))).astype(bf16)
                dk_ref[:reach, :] += mm(ds, q)
                dv_ref[:reach, :] += mm(probs.astype(bf16), do)
                sides.append(mm_tn(ds, keys[:reach]))
            if len(sides) == 1:
                blocks.append(jnp.where(half_mask(span, 0), sides[0], 0.0))
            else:
                blocks.append(jnp.where(half_mask(span, 0), sides[0], sides[1]))
        dq = jnp.concatenate(blocks, axis=0) * (HD**-0.5)
        da_ref[:, cols] = rotated(dq, cosine, -sine).astype(bf16)
    dk = dk_ref[...] * (HD**-0.5)
    dk = rotated(dk + pltpu.roll(dk, HD, 1), cosine, -sine)
    dv = dv_ref[...]
    dv = dv + pltpu.roll(dv, HD, 1)
    da_ref[:, wp + qwp :] = jnp.where(lower, dk, dv).astype(bf16)


def mixer_back_kernel(
    dims, share, place_ref, pb_ref, dy_ref, y_ref, wzx_ref, wbc_ref, wsp_ref, da_ref, wq_ref, x_ref, seqc_ref, seqr_ref, masks_ref,
    convx_ref, convs_ref, bias_ref, rate_ref, skip_ref, gn2_ref,
    dxb_ref, dact_ref, dact_send_ref, small_ref,
    neg_ref, gt_ref, dgt_ref, dsum_ref, ddir_ref,
):
    heads, qheads, wp, qwp, span = dims
    rows = x_ref.shape[0]
    masks = {k: masks_ref[:, k : k + 1] for k in (1, 2, 3)}
    linked_t = link_bias(seqc_ref[...], seqr_ref[...], True)
    neg_ref[...] = jnp.where(linked_t, 0.0, far)
    dt = step_parts(pb_ref[:, wp + 256 :], bias_ref[...])
    linked = link_bias(seqc_ref[...], seqr_ref[...], False)
    decay = mm_exact(jnp.where(linked, 1.0, 0.0), -dt * rate_ref[...])
    decay_t = decay.T
    state = pb_ref[:, wp : wp + 256]
    sterms = conv_terms(state, masks)
    sconv = sum(t * convs_ref[k : k + 1, :] for k, t in enumerate(sterms))
    ssig = jax.nn.sigmoid(sconv)
    bcc = (sconv * ssig).astype(bf16)
    bm, cm = bcc[:, :128], bcc[:, 128:]
    gt_ref[...] = mm_nt(bm, cm)
    small_ref[...] = jnp.zeros_like(small_ref)
    dgt_ref[...] = jnp.zeros_like(dgt_ref)
    for p in range(wp // LANES):
        cols = slice(p * LANES, (p + 1) * LANES)
        width = HD * min(2, heads - 2 * p)
        terms = conv_terms(pb_ref[:, cols], masks)
        conv = sum(t * convx_ref[k : k + 1, cols] for k, t in enumerate(terms))
        csig = jax.nn.sigmoid(conv)
        xc = conv * csig
        dt_cols = spread_heads(dt, 2 * p, width)
        xdt = (xc * dt_cols).astype(bf16)
        skip = skip_ref[:, cols]
        scanned = y_ref[:, cols] - skip * xc
        dy = dy_ref[:, cols]
        small_ref[6:7, cols] = jnp.sum(dy * xc, axis=0, keepdims=True)
        dyb = dy.astype(bf16)
        blocks = []
        for a in range(rows // span):
            here = slice(a * span, (a + 1) * span)
            sides = []
            for side in range(width // HD):
                h = 2 * p + side
                dys = jnp.where(half_mask(rows - a * span, side), dyb[a * span :], jnp.zeros((), bf16))
                gap = decay_t[h : h + 1, a * span :] - decay[here, h : h + 1]
                falloff = jnp.exp(gap + neg_ref[here, a * span :])
                mixing = (gt_ref[here, a * span :] * falloff).astype(bf16)
                sides.append(mm(mixing, dyb[a * span :]))
                dgt_ref[here, a * span :] += mm_nt(xdt[here], dys) * falloff
            blocks.append(sides[0] if len(sides) == 1 else jnp.where(half_mask(span, 0), sides[0], sides[1]))
        dxdt = jnp.concatenate(blocks, axis=0)
        dsum_ref[:, cols] = dyb.astype(f32) * scanned - xdt.astype(f32) * dxdt
        ddir_ref[:, cols] = dxdt * xc
        dconv = (dxdt * dt_cols + skip * dy) * (csig * (1.0 + conv * (1.0 - csig)))
        small_ref[2:6, cols] = jnp.concatenate([jnp.sum(t * dconv, axis=0, keepdims=True) for t in terms], axis=0)
        dxb_ref[:, cols] = conv_back(dconv, masks, convx_ref[:, cols]).astype(bf16)

    dgt = dgt_ref[...].astype(bf16)
    dbcc = jnp.concatenate([mm(dgt, cm), mm_tn(dgt, bm)], axis=1)
    dsconv = dbcc * (ssig * (1.0 + sconv * (1.0 - ssig)))
    small_ref[2:6, wp : wp + 256] = jnp.concatenate([jnp.sum(t * dsconv, axis=0, keepdims=True) for t in sterms], axis=0)
    dxb_ref[:, wp : wp + 256] = conv_back(dsconv, masks, convs_ref[...]).astype(bf16)

    head_of = lax.broadcasted_iota(jnp.int32, (wp, LANES), 0) // HD
    pick = jnp.where(head_of == lax.broadcasted_iota(jnp.int32, (wp, LANES), 1), 1.0, 0.0)
    ds = mm_exact(dsum_ref[...], pick)
    ddirect = mm_exact(ddir_ref[...], pick)
    dlog = mm_exact(jnp.where(linked_t, 1.0, 0.0), ds)
    rate = rate_ref[...]
    ddt = ddirect - rate * dlog
    dstep = ddt * jax.nn.sigmoid(pb_ref[:, wp + 256 :] + bias_ref[...])
    dstep = jnp.where(lane_ids(rows) < heads, dstep, 0.0)
    dxb_ref[:, wp + 256 :] = dstep.astype(bf16)
    small_ref[6:7, wp : wp + LANES] = jnp.sum(dstep, axis=0, keepdims=True)
    small_ref[6:7, wp + LANES : wp + 256] = -rate * jnp.sum(dt * dlog, axis=0, keepdims=True)
    finish(dxb_ref)
    dact = mm_nt(da_ref[:, :wp], wzx_ref[:, :wp]) + mm_nt(dxb_ref[:, :wp], wzx_ref[:, wp:])
    dact = dact + mm_nt(dxb_ref[:, wp : wp + 256], wbc_ref[...]) + mm_nt(da_ref[:, wp : wp + qwp], wq_ref[...])
    dact = dact + mm_nt(dxb_ref[:, wp + 256 :], wsp_ref[:, :LANES]) + mm_nt(da_ref[:, wp + qwp :], wsp_ref[:, LANES:])
    dact_ref[...] = dact.astype(bf16)
    finish(dact_ref)
    dact_send_ref[...] = dact_ref[pl.ds(pl.multiple_of(place_ref[1] * share, 16), share), :]
    finish(dact_send_ref)
    x = x_ref[...].astype(f32)
    r1 = lax.rsqrt(jnp.mean(x * x, axis=-1, keepdims=True) + norm_eps)
    small_ref[0:1, :] = jnp.sum(dact * x * r1, axis=0, keepdims=True)
    small_ref[1:2, :] = gn2_ref[...] * (share / rows)


def pieces_of(width, most):
    groups = width // LANES
    count = -(-groups // (most // LANES))
    edges = [(i * groups // count) * LANES for i in range(count + 1)]
    return list(zip(edges[:-1], edges[1:]))


def grad_kernel(cuts, pieces, block, bit_ref, *refs):
    pairs = len(cuts)
    ins, refs = refs[: 2 * pairs], refs[2 * pairs :]
    sents, kepts, refs = refs[: len(pieces)], refs[len(pieces) : 2 * len(pieces)], refs[2 * len(pieces) :]
    buffers, refs = refs[: 2 * pairs], refs[2 * pairs :]
    turned, stage, in_sems, sent_sems, kept_sems = refs
    fetched = [Fetched(ins[i], buffers[i], in_sems.at[i]) for i in range(2 * pairs)]
    bit = bit_ref[0]
    count = turned.shape[0] // (2 * block)
    copies, at, sent_to = [], 0, 0
    for k, (low, high) in enumerate(cuts):
        turned[...] = fetched[2 * k][...].astype(f32).T.astype(bf16)
        for start in range(low, high, 512):
            stop = min(start + 512, high)
            full = mm(turned[...], fetched[2 * k + 1][:, start:stop]).astype(bf16)
            for j in range(2 * count):
                side = 1 - bit if j % 2 == 0 else bit
                stage[side, (j // 2) * block : (j // 2 + 1) * block, at : at + stop - start] = full[j * block : (j + 1) * block]
            at += stop - start
            while sent_to < len(pieces) and pieces[sent_to][1] <= at:
                cols = pl.ds(pieces[sent_to][0], pieces[sent_to][1] - pieces[sent_to][0])
                copies.append(pltpu.make_async_copy(stage.at[0, :, cols], sents[sent_to], sent_sems.at[sent_to]))
                copies.append(pltpu.make_async_copy(stage.at[1, :, cols], kepts[sent_to], kept_sems.at[sent_to]))
                copies[-2].start()
                copies[-1].start()
                sent_to += 1
    for copy in copies:
        copy.wait()


def plain_params(flops=1000):
    return dict(
        compiler_params=pltpu.CompilerParams(vmem_limit_bytes=63 * 1024 * 1024),
        cost_estimate=pl.CostEstimate(flops=flops, bytes_accessed=1000, transcendentals=0),
    )


def weight_halves(pairs, bit, block, most, after=()):
    args = [a for left, right, _, _ in pairs for a in (left, right)]
    cuts = [(low, high) for _, _, low, high in pairs]
    rows, model = pairs[0][0].shape
    width = sum(high - low for low, high in cuts)
    pieces = pieces_of(width, most)
    outs = [(model // 2, high - low) for low, high in pieces] * 2

    def wrapped(bit_ref, *refs):
        grad_kernel(cuts, pieces, block, bit_ref, *refs[: len(args)], *refs[len(args) + len(after) :])

    outs = pl.pallas_call(
        wrapped,
        out_shape=[jax.ShapeDtypeStruct(s, bf16) for s in outs],
        in_specs=[pl.BlockSpec(memory_space=pltpu.SMEM)] + [pl.BlockSpec(memory_space=pltpu.HBM)] * (len(args) + len(after)),
        out_specs=[pl.BlockSpec(memory_space=pltpu.HBM)] * len(outs),
        scratch_shapes=[pltpu.VMEM(a.shape, a.dtype) for a in args]
        + [
            pltpu.VMEM((model, rows), bf16), pltpu.VMEM((2, model // 2, width), bf16),
            pltpu.SemaphoreType.DMA((len(args),)), pltpu.SemaphoreType.DMA((len(pieces),)),
            pltpu.SemaphoreType.DMA((len(pieces),)),
        ],
        **plain_params(),
    )(bit, *args, *after)
    return outs[: len(pieces)], outs[len(pieces) :]


def step_kernel(pieces, sources, block, small, which_ref, *refs):
    arrays, refs = refs[: 2 * sources], refs[2 * sources :]
    if small:
        small_own, small_other, refs = refs[0], refs[1], refs[2:]
    away, mine, refs = refs[0], refs[1], refs[2:]
    if small:
        small_ref, refs = refs[0], refs[1:]
    kept_buf, arrived_buf, away_buf, mine_buf, kept_sems, arrived_sems, away_sems, mine_sems = refs
    which = which_ref[0]
    ins, outs = [], []
    for k, (source, low, at, width) in enumerate(pieces):
        cols, here = pl.ds(low, width), pl.ds(at, width)
        ins.append(pltpu.make_async_copy(arrays[2 * source].at[:, cols], kept_buf.at[:, here], kept_sems.at[k]))
        ins.append(pltpu.make_async_copy(arrays[2 * source + 1].at[:, cols], arrived_buf.at[:, here], arrived_sems.at[k]))
        ins[-2].start()
        ins[-1].start()
    if small:
        small_ref[...] = small_own[...] + small_other[...]
    for k, (source, low, at, width) in enumerate(pieces):
        ins[2 * k].wait()
        ins[2 * k + 1].wait()
        here = pl.ds(at, width)
        for out, target, sems, side in ((away_buf, away, away_sems, 1 - which), (mine_buf, mine, mine_sems, which)):
            for i in range(kept_buf.shape[0] // (2 * block)):
                rows = pl.ds(pl.multiple_of((2 * i + side) * block, block), block)
                total = kept_buf[rows, at : at + width].astype(f32) + arrived_buf[rows, at : at + width].astype(f32)
                out[i * block : (i + 1) * block, at : at + width] = total.astype(bf16)
            outs.append(pltpu.make_async_copy(out.at[:, here], target.at[:, here], sems.at[k]))
            outs[-1].start()
    for copy in outs:
        copy.wait()


def step_call(which, sources, block, after, small=()):
    rows = sources[0][0].shape[0]
    pieces, at = [], 0
    for i, (kept, _) in enumerate(sources):
        for low, high in pieces_of(kept.shape[1], 512):
            pieces.append((i, low, at + low, high - low))
        at += kept.shape[1]
    args = [a for pair in sources for a in pair]

    def wrapped(which_ref, *refs):
        used = len(args) + len(small)
        step_kernel(pieces, len(sources), block, bool(small), which_ref, *refs[:used], *refs[used + len(after) :])

    half = (rows // 2, at)
    anywhere = pl.BlockSpec(memory_space=pltpu.HBM)
    inside = pl.BlockSpec(memory_space=pltpu.VMEM)
    return pl.pallas_call(
        wrapped,
        out_shape=[jax.ShapeDtypeStruct(half, bf16)] * 2 + [jax.ShapeDtypeStruct(a.shape, f32) for a in small[:1]],
        in_specs=[pl.BlockSpec(memory_space=pltpu.SMEM)] + [anywhere] * len(args) + [inside] * len(small)
        + [anywhere] * len(after),
        out_specs=[anywhere] * 2 + [inside] * len(small[:1]),
        scratch_shapes=[pltpu.VMEM((rows, at), bf16)] * 2
        + [pltpu.VMEM(half, bf16)] * 2
        + [pltpu.SemaphoreType.DMA((len(pieces),))] * 4,
        **plain_params(),
    )(which, *args, *small, *after)


class Fetched:
    def __init__(self, source, held, sem):
        self.held, self.copy, self.ready = held, pltpu.make_async_copy(source, held, sem), False
        self.shape, self.dtype = held.shape, held.dtype
        self.copy.start()

    def __getitem__(self, key):
        if not self.ready:
            self.copy.wait()
            self.ready = True
        return self.held[key]


class Stored:
    def __init__(self, held, target, sem):
        self.held, self.copy, self.sent = held, pltpu.make_async_copy(held, target, sem), False
        self.shape, self.dtype = held.shape, held.dtype

    def __getitem__(self, key):
        return self.held[key]

    def __setitem__(self, key, value):
        self.held[key] = value

    def finish(self):
        if not self.sent:
            self.copy.start()
            self.sent = True


LARGE = 1 << 16
COST_US = 1100000000


def finish(*refs):
    for ref in refs:
        if isinstance(ref, Stored):
            ref.finish()


def call(kernel, outs, scratch, args, scalars=0, after=(), flops=1000):
    count = len(args)
    large_in = [i >= scalars and a.size * a.dtype.itemsize >= LARGE for i, a in enumerate(args)]
    large_out = [s[0] * s[1] * jnp.dtype(t).itemsize >= LARGE for s, t in outs]
    buffers = [pltpu.VMEM(a.shape, a.dtype) for a, big in zip(args, large_in) if big]
    buffers += [pltpu.VMEM(s, t) for (s, t), big in zip(outs, large_out) if big]
    copies = len(buffers)

    def wrapped(*refs):
        ins, rest = list(refs[:count]), refs[count + len(after) :]
        results, rest = list(rest[: len(outs)]), rest[len(outs) :]
        held, sems, inner = rest[:copies], rest[copies], rest[copies + 1 :]
        slot = 0
        for i, big in enumerate(large_in):
            if big:
                ins[i] = Fetched(ins[i], held[slot], sems.at[slot])
                slot += 1
        for i, big in enumerate(large_out):
            if big:
                results[i] = Stored(held[slot], results[i], sems.at[slot])
                slot += 1
        kernel(*ins, *results, *inner)
        finish(*results)
        for ref in ins:
            if isinstance(ref, Fetched) and not ref.ready:
                ref.copy.wait()
        for ref in results:
            if isinstance(ref, Stored):
                ref.copy.wait()

    spaces = [pltpu.SMEM] * scalars + [pltpu.HBM if big else pltpu.VMEM for big in large_in[scalars:]] + [pltpu.HBM] * len(after)
    return pl.pallas_call(
        wrapped,
        out_shape=[jax.ShapeDtypeStruct(s, t) for s, t in outs],
        in_specs=[pl.BlockSpec(memory_space=space) for space in spaces],
        out_specs=[pl.BlockSpec(memory_space=pltpu.HBM if big else pltpu.VMEM) for big in large_out],
        scratch_shapes=buffers + [pltpu.SemaphoreType.DMA((max(copies, 1),))] + [pltpu.VMEM(s, t) for s, t in scratch],
        **plain_params(flops),
    )(*args, *after)


def swap(values):
    return lax.ppermute(values, "tensor", [(0, 1), (1, 0)])


def gather_rows(values, me, count):
    if count != 2:
        return lax.all_gather(values, "tensor", axis=0, tiled=True)
    other = swap(values)
    first = jnp.where(me == 0, values, other)
    return jnp.concatenate([first, jnp.where(me == 0, other, values)], axis=0)


def both_parts(part, count):
    if count != 2:
        return (lax.psum(part, "tensor"), jnp.zeros_like(part))
    return (part, swap(part))


def scatter_rows(part, me, count):
    if count != 2:
        return lax.psum_scatter(part, "tensor", scatter_dimension=0, tiled=True).astype(f32)
    halves = part.reshape(2, part.shape[0] // 2, part.shape[1])
    arrived = swap(lax.dynamic_index_in_dim(halves, 1 - me, 0, keepdims=False))
    return lax.dynamic_index_in_dim(halves, me, 0, keepdims=False).astype(f32) + arrived.astype(f32)


def partners(count, bit):
    return [(i, i ^ bit) for i in range(count)]


def exchange(sent, count, bit):
    return lax.ppermute(sent, "dp", partners(count, bit))


class Reduction:
    def __init__(self, parts, index, count, block, bit=1, small=None):
        self.parts, self.index, self.count, self.block, self.bit = parts, index, count, block, bit
        self.small = small
        self.small_arrived = None if small is None else exchange(small, count, bit)

    def done(self):
        return self.bit * 2 >= self.count

    def step(self, after=()):
        if self.done():
            return after
        self.bit *= 2
        which = ((self.index // self.bit) % 2).astype(jnp.int32).reshape(1)
        small = () if self.small is None else (self.small, self.small_arrived)
        sent, kept, *small = step_call(which, self.parts, self.block, after, small)
        self.parts = [(kept, exchange(sent, self.count, self.bit))]
        if small:
            self.small = small[0]
            self.small_arrived = exchange(self.small, self.count, self.bit)
        return (sent,)

    def total(self, after):
        kept, arrived = self.parts[0]
        if self.bit > 1:
            arrived = lax.optimization_barrier((arrived, after[0]))[0]
        return kept.astype(f32) + arrived.astype(f32)


def segments(lengths, row_count):
    seq_ends = jnp.cumsum(lengths)
    places = jnp.arange(row_count, dtype=jnp.int32)
    passed = places[:, None] >= seq_ends[None, :]
    seq_ids = jnp.sum(passed.astype(jnp.int32), axis=1)
    starts = jnp.max(jnp.where(passed, seq_ends[None, :], 0), axis=1)
    is_live = (places < seq_ends[-1]).astype(f32)
    return (seq_ids, places - starts, is_live)


def body(
    dp_count, tensor_count, tokens, cotangent, seq_lengths, norm1_gain, norm2_gain, mixer_in, state_in, step_in,
    conv_inner, conv_state, step_bias, decay_log, skip_gain, mixer_out, query_in, key_value, attend_out, gate_up,
    down_out,
):
    share, model = tokens.shape
    rows = share * tensor_count
    me = lax.axis_index("tensor")
    index = lax.axis_index("dp")
    inner = mixer_in.shape[2]
    heads = step_in.shape[1]
    query_width = query_in.shape[1]
    qheads = query_width // HD
    wp, qwp = padded(inner), padded(query_width)
    span = min(LANES, rows)
    dims = (heads, qheads, wp, qwp, span)

    if tensor_count == 2:
        x_own, x_other = tokens, swap(tokens)
    else:
        x_own = x_other = gather_rows(tokens, me, tensor_count)
    place = jnp.stack([me, lax.rem(me + 1, tensor_count)]).astype(jnp.int32)
    seq_ids, positions, is_live = segments(seq_lengths[0], rows)
    live_share = lax.dynamic_slice_in_dim(is_live, me * share, share, 0)[:, None]
    dout_rows = gather_rows(lax.optimization_barrier((cotangent, x_other))[0], me, tensor_count)
    dout_rows = dout_rows * is_live[:, None].astype(bf16)

    seq_col = seq_ids.astype(f32)[:, None]
    seq_row = seq_ids.astype(f32)[None, :]
    shifts = jnp.minimum(jnp.arange(LANES, dtype=jnp.int32), 4)[None, :]
    masks = (positions[:, None] >= shifts).astype(f32)
    lane = jnp.arange(LANES)
    frequency = rope_base ** (-2.0 * (lane % (HD // 2)).astype(f32) / HD)
    angles = positions.astype(f32)[:, None] * frequency[None, :]
    cosine = jnp.cos(angles)
    sine = jnp.sin(angles) * jnp.where(lane % HD < HD // 2, -1.0, 1.0)[None, :]

    key_index = me * qheads // (QH // KVH)
    pair_local = lax.dynamic_slice_in_dim(key_value, key_index * HD, HD, 2).reshape(model, 2 * HD)
    if inner == wp:
        wzx = mixer_in.reshape(model, 2 * inner)
    else:
        wzx = pad_to(mixer_in, wp).reshape(model, 2 * wp)
    wsp = jnp.concatenate([pad_to(step_in, LANES), pair_local], axis=1)
    wq, wmix, watt = pad_to(query_in, qwp), pad_to(mixer_out, wp), pad_to(attend_out, qwp)
    taps = pad_to(conv_inner, wp)
    bias = pad_to(step_bias[None], LANES)
    rate = pad_to(jnp.exp(decay_log)[None], LANES)
    skip = pad_to(jnp.repeat(skip_gain, HD)[None], wp)
    gain1, gain2 = norm1_gain[None], norm2_gain[None]

    x_rows, act, pa, pb, y, cat, part = call(
        functools.partial(front_kernel, dims),
        [
            ((rows, model), bf16), ((rows, model), bf16), ((rows, wp + qwp + LANES), f32), ((rows, wp + 384), f32),
            ((rows, wp), f32), ((rows, wp + qwp), bf16), ((rows, model), bf16),
        ],
        [((rows, rows), f32), ((rows, rows), f32), ((rows, LANES), bf16)],
        (
            place, x_own, x_other, state_in, wsp, wzx, wq, wmix, watt, gain1, seq_col, seq_row, masks, cosine, sine, taps,
            conv_state, bias, rate, skip,
        ),
        1, (), 10 * COST_US,
    )
    own, other = both_parts(part, tensor_count)
    wgu = lax.optimization_barrier((gate_up, part))[0].reshape(model, -1)
    dhidden = mm(dout_rows, down_out)
    ff2 = wgu.shape[1]
    h1, n2, hidden, dgu, ffn_part, dn2_part = call(
        middle_kernel,
        [
            ((rows, model), f32), ((rows, model), bf16), ((rows, ff2 // 2), bf16), ((rows, ff2), bf16),
            ((rows, model), bf16), ((rows, model), bf16),
        ],
        [],
        (x_rows, own, other, gain2, wgu, down_out, dhidden),
    )
    dn2_own, dn2_other = both_parts(dn2_part, tensor_count)

    bit = (index % 2).astype(jnp.int32).reshape(1)
    block = model // dp_count

    def reduction(pairs, most, after=(), small=None):
        sent, kept = weight_halves(pairs, bit, block, most, after)
        parts = [(stay, exchange(go, dp_count, 1)) for go, stay in zip(sent, kept)]
        return Reduction(parts, index, dp_count, block, 1, small)

    most = max(LANES, ff2 * 5 // 16 // LANES * LANES)
    cut = ff2 - ff2 // 4
    ffn_a = reduction([(dout_rows, hidden, 0, most)], most)
    ffn_b = reduction([(dout_rows, hidden, most, ff2 // 2), (n2, dgu, 0, cut)], most, (ffn_a.parts[0][0],))
    order = ffn_a.step((ffn_b.parts[0][0],))
    order = ffn_b.step(order)

    dh1_share, ffn_send, dmix, dy, da, gn2 = call(
        functools.partial(attend_back_kernel, dims, share),
        [
            ((share, model), f32), ((share, model), bf16), ((rows, model), bf16), ((rows, wp), f32),
            ((rows, wp + qwp + LANES), bf16), ((1, model), f32),
        ],
        [((rows, rows), f32), ((rows, model), f32), ((rows, qwp), bf16), ((rows, LANES), f32), ((rows, LANES), f32)],
        (
            place, dn2_own, dn2_other, ffn_part, h1, dout_rows, gain2, wmix, watt, seq_col, seq_row, cosine, sine, pa, y,
        ),
        1, order, 40 * COST_US,
    )
    order = ffn_a.step((dmix,))
    mix_out = reduction([(dmix, cat, 0, wp + qwp), (n2, dgu, cut, ff2)], 512, order)
    mix_a = reduction([(act, da, 0, wp + qwp + LANES)], 2048, (mix_out.parts[0][0],))
    order = ffn_a.step((mix_a.parts[0][0],))
    order = ffn_b.step(order)
    order = mix_out.step(order)
    ffn_arrived = swap(ffn_send) if tensor_count == 2 else ffn_send

    dxb, dact, dact_send, small = call(
        functools.partial(mixer_back_kernel, dims, share),
        [((rows, wp + 384), bf16), ((rows, model), bf16), ((share, model), bf16), ((8, model), f32)],
        [
            ((rows, rows), f32), ((rows, rows), f32), ((rows, rows), f32), ((rows, wp), f32), ((rows, wp), f32),
        ],
        (
            place, pb, dy, y, wzx, state_in, wsp, da, wq, x_rows, seq_col, seq_row, masks, taps, conv_state, bias, rate,
            skip, gn2,
        ),
        1, order + (ffn_arrived,), 40 * COST_US,
    )
    mix_b = reduction([(act, dxb, 0, wp + 384)], 384, (), small)
    order = mix_a.step((mix_b.parts[0][0],))
    order = ffn_b.step(order)
    order = mix_out.step(order)
    order = mix_b.step(order)
    ffn_b_total = ffn_b.total(order) if ffn_b.done() else None
    order = mix_a.step(order if ffn_b_total is None else order + (ffn_b_total,))
    order = mix_out.step(order)
    if tensor_count == 2:
        dact_mine = lax.dynamic_slice_in_dim(dact, me * share, share, 0).astype(f32)
        dact_share = dact_mine + lax.optimization_barrier((swap(dact_send), order[0]))[0].astype(f32)
    else:
        dact_share = scatter_rows(dact, me, tensor_count)
    for r in [mix_b, mix_a] + 4 * [ffn_a, ffn_b, mix_out, mix_a, mix_b]:
        order = r.step(order)
    ffn_b = ffn_b.total(order) if ffn_b_total is None else ffn_b_total
    ffn_a, out_total, first_total = (r.total(order) for r in (ffn_a, mix_out, mix_a))
    rest = ff2 // 2 - most
    down_total = jnp.concatenate([ffn_a, ffn_b[:, :rest]], axis=1)
    up_total = jnp.concatenate([ffn_b[:, rest:], out_total[:, wp + qwp :]], axis=1)
    mix_b, minor = mix_b.total(order), mix_b.small + mix_b.small_arrived
    second_total, state_total = mix_b[:, :wp], mix_b[:, wp : wp + 256]
    step_total = mix_b[:, wp + 256 :]

    if tensor_count == 2:
        ffn_mine = lax.dynamic_slice_in_dim(ffn_part, me * share, share, 0).astype(f32)
        ffn_share = ffn_mine + ffn_arrived.astype(f32)
    else:
        ffn_share = scatter_rows(ffn_part, me, tensor_count)
    h1_share = lax.dynamic_slice_in_dim(h1, me * share, share, 0)
    block_out = ((h1_share + ffn_share) * live_share).astype(bf16)

    x_share = tokens.astype(f32)
    r1 = lax.rsqrt(jnp.mean(x_share * x_share, axis=-1, keepdims=True) + norm_eps)
    u = dact_share * gain1
    token_grad = dh1_share + r1 * u - x_share * (r1 * r1 * r1 * jnp.mean(u * x_share, axis=-1, keepdims=True))

    shared = minor + swap(minor) if tensor_count == 2 else lax.psum(minor, "tensor")
    g_norm1, g_norm2, g_conv_state = shared[0], shared[1], shared[2:6, wp : wp + 256]
    g_conv_inner = minor[2:6, :inner]
    g_skip = jnp.sum(minor[6, :wp].reshape(-1, HD), axis=1)[:heads]
    g_bias = minor[6, wp : wp + heads]
    g_decay = minor[6, wp + LANES : wp + LANES + heads]

    both = jnp.concatenate([state_total, first_total[:, wp + qwp :]], axis=1).astype(bf16)
    placed = lambda pair: lax.dynamic_update_slice_in_dim(
        jnp.zeros((block,) + key_value.shape[1:], f32), pair.astype(f32).reshape(block, 2, HD), key_index * HD, 2
    )
    if tensor_count == 2:
        arrived = swap(both)
        g_state = both[:, :256].astype(f32) + arrived[:, :256].astype(f32)
        mine = both[:, 256:].reshape(block, 2, HD)
        theirs = arrived[:, 256:].reshape(block, 2, HD)
        g_pair = jnp.concatenate(
            [jnp.where(me == 0, mine, theirs), jnp.where(me == 0, theirs, mine)], axis=2
        ).astype(f32)
    else:
        g_state = lax.psum(both[:, :256], "tensor").astype(f32)
        g_pair = lax.psum(placed(both[:, 256:]).astype(bf16), "tensor").astype(f32)

    g_mixer_in = jnp.stack([first_total[:, :inner], second_total[:, :inner]], axis=1)
    return (
        block_out,
        token_grad.astype(bf16),
        g_norm1,
        g_norm2,
        g_mixer_in,
        g_state,
        step_total[:, :heads],
        g_conv_inner,
        g_conv_state,
        g_bias,
        g_decay,
        g_skip,
        out_total[:, :inner],
        first_total[:, wp : wp + query_width],
        g_pair,
        out_total[:, wp : wp + query_width],
        up_total.reshape(block, 2, ff2 // 2),
        down_total,
    )


def solution(mesh):
    return jax.shard_map(
        functools.partial(body, mesh.shape["dp"], mesh.shape["tensor"]),
        mesh=mesh,
        in_specs=(
            P(("dp", "tensor"), None),
            P(("dp", "tensor"), None),
            P("dp", None),
            P(),
            P(),
            P(None, None, "tensor"),
            P(),
            P(None, "tensor"),
            P(None, "tensor"),
            P(),
            P("tensor"),
            P("tensor"),
            P("tensor"),
            P(None, "tensor"),
            P(None, "tensor"),
            P(),
            P(None, "tensor"),
            P(None, None, "tensor"),
            P(None, "tensor"),
        ),
        out_specs=(
            P(("dp", "tensor"), None),
            P(("dp", "tensor"), None),
            P(),
            P(),
            P("dp", None, "tensor"),
            P("dp", None),
            P("dp", "tensor"),
            P(None, "tensor"),
            P(),
            P("tensor"),
            P("tensor"),
            P("tensor"),
            P("dp", "tensor"),
            P("dp", "tensor"),
            P("dp", None, None),
            P("dp", "tensor"),
            P("dp", None, "tensor"),
            P("dp", "tensor"),
        ),
        check_vma=False,
    )
```

```python
import functools

import jax
import jax.numpy as jnp
from jax import lax
from jax.experimental import pallas as pl
from jax.experimental.pallas import tpu as pltpu
from jax.sharding import PartitionSpec as P

HD = 64
QH = 8
KVH = 2
LANES = 128

rope_base = 100000000000.0
norm_eps = 1e-05
far = -1e30
highest = lax.Precision.HIGHEST
f32 = jnp.float32
bf16 = jnp.bfloat16


def padded(width):
    return -(-width // LANES) * LANES


def pad_to(values, width):
    return jnp.pad(values, [(0, 0)] * (values.ndim - 1) + [(0, width - values.shape[-1])])


def mm(left, right):
    return jnp.dot(left, right, preferred_element_type=f32)


def mm_nt(left, right):
    return lax.dot_general(left, right, (((1,), (1,)), ((), ())), preferred_element_type=f32)


def mm_tn(left, right):
    return lax.dot_general(left, right, (((0,), (0,)), ((), ())), preferred_element_type=f32)


def mm_exact(left, right):
    return jnp.dot(left, right, preferred_element_type=f32, precision=highest)


def lane_ids(rows):
    return lax.broadcasted_iota(jnp.int32, (rows, LANES), 1)


def partner_half(values):
    lane = lane_ids(values.shape[0])
    return jnp.where(lane % HD < HD // 2, pltpu.roll(values, LANES - HD // 2, 1), pltpu.roll(values, HD // 2, 1))


def rotated(values, cosine, signed_sine):
    return values * cosine + partner_half(values) * signed_sine


def conv_terms(values, masks):
    return [pltpu.roll(values, offset, 0) * masks[offset] for offset in (3, 2, 1)] + [values]


def conv_back(grad, masks, taps):
    rows = grad.shape[0]
    total = grad * taps[3:4]
    for offset in (1, 2, 3):
        total = total + pltpu.roll(grad * masks[offset], rows - offset, 0) * taps[3 - offset : 4 - offset]
    return total


def link_bias(seq_col, seq_row, transposed):
    rows = seq_col.shape[0]
    down = lax.broadcasted_iota(jnp.int32, (rows, rows), 0)
    across = lax.broadcasted_iota(jnp.int32, (rows, rows), 1)
    ordered = down <= across if transposed else down >= across
    return (seq_col == seq_row) & ordered


def step_parts(raw, bias):
    shifted = raw + bias
    return jnp.maximum(shifted, 0.0) + jnp.log1p(jnp.exp(-jnp.abs(shifted)))


def spread_heads(columns, first, width):
    rows = columns.shape[0]
    low = jnp.broadcast_to(columns[:, first : first + 1], (rows, LANES))
    if width <= HD:
        return low
    high = jnp.broadcast_to(columns[:, first + 1 : first + 2], (rows, LANES))
    return jnp.where(lane_ids(rows) < HD, low, high)


def half_mask(rows, side):
    lane = lane_ids(rows)
    return lane < HD if side == 0 else lane >= HD


def front_kernel(
    dims, place_ref, own_ref, other_ref, wbc_ref, wsp_ref, wzx_ref, wq_ref, wmix_ref, watt_ref, gain_ref, seqc_ref,
    seqr_ref, masks_ref, cos_ref, sin_ref, convx_ref, convs_ref, bias_ref, rate_ref, skip_ref,
    x_ref, act_ref, pa_ref, pb_ref, y_ref, cat_ref, part_ref, neg_ref, g_ref, xdt_ref,
):
    heads, qheads, wp, qwp, span = dims
    rows = x_ref.shape[0]
    share = own_ref.shape[0]
    if share == rows:
        x_ref[...] = own_ref[...]
    else:
        x_ref[pl.ds(pl.multiple_of(place_ref[0] * share, 16), share), :] = own_ref[...]
        x_ref[pl.ds(pl.multiple_of(place_ref[1] * share, 16), share), :] = other_ref[...]
    finish(x_ref)
    x = x_ref[...].astype(f32)
    act = (x * lax.rsqrt(jnp.mean(x * x, axis=-1, keepdims=True) + norm_eps) * gain_ref[...]).astype(bf16)
    act_ref[...] = act
    finish(act_ref)
    pb_ref[:, wp : wp + 256] = mm(act, wbc_ref[...])
    pb_ref[:, wp + 256 :] = mm(act, wsp_ref[:, :LANES])
    pb_ref[:, :wp] = mm(act, wzx_ref[:, wp:])
    pa_ref[:, wp : wp + qwp] = mm(act, wq_ref[...])
    pa_ref[:, wp + qwp :] = mm(act, wsp_ref[:, LANES:])
    pa_ref[:, :wp] = mm(act, wzx_ref[:, :wp])
    finish(pa_ref, pb_ref)
    masks = {k: masks_ref[:, k : k + 1] for k in (1, 2, 3)}
    linked = link_bias(seqc_ref[...], seqr_ref[...], False)
    neg_ref[...] = jnp.where(linked, 0.0, far)
    dt = step_parts(pb_ref[:, wp + 256 :], bias_ref[...])
    decay = mm_exact(jnp.where(linked, 1.0, 0.0), -dt * rate_ref[...])
    decay_t = decay.T
    terms = conv_terms(pb_ref[:, wp : wp + 256], masks)
    bcc = sum(t * convs_ref[k : k + 1, :] for k, t in enumerate(terms))
    bcc = (bcc * jax.nn.sigmoid(bcc)).astype(bf16)
    g_ref[...] = mm_nt(bcc[:, 128:], bcc[:, :128])

    for p in range(wp // LANES):
        cols = slice(p * LANES, (p + 1) * LANES)
        width = HD * min(2, heads - 2 * p)
        conv = sum(t * convx_ref[k : k + 1, cols] for k, t in enumerate(conv_terms(pb_ref[:, cols], masks)))
        xc = conv * jax.nn.sigmoid(conv)
        xdt_ref[...] = (xc * spread_heads(dt, 2 * p, width)).astype(bf16)
        blocks = []
        for a in range(rows // span):
            here = slice(a * span, (a + 1) * span)
            reach = (a + 1) * span
            sides = []
            for h in range(2 * p, 2 * p + width // HD):
                gap = decay[here, h : h + 1] - decay_t[h : h + 1, :reach]
                mixing = g_ref[here, :reach] * jnp.exp(gap + neg_ref[here, :reach])
                sides.append(mm(mixing.astype(bf16), xdt_ref[:reach, :]))
            blocks.append(sides[0] if len(sides) == 1 else jnp.where(half_mask(span, 0), sides[0], sides[1]))
        y = jnp.concatenate(blocks, axis=0) + skip_ref[:, cols] * xc
        y_ref[:, cols] = y
        z = pa_ref[:, cols]
        cat_ref[:, cols] = (y * (z * jax.nn.sigmoid(z))).astype(bf16)

    finish(y_ref)
    cosine, sine = cos_ref[...], sin_ref[...]
    pair = pa_ref[:, wp + qwp :]
    swapped = pltpu.roll(pair, HD, 1)
    lower = half_mask(rows, 0)
    keys = rotated(jnp.where(lower, pair, swapped), cosine, sine).astype(bf16)
    values = jnp.where(lower, swapped, pair).astype(bf16)
    for p in range(qwp // LANES):
        cols = slice(wp + p * LANES, wp + (p + 1) * LANES)
        queries = rotated(pa_ref[:, cols], cosine, sine).astype(bf16)
        for a in range(rows // span):
            here = slice(a * span, (a + 1) * span)
            reach = (a + 1) * span
            sides = []
            for side in range(min(2, qheads - 2 * p)):
                q = jnp.where(half_mask(span, side), queries[here], jnp.zeros((), bf16))
                scores = mm_nt(q, keys[:reach]) * (HD**-0.5) + neg_ref[here, :reach]
                weights = jnp.exp(scores - jnp.max(scores, axis=-1, keepdims=True))
                probs = weights / jnp.sum(weights, axis=-1, keepdims=True)
                sides.append(mm(probs.astype(bf16), values[:reach]))
            if len(sides) == 1:
                out = jnp.where(half_mask(span, 0), sides[0], 0.0)
            else:
                out = jnp.where(half_mask(span, 0), sides[0], sides[1])
            cat_ref[here, cols] = out.astype(bf16)
    finish(cat_ref)
    part_ref[...] = (mm_nt(cat_ref[:, :wp], wmix_ref[...]) + mm_nt(cat_ref[:, wp:], watt_ref[...])).astype(bf16)


def middle_kernel(
    x_ref, own_ref, other_ref, gain_ref, wgu_ref, down_ref, dhid_ref,
    h1_ref, n2_ref, hidden_ref, dgu_ref, out_ref, dn2_ref,
):
    width = down_ref.shape[1]
    h1 = x_ref[...].astype(f32) + (own_ref[...].astype(f32) + other_ref[...].astype(f32))
    h1_ref[...] = h1
    finish(h1_ref)
    n2 = (h1 * lax.rsqrt(jnp.mean(h1 * h1, axis=-1, keepdims=True) + norm_eps) * gain_ref[...]).astype(bf16)
    n2_ref[...] = n2
    finish(n2_ref)
    gate = mm(n2, wgu_ref[:, :width])
    up = mm(n2, wgu_ref[:, width:])
    sig = jax.nn.sigmoid(gate)
    silu = gate * sig
    hidden = (silu * up).astype(bf16)
    hidden_ref[...] = hidden
    finish(hidden_ref)
    dhid = dhid_ref[...].astype(f32)
    dgu_ref[:, :width] = (dhid * up * (sig * (1.0 + gate * (1.0 - sig)))).astype(bf16)
    dgu_ref[:, width:] = (dhid * silu).astype(bf16)
    finish(dgu_ref)
    dn2_ref[...] = mm_nt(dgu_ref[...], wgu_ref[...]).astype(bf16)
    finish(dn2_ref)
    out_ref[...] = mm_nt(hidden, down_ref[...]).astype(bf16)


def attend_back_kernel(
    dims, share, place_ref, own_ref, other_ref, ffn_ref, h1_ref, dout_ref, gain2_ref, wmix_ref, watt_ref, seqc_ref,
    seqr_ref, cos_ref, sin_ref, pa_ref, y_ref,
    dh1_ref, ffn_send_ref, dmix_ref, dy_ref, da_ref, gn2_ref,
    neg_ref, dh1_all_ref, datt_ref, dk_ref, dv_ref,
):
    heads, qheads, wp, qwp, span = dims
    rows = own_ref.shape[0]
    dn2 = own_ref[...].astype(f32) + other_ref[...].astype(f32)
    h1 = h1_ref[...]
    r2 = lax.rsqrt(jnp.mean(h1 * h1, axis=-1, keepdims=True) + norm_eps)
    u = dn2 * gain2_ref[...]
    dh1 = dout_ref[...].astype(f32) + r2 * u - h1 * (r2 * r2 * r2 * jnp.mean(u * h1, axis=-1, keepdims=True))
    gn2_ref[...] = jnp.sum(dn2 * h1 * r2, axis=0, keepdims=True)
    dh1_all_ref[...] = dh1
    dh1_ref[...] = dh1_all_ref[pl.ds(pl.multiple_of(place_ref[0] * share, 16), share), :]
    ffn_send_ref[...] = ffn_ref[pl.ds(pl.multiple_of(place_ref[1] * share, 16), share), :]
    dmix = dh1.astype(bf16)
    dmix_ref[...] = dmix
    finish(dh1_ref, ffn_send_ref, dmix_ref)
    datt_ref[...] = mm(dmix, watt_ref[...]).astype(bf16)
    for p in range(wp // LANES):
        cols = slice(p * LANES, (p + 1) * LANES)
        dgated = mm(dmix, wmix_ref[:, cols])
        z = pa_ref[:, cols]
        sig = jax.nn.sigmoid(z)
        dy_ref[:, cols] = dgated * (z * sig)
        da_ref[:, cols] = (dgated * y_ref[:, cols] * (sig * (1.0 + z * (1.0 - sig)))).astype(bf16)
    finish(dy_ref)

    linked_t = link_bias(seqc_ref[...], seqr_ref[...], True)
    neg_ref[...] = jnp.where(linked_t, 0.0, far)
    lower = half_mask(rows, 0)
    cosine, sine = cos_ref[...], sin_ref[...]
    pair = pa_ref[:, wp + qwp :]
    swapped = pltpu.roll(pair, HD, 1)
    keys = rotated(jnp.where(lower, pair, swapped), cosine, sine).astype(bf16)
    values = jnp.where(lower, swapped, pair).astype(bf16)
    dk_ref[...] = jnp.zeros_like(dk_ref)
    dv_ref[...] = jnp.zeros_like(dv_ref)
    for p in range(qwp // LANES):
        cols = slice(wp + p * LANES, wp + (p + 1) * LANES)
        queries = rotated(pa_ref[:, cols], cosine, sine).astype(bf16)
        datt = datt_ref[:, p * LANES : (p + 1) * LANES]
        blocks = []
        for a in range(rows // span):
            here = slice(a * span, (a + 1) * span)
            reach = (a + 1) * span
            sides = []
            for side in range(min(2, qheads - 2 * p)):
                half = half_mask(span, side)
                q = jnp.where(half, queries[here], jnp.zeros((), bf16))
                do = jnp.where(half, datt[here], jnp.zeros((), bf16))
                scores = mm_nt(keys[:reach], q) * (HD**-0.5) + neg_ref[:reach, here]
                weights = jnp.exp(scores - jnp.max(scores, axis=0, keepdims=True))
                probs = weights / jnp.sum(weights, axis=0, keepdims=True)
                dp = mm_nt(values[:reach], do)
                ds = (probs * (dp - jnp.sum(probs * dp, axis=0, keepdims=True))).astype(bf16)
                dk_ref[:reach, :] += mm(ds, q)
                dv_ref[:reach, :] += mm(probs.astype(bf16), do)
                sides.append(mm_tn(ds, keys[:reach]))
            if len(sides) == 1:
                blocks.append(jnp.where(half_mask(span, 0), sides[0], 0.0))
            else:
                blocks.append(jnp.where(half_mask(span, 0), sides[0], sides[1]))
        dq = jnp.concatenate(blocks, axis=0) * (HD**-0.5)
        da_ref[:, cols] = rotated(dq, cosine, -sine).astype(bf16)
    dk = dk_ref[...] * (HD**-0.5)
    dk = rotated(dk + pltpu.roll(dk, HD, 1), cosine, -sine)
    dv = dv_ref[...]
    dv = dv + pltpu.roll(dv, HD, 1)
    da_ref[:, wp + qwp :] = jnp.where(lower, dk, dv).astype(bf16)


def mixer_back_kernel(
    dims, share, place_ref, pb_ref, dy_ref, y_ref, wzx_ref, wbc_ref, wsp_ref, da_ref, wq_ref, x_ref, seqc_ref, seqr_ref, masks_ref,
    convx_ref, convs_ref, bias_ref, rate_ref, skip_ref, gn2_ref,
    dxb_ref, dact_ref, dact_send_ref, small_ref,
    neg_ref, gt_ref, dgt_ref, dsum_ref, ddir_ref,
):
    heads, qheads, wp, qwp, span = dims
    rows = x_ref.shape[0]
    masks = {k: masks_ref[:, k : k + 1] for k in (1, 2, 3)}
    linked_t = link_bias(seqc_ref[...], seqr_ref[...], True)
    neg_ref[...] = jnp.where(linked_t, 0.0, far)
    dt = step_parts(pb_ref[:, wp + 256 :], bias_ref[...])
    linked = link_bias(seqc_ref[...], seqr_ref[...], False)
    decay = mm_exact(jnp.where(linked, 1.0, 0.0), -dt * rate_ref[...])
    decay_t = decay.T
    state = pb_ref[:, wp : wp + 256]
    sterms = conv_terms(state, masks)
    sconv = sum(t * convs_ref[k : k + 1, :] for k, t in enumerate(sterms))
    ssig = jax.nn.sigmoid(sconv)
    bcc = (sconv * ssig).astype(bf16)
    bm, cm = bcc[:, :128], bcc[:, 128:]
    gt_ref[...] = mm_nt(bm, cm)
    small_ref[...] = jnp.zeros_like(small_ref)
    dgt_ref[...] = jnp.zeros_like(dgt_ref)
    for p in range(wp // LANES):
        cols = slice(p * LANES, (p + 1) * LANES)
        width = HD * min(2, heads - 2 * p)
        terms = conv_terms(pb_ref[:, cols], masks)
        conv = sum(t * convx_ref[k : k + 1, cols] for k, t in enumerate(terms))
        csig = jax.nn.sigmoid(conv)
        xc = conv * csig
        dt_cols = spread_heads(dt, 2 * p, width)
        xdt = (xc * dt_cols).astype(bf16)
        skip = skip_ref[:, cols]
        scanned = y_ref[:, cols] - skip * xc
        dy = dy_ref[:, cols]
        small_ref[6:7, cols] = jnp.sum(dy * xc, axis=0, keepdims=True)
        dyb = dy.astype(bf16)
        blocks = []
        for a in range(rows // span):
            here = slice(a * span, (a + 1) * span)
            sides = []
            for side in range(width // HD):
                h = 2 * p + side
                dys = jnp.where(half_mask(rows - a * span, side), dyb[a * span :], jnp.zeros((), bf16))
                gap = decay_t[h : h + 1, a * span :] - decay[here, h : h + 1]
                falloff = jnp.exp(gap + neg_ref[here, a * span :])
                mixing = (gt_ref[here, a * span :] * falloff).astype(bf16)
                sides.append(mm(mixing, dyb[a * span :]))
                dgt_ref[here, a * span :] += mm_nt(xdt[here], dys) * falloff
            blocks.append(sides[0] if len(sides) == 1 else jnp.where(half_mask(span, 0), sides[0], sides[1]))
        dxdt = jnp.concatenate(blocks, axis=0)
        dsum_ref[:, cols] = dyb.astype(f32) * scanned - xdt.astype(f32) * dxdt
        ddir_ref[:, cols] = dxdt * xc
        dconv = (dxdt * dt_cols + skip * dy) * (csig * (1.0 + conv * (1.0 - csig)))
        small_ref[2:6, cols] = jnp.concatenate([jnp.sum(t * dconv, axis=0, keepdims=True) for t in terms], axis=0)
        dxb_ref[:, cols] = conv_back(dconv, masks, convx_ref[:, cols]).astype(bf16)

    dgt = dgt_ref[...].astype(bf16)
    dbcc = jnp.concatenate([mm(dgt, cm), mm_tn(dgt, bm)], axis=1)
    dsconv = dbcc * (ssig * (1.0 + sconv * (1.0 - ssig)))
    small_ref[2:6, wp : wp + 256] = jnp.concatenate([jnp.sum(t * dsconv, axis=0, keepdims=True) for t in sterms], axis=0)
    dxb_ref[:, wp : wp + 256] = conv_back(dsconv, masks, convs_ref[...]).astype(bf16)

    head_of = lax.broadcasted_iota(jnp.int32, (wp, LANES), 0) // HD
    pick = jnp.where(head_of == lax.broadcasted_iota(jnp.int32, (wp, LANES), 1), 1.0, 0.0)
    ds = mm_exact(dsum_ref[...], pick)
    ddirect = mm_exact(ddir_ref[...], pick)
    dlog = mm_exact(jnp.where(linked_t, 1.0, 0.0), ds)
    rate = rate_ref[...]
    ddt = ddirect - rate * dlog
    dstep = ddt * jax.nn.sigmoid(pb_ref[:, wp + 256 :] + bias_ref[...])
    dstep = jnp.where(lane_ids(rows) < heads, dstep, 0.0)
    dxb_ref[:, wp + 256 :] = dstep.astype(bf16)
    small_ref[6:7, wp : wp + LANES] = jnp.sum(dstep, axis=0, keepdims=True)
    small_ref[6:7, wp + LANES : wp + 256] = -rate * jnp.sum(dt * dlog, axis=0, keepdims=True)
    finish(dxb_ref)
    dact = mm_nt(da_ref[:, :wp], wzx_ref[:, :wp]) + mm_nt(dxb_ref[:, :wp], wzx_ref[:, wp:])
    dact = dact + mm_nt(dxb_ref[:, wp : wp + 256], wbc_ref[...]) + mm_nt(da_ref[:, wp : wp + qwp], wq_ref[...])
    dact = dact + mm_nt(dxb_ref[:, wp + 256 :], wsp_ref[:, :LANES]) + mm_nt(da_ref[:, wp + qwp :], wsp_ref[:, LANES:])
    dact_ref[...] = dact.astype(bf16)
    finish(dact_ref)
    dact_send_ref[...] = dact_ref[pl.ds(pl.multiple_of(place_ref[1] * share, 16), share), :]
    finish(dact_send_ref)
    x = x_ref[...].astype(f32)
    r1 = lax.rsqrt(jnp.mean(x * x, axis=-1, keepdims=True) + norm_eps)
    small_ref[0:1, :] = jnp.sum(dact * x * r1, axis=0, keepdims=True)
    small_ref[1:2, :] = gn2_ref[...] * (share / rows)


def pieces_of(width, most):
    groups = width // LANES
    count = -(-groups // (most // LANES))
    edges = [(i * groups // count) * LANES for i in range(count + 1)]
    return list(zip(edges[:-1], edges[1:]))


def grad_kernel(cuts, pieces, block, bit_ref, *refs):
    pairs = len(cuts)
    ins, refs = refs[: 2 * pairs], refs[2 * pairs :]
    sents, kepts, refs = refs[: len(pieces)], refs[len(pieces) : 2 * len(pieces)], refs[2 * len(pieces) :]
    buffers, refs = refs[: 2 * pairs], refs[2 * pairs :]
    turned, stage, in_sems, sent_sems, kept_sems = refs
    fetched = [Fetched(ins[i], buffers[i], in_sems.at[i]) for i in range(2 * pairs)]
    bit = bit_ref[0]
    count = turned.shape[0] // (2 * block)
    copies, at, sent_to = [], 0, 0
    for k, (low, high) in enumerate(cuts):
        turned[...] = fetched[2 * k][...].astype(f32).T.astype(bf16)
        for start in range(low, high, 512):
            stop = min(start + 512, high)
            full = mm(turned[...], fetched[2 * k + 1][:, start:stop]).astype(bf16)
            for j in range(2 * count):
                side = 1 - bit if j % 2 == 0 else bit
                stage[side, (j // 2) * block : (j // 2 + 1) * block, at : at + stop - start] = full[j * block : (j + 1) * block]
            at += stop - start
            while sent_to < len(pieces) and pieces[sent_to][1] <= at:
                cols = pl.ds(pieces[sent_to][0], pieces[sent_to][1] - pieces[sent_to][0])
                copies.append(pltpu.make_async_copy(stage.at[0, :, cols], sents[sent_to], sent_sems.at[sent_to]))
                copies.append(pltpu.make_async_copy(stage.at[1, :, cols], kepts[sent_to], kept_sems.at[sent_to]))
                copies[-2].start()
                copies[-1].start()
                sent_to += 1
    for copy in copies:
        copy.wait()


def plain_params(flops=1000, megabytes=40):
    return dict(
        compiler_params=pltpu.CompilerParams(vmem_limit_bytes=megabytes * 1024 * 1024),
        cost_estimate=pl.CostEstimate(flops=flops, bytes_accessed=1000, transcendentals=0),
    )


def weight_halves(pairs, bit, block, most, after=()):
    args = [a for left, right, _, _ in pairs for a in (left, right)]
    cuts = [(low, high) for _, _, low, high in pairs]
    rows, model = pairs[0][0].shape
    width = sum(high - low for low, high in cuts)
    pieces = pieces_of(width, most)
    outs = [(model // 2, high - low) for low, high in pieces] * 2

    def wrapped(bit_ref, *refs):
        grad_kernel(cuts, pieces, block, bit_ref, *refs[: len(args)], *refs[len(args) + len(after) :])

    outs = pl.pallas_call(
        wrapped,
        out_shape=[jax.ShapeDtypeStruct(s, bf16) for s in outs],
        in_specs=[pl.BlockSpec(memory_space=pltpu.SMEM)] + [pl.BlockSpec(memory_space=pl.ANY)] * (len(args) + len(after)),
        out_specs=[pl.BlockSpec(memory_space=pl.ANY)] * len(outs),
        scratch_shapes=[pltpu.VMEM(a.shape, a.dtype) for a in args]
        + [
            pltpu.VMEM((model, rows), bf16), pltpu.VMEM((2, model // 2, width), bf16),
            pltpu.SemaphoreType.DMA((len(args),)), pltpu.SemaphoreType.DMA((len(pieces),)),
            pltpu.SemaphoreType.DMA((len(pieces),)),
        ],
        **plain_params(megabytes=24),
    )(bit, *args, *after)
    return outs[: len(pieces)], outs[len(pieces) :]


def step_kernel(pieces, sources, block, small, which_ref, *refs):
    arrays, refs = refs[: 2 * sources], refs[2 * sources :]
    if small:
        small_own, small_other, refs = refs[0], refs[1], refs[2:]
    away, mine, refs = refs[0], refs[1], refs[2:]
    if small:
        small_ref, refs = refs[0], refs[1:]
    kept_buf, arrived_buf, away_buf, mine_buf, kept_sems, arrived_sems, away_sems, mine_sems = refs
    which = which_ref[0]
    ins, outs = [], []
    for k, (source, low, at, width) in enumerate(pieces):
        cols, here = pl.ds(low, width), pl.ds(at, width)
        ins.append(pltpu.make_async_copy(arrays[2 * source].at[:, cols], kept_buf.at[:, here], kept_sems.at[k]))
        ins.append(pltpu.make_async_copy(arrays[2 * source + 1].at[:, cols], arrived_buf.at[:, here], arrived_sems.at[k]))
        ins[-2].start()
        ins[-1].start()
    if small:
        small_ref[...] = small_own[...] + small_other[...]
    for k, (source, low, at, width) in enumerate(pieces):
        ins[2 * k].wait()
        ins[2 * k + 1].wait()
        here = pl.ds(at, width)
        for out, target, sems, side in ((away_buf, away, away_sems, 1 - which), (mine_buf, mine, mine_sems, which)):
            for i in range(kept_buf.shape[0] // (2 * block)):
                rows = pl.ds(pl.multiple_of((2 * i + side) * block, block), block)
                total = kept_buf[rows, at : at + width].astype(f32) + arrived_buf[rows, at : at + width].astype(f32)
                out[i * block : (i + 1) * block, at : at + width] = total.astype(bf16)
            outs.append(pltpu.make_async_copy(out.at[:, here], target.at[:, here], sems.at[k]))
            outs[-1].start()
    for copy in outs:
        copy.wait()


def step_call(which, sources, block, after, small=()):
    rows = sources[0][0].shape[0]
    pieces, at = [], 0
    for i, (kept, _) in enumerate(sources):
        for low, high in pieces_of(kept.shape[1], 512):
            pieces.append((i, low, at + low, high - low))
        at += kept.shape[1]
    args = [a for pair in sources for a in pair]

    def wrapped(which_ref, *refs):
        used = len(args) + len(small)
        step_kernel(pieces, len(sources), block, bool(small), which_ref, *refs[:used], *refs[used + len(after) :])

    half = (rows // 2, at)
    anywhere = pl.BlockSpec(memory_space=pl.ANY)
    inside = pl.BlockSpec(memory_space=pltpu.VMEM)
    return pl.pallas_call(
        wrapped,
        out_shape=[jax.ShapeDtypeStruct(half, bf16)] * 2 + [jax.ShapeDtypeStruct(a.shape, f32) for a in small[:1]],
        in_specs=[pl.BlockSpec(memory_space=pltpu.SMEM)] + [anywhere] * len(args) + [inside] * len(small)
        + [anywhere] * len(after),
        out_specs=[anywhere] * 2 + [inside] * len(small[:1]),
        scratch_shapes=[pltpu.VMEM((rows, at), bf16)] * 2
        + [pltpu.VMEM(half, bf16)] * 2
        + [pltpu.SemaphoreType.DMA((len(pieces),))] * 4,
        **plain_params(megabytes=16),
    )(which, *args, *small, *after)


def shared_kernel(wp, own_ref, other_ref, out_ref):
    row = lax.broadcasted_iota(jnp.int32, own_ref.shape, 0)
    lane = lax.broadcasted_iota(jnp.int32, own_ref.shape, 1)
    shared = (row < 2) | ((row < 6) & (lane >= wp) & (lane < wp + 256))
    out_ref[...] = own_ref[...] + jnp.where(shared, other_ref[...], 0.0)


class Fetched:
    def __init__(self, source, held, sem):
        self.held, self.copy, self.ready = held, pltpu.make_async_copy(source, held, sem), False
        self.shape, self.dtype = held.shape, held.dtype
        self.copy.start()

    def __getitem__(self, key):
        if not self.ready:
            self.copy.wait()
            self.ready = True
        return self.held[key]


class Stored:
    def __init__(self, held, target, sem):
        self.held, self.copy, self.sent = held, pltpu.make_async_copy(held, target, sem), False
        self.shape, self.dtype = held.shape, held.dtype

    def __getitem__(self, key):
        return self.held[key]

    def __setitem__(self, key, value):
        self.held[key] = value

    def finish(self):
        if not self.sent:
            self.copy.start()
            self.sent = True


LARGE = 1 << 16
COST_US = 1100000000


def finish(*refs):
    for ref in refs:
        if isinstance(ref, Stored):
            ref.finish()


def call(kernel, outs, scratch, args, scalars=0, after=(), flops=1000):
    count = len(args)
    large_in = [i >= scalars and a.size * a.dtype.itemsize >= LARGE for i, a in enumerate(args)]
    large_out = [s[0] * s[1] * jnp.dtype(t).itemsize >= LARGE for s, t in outs]
    buffers = [pltpu.VMEM(a.shape, a.dtype) for a, big in zip(args, large_in) if big]
    buffers += [pltpu.VMEM(s, t) for (s, t), big in zip(outs, large_out) if big]
    copies = len(buffers)

    def wrapped(*refs):
        ins, rest = list(refs[:count]), refs[count + len(after) :]
        results, rest = list(rest[: len(outs)]), rest[len(outs) :]
        held, sems, inner = rest[:copies], rest[copies], rest[copies + 1 :]
        slot = 0
        for i, big in enumerate(large_in):
            if big:
                ins[i] = Fetched(ins[i], held[slot], sems.at[slot])
                slot += 1
        for i, big in enumerate(large_out):
            if big:
                results[i] = Stored(held[slot], results[i], sems.at[slot])
                slot += 1
        kernel(*ins, *results, *inner)
        finish(*results)
        for ref in ins:
            if isinstance(ref, Fetched) and not ref.ready:
                ref.copy.wait()
        for ref in results:
            if isinstance(ref, Stored):
                ref.copy.wait()

    spaces = [pltpu.SMEM] * scalars + [pl.ANY if big else pltpu.VMEM for big in large_in[scalars:]] + [pl.ANY] * len(after)
    return pl.pallas_call(
        wrapped,
        out_shape=[jax.ShapeDtypeStruct(s, t) for s, t in outs],
        in_specs=[pl.BlockSpec(memory_space=space) for space in spaces],
        out_specs=[pl.BlockSpec(memory_space=pl.ANY if big else pltpu.VMEM) for big in large_out],
        scratch_shapes=buffers + [pltpu.SemaphoreType.DMA((max(copies, 1),))] + [pltpu.VMEM(s, t) for s, t in scratch],
        **plain_params(flops),
    )(*args, *after)


def swap(values):
    return lax.ppermute(values, "tensor", [(0, 1), (1, 0)])


def gather_rows(values, me, count):
    if count != 2:
        return lax.all_gather(values, "tensor", axis=0, tiled=True)
    other = swap(values)
    first = jnp.where(me == 0, values, other)
    return jnp.concatenate([first, jnp.where(me == 0, other, values)], axis=0)


def both_parts(part, count):
    if count != 2:
        return (lax.psum(part, "tensor"), jnp.zeros_like(part))
    return (part, swap(part))


def scatter_rows(part, me, count):
    if count != 2:
        return lax.psum_scatter(part, "tensor", scatter_dimension=0, tiled=True).astype(f32)
    halves = part.reshape(2, part.shape[0] // 2, part.shape[1])
    arrived = swap(lax.dynamic_index_in_dim(halves, 1 - me, 0, keepdims=False))
    return lax.dynamic_index_in_dim(halves, me, 0, keepdims=False).astype(f32) + arrived.astype(f32)


def partners(count, bit):
    return [(i, i ^ bit) for i in range(count)]


def exchange(sent, count, bit):
    return lax.ppermute(sent, "dp", partners(count, bit))


class Reduction:
    def __init__(self, parts, index, count, block, bit=1, small=None):
        self.parts, self.index, self.count, self.block, self.bit = parts, index, count, block, bit
        self.small = small
        self.small_arrived = None if small is None else exchange(small, count, bit)

    def with_other(self, other):
        return Reduction(self.parts + other.parts, self.index, self.count, self.block, self.bit)

    def done(self):
        return self.bit * 2 >= self.count

    def step(self, after=()):
        if self.done():
            return after
        self.bit *= 2
        which = ((self.index // self.bit) % 2).astype(jnp.int32).reshape(1)
        small = () if self.small is None else (self.small, self.small_arrived)
        sent, kept, *small = step_call(which, self.parts, self.block, after, small)
        self.parts = [(kept, exchange(sent, self.count, self.bit))]
        if small:
            self.small = small[0]
            self.small_arrived = exchange(self.small, self.count, self.bit)
        return (sent,)

    def total(self, after):
        totals = []
        for kept, arrived in self.parts:
            if self.bit > 1:
                arrived = lax.optimization_barrier((arrived, after[0]))[0]
            totals.append(kept.astype(f32) + arrived.astype(f32))
        return totals[0] if len(totals) == 1 else jnp.concatenate(totals, axis=1)


def segments(lengths, row_count):
    seq_ends = jnp.cumsum(lengths)
    places = jnp.arange(row_count, dtype=jnp.int32)
    passed = places[:, None] >= seq_ends[None, :]
    seq_ids = jnp.sum(passed.astype(jnp.int32), axis=1)
    starts = jnp.max(jnp.where(passed, seq_ends[None, :], 0), axis=1)
    is_live = (places < seq_ends[-1]).astype(f32)
    return (seq_ids, places - starts, is_live)


def body(
    dp_count, tensor_count, tokens, cotangent, seq_lengths, norm1_gain, norm2_gain, mixer_in, state_in, step_in,
    conv_inner, conv_state, step_bias, decay_log, skip_gain, mixer_out, query_in, key_value, attend_out, gate_up,
    down_out,
):
    share, model = tokens.shape
    rows = share * tensor_count
    me = lax.axis_index("tensor")
    index = lax.axis_index("dp")
    inner = mixer_in.shape[2]
    heads = step_in.shape[1]
    query_width = query_in.shape[1]
    qheads = query_width // HD
    wp, qwp = padded(inner), padded(query_width)
    span = min(LANES, rows)
    dims = (heads, qheads, wp, qwp, span)

    if tensor_count == 2:
        x_own, x_other = tokens, swap(tokens)
    else:
        x_own = x_other = gather_rows(tokens, me, tensor_count)
    place = jnp.stack([me, lax.rem(me + 1, tensor_count)]).astype(jnp.int32)
    seq_ids, positions, is_live = segments(seq_lengths[0], rows)
    live_share = lax.dynamic_slice_in_dim(is_live, me * share, share, 0)[:, None]
    dout_rows = gather_rows(lax.optimization_barrier((cotangent, x_other))[0], me, tensor_count)
    dout_rows = dout_rows * is_live[:, None].astype(bf16)

    seq_col = seq_ids.astype(f32)[:, None]
    seq_row = seq_ids.astype(f32)[None, :]
    shifts = jnp.minimum(jnp.arange(LANES, dtype=jnp.int32), 4)[None, :]
    masks = (positions[:, None] >= shifts).astype(f32)
    lane = jnp.arange(LANES)
    frequency = rope_base ** (-2.0 * (lane % (HD // 2)).astype(f32) / HD)
    angles = positions.astype(f32)[:, None] * frequency[None, :]
    cosine = jnp.cos(angles)
    sine = jnp.sin(angles) * jnp.where(lane % HD < HD // 2, -1.0, 1.0)[None, :]

    key_index = me * qheads // (QH // KVH)
    pair_local = lax.dynamic_slice_in_dim(key_value, key_index * HD, HD, 2).reshape(model, 2 * HD)
    if inner == wp:
        wzx = mixer_in.reshape(model, 2 * inner)
    else:
        wzx = pad_to(mixer_in, wp).reshape(model, 2 * wp)
    wsp = jnp.concatenate([pad_to(step_in, LANES), pair_local], axis=1)
    wq, wmix, watt = pad_to(query_in, qwp), pad_to(mixer_out, wp), pad_to(attend_out, qwp)
    taps = pad_to(conv_inner, wp)
    bias = pad_to(step_bias[None], LANES)
    rate = pad_to(jnp.exp(decay_log)[None], LANES)
    skip = pad_to(jnp.repeat(skip_gain, HD)[None], wp)
    gain1, gain2 = norm1_gain[None], norm2_gain[None]

    x_rows, act, pa, pb, y, cat, part = call(
        functools.partial(front_kernel, dims),
        [
            ((rows, model), bf16), ((rows, model), bf16), ((rows, wp + qwp + LANES), f32), ((rows, wp + 384), f32),
            ((rows, wp), f32), ((rows, wp + qwp), bf16), ((rows, model), bf16),
        ],
        [((rows, rows), f32), ((rows, rows), f32), ((rows, LANES), bf16)],
        (
            place, x_own, x_other, state_in, wsp, wzx, wq, wmix, watt, gain1, seq_col, seq_row, masks, cosine, sine, taps,
            conv_state, bias, rate, skip,
        ),
        1, (), 10 * COST_US,
    )
    own, other = both_parts(part, tensor_count)
    wgu = lax.optimization_barrier((gate_up, part))[0].reshape(model, -1)
    dhidden = mm(dout_rows, down_out)
    ff2 = wgu.shape[1]
    h1, n2, hidden, dgu, ffn_part, dn2_part = call(
        middle_kernel,
        [
            ((rows, model), f32), ((rows, model), bf16), ((rows, ff2 // 2), bf16), ((rows, ff2), bf16),
            ((rows, model), bf16), ((rows, model), bf16),
        ],
        [],
        (x_rows, own, other, gain2, wgu, down_out, dhidden),
    )
    dn2_own, dn2_other = both_parts(dn2_part, tensor_count)

    bit = (index % 2).astype(jnp.int32).reshape(1)
    block = model // dp_count

    def reduction(pairs, most, after=(), small=None):
        sent, kept = weight_halves(pairs, bit, block, most, after)
        parts = [(stay, exchange(go, dp_count, 1)) for go, stay in zip(sent, kept)]
        return Reduction(parts, index, dp_count, block, 1, small)

    most = max(LANES, ff2 * 5 // 16 // LANES * LANES)
    cut = ff2 - ff2 // 4
    ffn_a = reduction([(dout_rows, hidden, 0, most)], most)
    ffn_b = reduction([(dout_rows, hidden, most, ff2 // 2), (n2, dgu, 0, cut)], most, (ffn_a.parts[0][0],))
    order = ffn_a.step((ffn_b.parts[0][0],))
    order = ffn_b.step(order)

    dh1_share, ffn_send, dmix, dy, da, gn2 = call(
        functools.partial(attend_back_kernel, dims, share),
        [
            ((share, model), f32), ((share, model), bf16), ((rows, model), bf16), ((rows, wp), f32),
            ((rows, wp + qwp + LANES), bf16), ((1, model), f32),
        ],
        [((rows, rows), f32), ((rows, model), f32), ((rows, qwp), bf16), ((rows, LANES), f32), ((rows, LANES), f32)],
        (
            place, dn2_own, dn2_other, ffn_part, h1, dout_rows, gain2, wmix, watt, seq_col, seq_row, cosine, sine, pa, y,
        ),
        1, order, 40 * COST_US,
    )
    mix_out = reduction([(dmix, cat, 0, wp + qwp), (n2, dgu, cut, ff2)], 512)
    mix_a = reduction([(act, da, 0, wp + qwp + LANES)], 2048, (mix_out.parts[0][0],))
    ffn = ffn_a.with_other(ffn_b)
    order = ffn.step((mix_a.parts[0][0],))
    order = mix_out.step(order)
    ffn_arrived = swap(ffn_send) if tensor_count == 2 else ffn_send

    dxb, dact, dact_send, small = call(
        functools.partial(mixer_back_kernel, dims, share),
        [((rows, wp + 384), bf16), ((rows, model), bf16), ((share, model), bf16), ((8, model), f32)],
        [
            ((rows, rows), f32), ((rows, rows), f32), ((rows, rows), f32), ((rows, wp), f32), ((rows, wp), f32),
        ],
        (
            place, pb, dy, y, wzx, state_in, wsp, da, wq, x_rows, seq_col, seq_row, masks, taps, conv_state, bias, rate,
            skip, gn2,
        ),
        1, order + (ffn_arrived,), 40 * COST_US,
    )
    if tensor_count == 2:
        summed = swap(small)
    else:
        summed = lax.psum(small, "tensor") - small
    small = call(functools.partial(shared_kernel, wp), [((8, model), f32)], [], (small, summed))[0]
    mix_b = reduction([(act, dxb, 0, wp + 384)], 384, (), small)
    order = mix_a.step((mix_b.parts[0][0],))
    order = ffn.step(order)
    order = mix_out.step(order)
    order = mix_b.step(order)
    ffn_total = ffn.total(order) if ffn.done() else None
    order = mix_a.step(order if ffn_total is None else order + (ffn_total,))
    order = mix_out.step(order)
    if tensor_count == 2:
        dact_mine = lax.dynamic_slice_in_dim(dact, me * share, share, 0).astype(f32)
        dact_share = dact_mine + lax.optimization_barrier((swap(dact_send), order[0]))[0].astype(f32)
    else:
        dact_share = scatter_rows(dact, me, tensor_count)
    for r in [mix_b, mix_a] + 4 * [ffn, mix_out, mix_a]:
        order = r.step(order)
    out_total = mix_out.total(order)
    while not mix_b.done():
        order = mix_b.step(order)
    if ffn_total is None:
        ffn_total = ffn.total(order)
    first_total = mix_a.total(order)
    down_total = ffn_total[:, : ff2 // 2]
    up_total = jnp.concatenate([ffn_total[:, ff2 // 2 :], out_total[:, wp + qwp :]], axis=1)
    mix_b, minor = mix_b.total(order), mix_b.small + mix_b.small_arrived
    second_total, state_total = mix_b[:, :wp], mix_b[:, wp : wp + 256]
    step_total = mix_b[:, wp + 256 :]

    if tensor_count == 2:
        ffn_mine = lax.dynamic_slice_in_dim(ffn_part, me * share, share, 0).astype(f32)
        ffn_share = ffn_mine + ffn_arrived.astype(f32)
    else:
        ffn_share = scatter_rows(ffn_part, me, tensor_count)
    h1_share = lax.dynamic_slice_in_dim(h1, me * share, share, 0)
    block_out = ((h1_share + ffn_share) * live_share).astype(bf16)

    x_share = tokens.astype(f32)
    r1 = lax.rsqrt(jnp.mean(x_share * x_share, axis=-1, keepdims=True) + norm_eps)
    u = dact_share * gain1
    token_grad = dh1_share + r1 * u - x_share * (r1 * r1 * r1 * jnp.mean(u * x_share, axis=-1, keepdims=True))

    g_norm1, g_norm2, g_conv_state = minor[0], minor[1], minor[2:6, wp : wp + 256]
    g_conv_inner = minor[2:6, :inner]
    g_skip = jnp.sum(minor[6, :wp].reshape(-1, HD), axis=1)[:heads]
    g_bias = minor[6, wp : wp + heads]
    g_decay = minor[6, wp + LANES : wp + LANES + heads]

    both = jnp.concatenate([state_total, first_total[:, wp + qwp :]], axis=1).astype(bf16)
    placed = lambda pair: lax.dynamic_update_slice_in_dim(
        jnp.zeros((block,) + key_value.shape[1:], f32), pair.astype(f32).reshape(block, 2, HD), key_index * HD, 2
    )
    if tensor_count == 2:
        arrived = swap(both)
        g_state = both[:, :256].astype(f32) + arrived[:, :256].astype(f32)
        mine = both[:, 256:].reshape(block, 2, HD)
        theirs = arrived[:, 256:].reshape(block, 2, HD)
        g_pair = jnp.concatenate(
            [jnp.where(me == 0, mine, theirs), jnp.where(me == 0, theirs, mine)], axis=2
        ).astype(f32)
    else:
        g_state = lax.psum(both[:, :256], "tensor").astype(f32)
        g_pair = lax.psum(placed(both[:, 256:]).astype(bf16), "tensor").astype(f32)

    g_mixer_in = jnp.stack([first_total[:, :inner], second_total[:, :inner]], axis=1)
    return (
        block_out,
        token_grad.astype(bf16),
        g_norm1,
        g_norm2,
        g_mixer_in,
        g_state,
        step_total[:, :heads],
        g_conv_inner,
        g_conv_state,
        g_bias,
        g_decay,
        g_skip,
        out_total[:, :inner],
        first_total[:, wp : wp + query_width],
        g_pair,
        out_total[:, wp : wp + query_width],
        up_total.reshape(block, 2, ff2 // 2),
        down_total,
    )


def solution(mesh):
    return jax.shard_map(
        functools.partial(body, mesh.shape["dp"], mesh.shape["tensor"]),
        mesh=mesh,
        in_specs=(
            P(("dp", "tensor"), None),
            P(("dp", "tensor"), None),
            P("dp", None),
            P(),
            P(),
            P(None, None, "tensor"),
            P(),
            P(None, "tensor"),
            P(None, "tensor"),
            P(),
            P("tensor"),
            P("tensor"),
            P("tensor"),
            P(None, "tensor"),
            P(None, "tensor"),
            P(),
            P(None, "tensor"),
            P(None, None, "tensor"),
            P(None, "tensor"),
        ),
        out_specs=(
            P(("dp", "tensor"), None),
            P(("dp", "tensor"), None),
            P(),
            P(),
            P("dp", None, "tensor"),
            P("dp", None),
            P("dp", "tensor"),
            P(None, "tensor"),
            P(),
            P("tensor"),
            P("tensor"),
            P("tensor"),
            P("dp", "tensor"),
            P("dp", "tensor"),
            P("dp", None, None),
            P("dp", "tensor"),
            P("dp", None, "tensor"),
            P("dp", "tensor"),
        ),
        check_vma=False,
    )
```

```python
import functools

import jax
import jax.numpy as jnp
from jax import lax
from jax.experimental import pallas as pl
from jax.experimental.pallas import tpu as pltpu
from jax.sharding import PartitionSpec as P

HD = 64
QH = 8
KVH = 2
LANES = 128

rope_base = 100000000000.0
norm_eps = 1e-05
far = -1e30
highest = lax.Precision.HIGHEST
f32 = jnp.float32
bf16 = jnp.bfloat16


def padded(width):
    return -(-width // LANES) * LANES


def pad_to(values, width):
    return jnp.pad(values, [(0, 0)] * (values.ndim - 1) + [(0, width - values.shape[-1])])


def mm(left, right):
    return jnp.dot(left, right, preferred_element_type=f32)


def mm_nt(left, right):
    return lax.dot_general(left, right, (((1,), (1,)), ((), ())), preferred_element_type=f32)


def mm_tn(left, right):
    return lax.dot_general(left, right, (((0,), (0,)), ((), ())), preferred_element_type=f32)


def mm_exact(left, right):
    return jnp.dot(left, right, preferred_element_type=f32, precision=highest)


def lane_ids(rows):
    return lax.broadcasted_iota(jnp.int32, (rows, LANES), 1)


def partner_half(values):
    lane = lane_ids(values.shape[0])
    return jnp.where(lane % HD < HD // 2, pltpu.roll(values, LANES - HD // 2, 1), pltpu.roll(values, HD // 2, 1))


def rotated(values, cosine, signed_sine):
    return values * cosine + partner_half(values) * signed_sine


def conv_terms(values, masks):
    return [pltpu.roll(values, offset, 0) * masks[offset] for offset in (3, 2, 1)] + [values]


def conv_back(grad, masks, taps):
    rows = grad.shape[0]
    total = grad * taps[3:4]
    for offset in (1, 2, 3):
        total = total + pltpu.roll(grad * masks[offset], rows - offset, 0) * taps[3 - offset : 4 - offset]
    return total


def link_bias(seq_col, seq_row, transposed):
    rows = seq_col.shape[0]
    down = lax.broadcasted_iota(jnp.int32, (rows, rows), 0)
    across = lax.broadcasted_iota(jnp.int32, (rows, rows), 1)
    ordered = down <= across if transposed else down >= across
    return (seq_col == seq_row) & ordered


def step_parts(raw, bias):
    shifted = raw + bias
    return jnp.maximum(shifted, 0.0) + jnp.log1p(jnp.exp(-jnp.abs(shifted)))


def spread_heads(columns, first, width):
    rows = columns.shape[0]
    low = jnp.broadcast_to(columns[:, first : first + 1], (rows, LANES))
    if width <= HD:
        return low
    high = jnp.broadcast_to(columns[:, first + 1 : first + 2], (rows, LANES))
    return jnp.where(lane_ids(rows) < HD, low, high)


def half_mask(rows, side):
    lane = lane_ids(rows)
    return lane < HD if side == 0 else lane >= HD


def front_kernel(
    dims, place_ref, own_ref, other_ref, wbc_ref, wsp_ref, wzx_ref, wq_ref, wmix_ref, watt_ref, gain_ref, seqc_ref,
    seqr_ref, masks_ref, cos_ref, sin_ref, convx_ref, convs_ref, bias_ref, rate_ref, skip_ref,
    x_ref, act_ref, pa_ref, pb_ref, y_ref, cat_ref, part_ref, neg_ref, g_ref, xdt_ref,
):
    heads, qheads, wp, qwp, span = dims
    rows = x_ref.shape[0]
    share = own_ref.shape[0]
    if share == rows:
        x_ref[...] = own_ref[...]
    else:
        x_ref[pl.ds(pl.multiple_of(place_ref[0] * share, 16), share), :] = own_ref[...]
        x_ref[pl.ds(pl.multiple_of(place_ref[1] * share, 16), share), :] = other_ref[...]
    finish(x_ref)
    x = x_ref[...].astype(f32)
    act = (x * lax.rsqrt(jnp.mean(x * x, axis=-1, keepdims=True) + norm_eps) * gain_ref[...]).astype(bf16)
    act_ref[...] = act
    finish(act_ref)
    pb_ref[:, wp : wp + 256] = mm(act, wbc_ref[...])
    pb_ref[:, wp + 256 :] = mm(act, wsp_ref[:, :LANES])
    pb_ref[:, :wp] = mm(act, wzx_ref[:, wp:])
    pa_ref[:, wp : wp + qwp] = mm(act, wq_ref[...])
    pa_ref[:, wp + qwp :] = mm(act, wsp_ref[:, LANES:])
    pa_ref[:, :wp] = mm(act, wzx_ref[:, :wp])
    finish(pa_ref, pb_ref)
    masks = {k: masks_ref[:, k : k + 1] for k in (1, 2, 3)}
    linked = link_bias(seqc_ref[...], seqr_ref[...], False)
    neg_ref[...] = jnp.where(linked, 0.0, far)
    dt = step_parts(pb_ref[:, wp + 256 :], bias_ref[...])
    decay = mm_exact(jnp.where(linked, 1.0, 0.0), -dt * rate_ref[...])
    decay_t = decay.T
    terms = conv_terms(pb_ref[:, wp : wp + 256], masks)
    bcc = sum(t * convs_ref[k : k + 1, :] for k, t in enumerate(terms))
    bcc = (bcc * jax.nn.sigmoid(bcc)).astype(bf16)
    g_ref[...] = mm_nt(bcc[:, 128:], bcc[:, :128])

    for p in range(wp // LANES):
        cols = slice(p * LANES, (p + 1) * LANES)
        width = HD * min(2, heads - 2 * p)
        conv = sum(t * convx_ref[k : k + 1, cols] for k, t in enumerate(conv_terms(pb_ref[:, cols], masks)))
        xc = conv * jax.nn.sigmoid(conv)
        xdt_ref[...] = (xc * spread_heads(dt, 2 * p, width)).astype(bf16)
        blocks = []
        for a in range(rows // span):
            here = slice(a * span, (a + 1) * span)
            reach = (a + 1) * span
            sides = []
            for h in range(2 * p, 2 * p + width // HD):
                gap = decay[here, h : h + 1] - decay_t[h : h + 1, :reach]
                mixing = g_ref[here, :reach] * jnp.exp(gap + neg_ref[here, :reach])
                sides.append(mm(mixing.astype(bf16), xdt_ref[:reach, :]))
            blocks.append(sides[0] if len(sides) == 1 else jnp.where(half_mask(span, 0), sides[0], sides[1]))
        y = jnp.concatenate(blocks, axis=0) + skip_ref[:, cols] * xc
        y_ref[:, cols] = y
        z = pa_ref[:, cols]
        cat_ref[:, cols] = (y * (z * jax.nn.sigmoid(z))).astype(bf16)

    finish(y_ref)
    cosine, sine = cos_ref[...], sin_ref[...]
    pair = pa_ref[:, wp + qwp :]
    swapped = pltpu.roll(pair, HD, 1)
    lower = half_mask(rows, 0)
    keys = rotated(jnp.where(lower, pair, swapped), cosine, sine).astype(bf16)
    values = jnp.where(lower, swapped, pair).astype(bf16)
    for p in range(qwp // LANES):
        cols = slice(wp + p * LANES, wp + (p + 1) * LANES)
        queries = rotated(pa_ref[:, cols], cosine, sine).astype(bf16)
        for a in range(rows // span):
            here = slice(a * span, (a + 1) * span)
            reach = (a + 1) * span
            sides = []
            for side in range(min(2, qheads - 2 * p)):
                q = jnp.where(half_mask(span, side), queries[here], jnp.zeros((), bf16))
                scores = mm_nt(q, keys[:reach]) * (HD**-0.5) + neg_ref[here, :reach]
                weights = jnp.exp(scores - jnp.max(scores, axis=-1, keepdims=True))
                probs = weights / jnp.sum(weights, axis=-1, keepdims=True)
                sides.append(mm(probs.astype(bf16), values[:reach]))
            if len(sides) == 1:
                out = jnp.where(half_mask(span, 0), sides[0], 0.0)
            else:
                out = jnp.where(half_mask(span, 0), sides[0], sides[1])
            cat_ref[here, cols] = out.astype(bf16)
    finish(cat_ref)
    part_ref[...] = (mm_nt(cat_ref[:, :wp], wmix_ref[...]) + mm_nt(cat_ref[:, wp:], watt_ref[...])).astype(bf16)


def middle_kernel(
    x_ref, own_ref, other_ref, gain_ref, wgu_ref, down_ref, dhid_ref,
    h1_ref, n2_ref, hidden_ref, dgu_ref, out_ref, dn2_ref,
):
    width = down_ref.shape[1]
    h1 = x_ref[...].astype(f32) + (own_ref[...].astype(f32) + other_ref[...].astype(f32))
    h1_ref[...] = h1
    finish(h1_ref)
    n2 = (h1 * lax.rsqrt(jnp.mean(h1 * h1, axis=-1, keepdims=True) + norm_eps) * gain_ref[...]).astype(bf16)
    n2_ref[...] = n2
    finish(n2_ref)
    gate = mm(n2, wgu_ref[:, :width])
    up = mm(n2, wgu_ref[:, width:])
    sig = jax.nn.sigmoid(gate)
    silu = gate * sig
    hidden = (silu * up).astype(bf16)
    hidden_ref[...] = hidden
    finish(hidden_ref)
    dhid = dhid_ref[...].astype(f32)
    dgu_ref[:, :width] = (dhid * up * (sig * (1.0 + gate * (1.0 - sig)))).astype(bf16)
    dgu_ref[:, width:] = (dhid * silu).astype(bf16)
    finish(dgu_ref)
    dn2_ref[...] = mm_nt(dgu_ref[...], wgu_ref[...]).astype(bf16)
    finish(dn2_ref)
    out_ref[...] = mm_nt(hidden, down_ref[...]).astype(bf16)


def attend_back_kernel(
    dims, share, place_ref, own_ref, other_ref, ffn_ref, h1_ref, dout_ref, gain2_ref, wmix_ref, watt_ref, seqc_ref,
    seqr_ref, cos_ref, sin_ref, pa_ref, y_ref,
    dh1_ref, ffn_send_ref, dmix_ref, dy_ref, da_ref, gn2_ref,
    neg_ref, dh1_all_ref, datt_ref, dk_ref, dv_ref,
):
    heads, qheads, wp, qwp, span = dims
    rows = own_ref.shape[0]
    dn2 = own_ref[...].astype(f32) + other_ref[...].astype(f32)
    h1 = h1_ref[...]
    r2 = lax.rsqrt(jnp.mean(h1 * h1, axis=-1, keepdims=True) + norm_eps)
    u = dn2 * gain2_ref[...]
    dh1 = dout_ref[...].astype(f32) + r2 * u - h1 * (r2 * r2 * r2 * jnp.mean(u * h1, axis=-1, keepdims=True))
    gn2_ref[...] = jnp.sum(dn2 * h1 * r2, axis=0, keepdims=True)
    dh1_all_ref[...] = dh1
    dh1_ref[...] = dh1_all_ref[pl.ds(pl.multiple_of(place_ref[0] * share, 16), share), :]
    ffn_send_ref[...] = ffn_ref[pl.ds(pl.multiple_of(place_ref[1] * share, 16), share), :]
    dmix = dh1.astype(bf16)
    dmix_ref[...] = dmix
    finish(dh1_ref, ffn_send_ref, dmix_ref)
    datt_ref[...] = mm(dmix, watt_ref[...]).astype(bf16)
    for p in range(wp // LANES):
        cols = slice(p * LANES, (p + 1) * LANES)
        dgated = mm(dmix, wmix_ref[:, cols])
        z = pa_ref[:, cols]
        sig = jax.nn.sigmoid(z)
        dy_ref[:, cols] = dgated * (z * sig)
        da_ref[:, cols] = (dgated * y_ref[:, cols] * (sig * (1.0 + z * (1.0 - sig)))).astype(bf16)
    finish(dy_ref)

    linked_t = link_bias(seqc_ref[...], seqr_ref[...], True)
    neg_ref[...] = jnp.where(linked_t, 0.0, far)
    lower = half_mask(rows, 0)
    cosine, sine = cos_ref[...], sin_ref[...]
    pair = pa_ref[:, wp + qwp :]
    swapped = pltpu.roll(pair, HD, 1)
    keys = rotated(jnp.where(lower, pair, swapped), cosine, sine).astype(bf16)
    values = jnp.where(lower, swapped, pair).astype(bf16)
    dk_ref[...] = jnp.zeros_like(dk_ref)
    dv_ref[...] = jnp.zeros_like(dv_ref)
    for p in range(qwp // LANES):
        cols = slice(wp + p * LANES, wp + (p + 1) * LANES)
        queries = rotated(pa_ref[:, cols], cosine, sine).astype(bf16)
        datt = datt_ref[:, p * LANES : (p + 1) * LANES]
        blocks = []
        for a in range(rows // span):
            here = slice(a * span, (a + 1) * span)
            reach = (a + 1) * span
            sides = []
            for side in range(min(2, qheads - 2 * p)):
                half = half_mask(span, side)
                q = jnp.where(half, queries[here], jnp.zeros((), bf16))
                do = jnp.where(half, datt[here], jnp.zeros((), bf16))
                scores = mm_nt(keys[:reach], q) * (HD**-0.5) + neg_ref[:reach, here]
                weights = jnp.exp(scores - jnp.max(scores, axis=0, keepdims=True))
                probs = weights / jnp.sum(weights, axis=0, keepdims=True)
                dp = mm_nt(values[:reach], do)
                ds = (probs * (dp - jnp.sum(probs * dp, axis=0, keepdims=True))).astype(bf16)
                dk_ref[:reach, :] += mm(ds, q)
                dv_ref[:reach, :] += mm(probs.astype(bf16), do)
                sides.append(mm_tn(ds, keys[:reach]))
            if len(sides) == 1:
                blocks.append(jnp.where(half_mask(span, 0), sides[0], 0.0))
            else:
                blocks.append(jnp.where(half_mask(span, 0), sides[0], sides[1]))
        dq = jnp.concatenate(blocks, axis=0) * (HD**-0.5)
        da_ref[:, cols] = rotated(dq, cosine, -sine).astype(bf16)
    dk = dk_ref[...] * (HD**-0.5)
    dk = rotated(dk + pltpu.roll(dk, HD, 1), cosine, -sine)
    dv = dv_ref[...]
    dv = dv + pltpu.roll(dv, HD, 1)
    da_ref[:, wp + qwp :] = jnp.where(lower, dk, dv).astype(bf16)


def mixer_back_kernel(
    dims, share, place_ref, pb_ref, dy_ref, y_ref, wzx_ref, wbc_ref, wsp_ref, da_ref, wq_ref, x_ref, seqc_ref, seqr_ref, masks_ref,
    convx_ref, convs_ref, bias_ref, rate_ref, skip_ref, gn2_ref,
    dxb_ref, dact_ref, dact_send_ref, small_ref,
    neg_ref, gt_ref, dgt_ref, dsum_ref, ddir_ref,
):
    heads, qheads, wp, qwp, span = dims
    rows = x_ref.shape[0]
    masks = {k: masks_ref[:, k : k + 1] for k in (1, 2, 3)}
    linked_t = link_bias(seqc_ref[...], seqr_ref[...], True)
    neg_ref[...] = jnp.where(linked_t, 0.0, far)
    dt = step_parts(pb_ref[:, wp + 256 :], bias_ref[...])
    linked = link_bias(seqc_ref[...], seqr_ref[...], False)
    decay = mm_exact(jnp.where(linked, 1.0, 0.0), -dt * rate_ref[...])
    decay_t = decay.T
    state = pb_ref[:, wp : wp + 256]
    sterms = conv_terms(state, masks)
    sconv = sum(t * convs_ref[k : k + 1, :] for k, t in enumerate(sterms))
    ssig = jax.nn.sigmoid(sconv)
    bcc = (sconv * ssig).astype(bf16)
    bm, cm = bcc[:, :128], bcc[:, 128:]
    gt_ref[...] = mm_nt(bm, cm)
    small_ref[...] = jnp.zeros_like(small_ref)
    dgt_ref[...] = jnp.zeros_like(dgt_ref)
    for p in range(wp // LANES):
        cols = slice(p * LANES, (p + 1) * LANES)
        width = HD * min(2, heads - 2 * p)
        terms = conv_terms(pb_ref[:, cols], masks)
        conv = sum(t * convx_ref[k : k + 1, cols] for k, t in enumerate(terms))
        csig = jax.nn.sigmoid(conv)
        xc = conv * csig
        dt_cols = spread_heads(dt, 2 * p, width)
        xdt = (xc * dt_cols).astype(bf16)
        skip = skip_ref[:, cols]
        scanned = y_ref[:, cols] - skip * xc
        dy = dy_ref[:, cols]
        small_ref[6:7, cols] = jnp.sum(dy * xc, axis=0, keepdims=True)
        dyb = dy.astype(bf16)
        blocks = []
        for a in range(rows // span):
            here = slice(a * span, (a + 1) * span)
            sides = []
            for side in range(width // HD):
                h = 2 * p + side
                dys = jnp.where(half_mask(rows - a * span, side), dyb[a * span :], jnp.zeros((), bf16))
                gap = decay_t[h : h + 1, a * span :] - decay[here, h : h + 1]
                falloff = jnp.exp(gap + neg_ref[here, a * span :])
                mixing = (gt_ref[here, a * span :] * falloff).astype(bf16)
                sides.append(mm(mixing, dyb[a * span :]))
                dgt_ref[here, a * span :] += mm_nt(xdt[here], dys) * falloff
            blocks.append(sides[0] if len(sides) == 1 else jnp.where(half_mask(span, 0), sides[0], sides[1]))
        dxdt = jnp.concatenate(blocks, axis=0)
        dsum_ref[:, cols] = dyb.astype(f32) * scanned - xdt.astype(f32) * dxdt
        ddir_ref[:, cols] = dxdt * xc
        dconv = (dxdt * dt_cols + skip * dy) * (csig * (1.0 + conv * (1.0 - csig)))
        small_ref[2:6, cols] = jnp.concatenate([jnp.sum(t * dconv, axis=0, keepdims=True) for t in terms], axis=0)
        dxb_ref[:, cols] = conv_back(dconv, masks, convx_ref[:, cols]).astype(bf16)

    dgt = dgt_ref[...].astype(bf16)
    dbcc = jnp.concatenate([mm(dgt, cm), mm_tn(dgt, bm)], axis=1)
    dsconv = dbcc * (ssig * (1.0 + sconv * (1.0 - ssig)))
    small_ref[2:6, wp : wp + 256] = jnp.concatenate([jnp.sum(t * dsconv, axis=0, keepdims=True) for t in sterms], axis=0)
    dxb_ref[:, wp : wp + 256] = conv_back(dsconv, masks, convs_ref[...]).astype(bf16)

    head_of = lax.broadcasted_iota(jnp.int32, (wp, LANES), 0) // HD
    pick = jnp.where(head_of == lax.broadcasted_iota(jnp.int32, (wp, LANES), 1), 1.0, 0.0)
    ds = mm_exact(dsum_ref[...], pick)
    ddirect = mm_exact(ddir_ref[...], pick)
    dlog = mm_exact(jnp.where(linked_t, 1.0, 0.0), ds)
    rate = rate_ref[...]
    ddt = ddirect - rate * dlog
    dstep = ddt * jax.nn.sigmoid(pb_ref[:, wp + 256 :] + bias_ref[...])
    dstep = jnp.where(lane_ids(rows) < heads, dstep, 0.0)
    dxb_ref[:, wp + 256 :] = dstep.astype(bf16)
    small_ref[6:7, wp : wp + LANES] = jnp.sum(dstep, axis=0, keepdims=True)
    small_ref[6:7, wp + LANES : wp + 256] = -rate * jnp.sum(dt * dlog, axis=0, keepdims=True)
    finish(dxb_ref)
    dact = mm_nt(da_ref[:, :wp], wzx_ref[:, :wp]) + mm_nt(dxb_ref[:, :wp], wzx_ref[:, wp:])
    dact = dact + mm_nt(dxb_ref[:, wp : wp + 256], wbc_ref[...]) + mm_nt(da_ref[:, wp : wp + qwp], wq_ref[...])
    dact = dact + mm_nt(dxb_ref[:, wp + 256 :], wsp_ref[:, :LANES]) + mm_nt(da_ref[:, wp + qwp :], wsp_ref[:, LANES:])
    dact_ref[...] = dact.astype(bf16)
    finish(dact_ref)
    dact_send_ref[...] = dact_ref[pl.ds(pl.multiple_of(place_ref[1] * share, 16), share), :]
    finish(dact_send_ref)
    x = x_ref[...].astype(f32)
    r1 = lax.rsqrt(jnp.mean(x * x, axis=-1, keepdims=True) + norm_eps)
    small_ref[0:1, :] = jnp.sum(dact * x * r1, axis=0, keepdims=True)
    small_ref[1:2, :] = gn2_ref[...] * (share / rows)


def pieces_of(width, most):
    groups = width // LANES
    count = -(-groups // (most // LANES))
    edges = [(i * groups // count) * LANES for i in range(count + 1)]
    return list(zip(edges[:-1], edges[1:]))


def grad_kernel(cuts, pieces, block, bit_ref, *refs):
    pairs = len(cuts)
    ins, refs = refs[: 2 * pairs], refs[2 * pairs :]
    sents, kepts, refs = refs[: len(pieces)], refs[len(pieces) : 2 * len(pieces)], refs[2 * len(pieces) :]
    buffers, refs = refs[: 2 * pairs], refs[2 * pairs :]
    turned, stage, in_sems, sent_sems, kept_sems = refs
    fetched = [Fetched(ins[i], buffers[i], in_sems.at[i]) for i in range(2 * pairs)]
    bit = bit_ref[0]
    count = turned.shape[0] // (2 * block)
    copies, at, sent_to = [], 0, 0
    for k, (low, high) in enumerate(cuts):
        turned[...] = fetched[2 * k][...].astype(f32).T.astype(bf16)
        for start in range(low, high, 512):
            stop = min(start + 512, high)
            full = mm(turned[...], fetched[2 * k + 1][:, start:stop]).astype(bf16)
            for j in range(2 * count):
                side = 1 - bit if j % 2 == 0 else bit
                stage[side, (j // 2) * block : (j // 2 + 1) * block, at : at + stop - start] = full[j * block : (j + 1) * block]
            at += stop - start
            while sent_to < len(pieces) and pieces[sent_to][1] <= at:
                cols = pl.ds(pieces[sent_to][0], pieces[sent_to][1] - pieces[sent_to][0])
                copies.append(pltpu.make_async_copy(stage.at[0, :, cols], sents[sent_to], sent_sems.at[sent_to]))
                copies.append(pltpu.make_async_copy(stage.at[1, :, cols], kepts[sent_to], kept_sems.at[sent_to]))
                copies[-2].start()
                copies[-1].start()
                sent_to += 1
    for copy in copies:
        copy.wait()


def plain_params(flops=1000, megabytes=52):
    return dict(
        compiler_params=pltpu.CompilerParams(vmem_limit_bytes=megabytes * 1024 * 1024),
        cost_estimate=pl.CostEstimate(flops=flops, bytes_accessed=1000, transcendentals=0),
    )


def weight_halves(pairs, bit, block, most, after=()):
    args = [a for left, right, _, _ in pairs for a in (left, right)]
    cuts = [(low, high) for _, _, low, high in pairs]
    rows, model = pairs[0][0].shape
    width = sum(high - low for low, high in cuts)
    pieces = pieces_of(width, most)
    outs = [(model // 2, high - low) for low, high in pieces] * 2

    def wrapped(bit_ref, *refs):
        grad_kernel(cuts, pieces, block, bit_ref, *refs[: len(args)], *refs[len(args) + len(after) :])

    outs = pl.pallas_call(
        wrapped,
        out_shape=[jax.ShapeDtypeStruct(s, bf16) for s in outs],
        in_specs=[pl.BlockSpec(memory_space=pltpu.SMEM)] + [pl.BlockSpec(memory_space=pltpu.HBM)] * (len(args) + len(after)),
        out_specs=[pl.BlockSpec(memory_space=pltpu.HBM)] * len(outs),
        scratch_shapes=[pltpu.VMEM(a.shape, a.dtype) for a in args]
        + [
            pltpu.VMEM((model, rows), bf16), pltpu.VMEM((2, model // 2, width), bf16),
            pltpu.SemaphoreType.DMA((len(args),)), pltpu.SemaphoreType.DMA((len(pieces),)),
            pltpu.SemaphoreType.DMA((len(pieces),)),
        ],
        **plain_params(),
    )(bit, *args, *after)
    return outs[: len(pieces)], outs[len(pieces) :]


def step_kernel(pieces, sources, block, small, which_ref, *refs):
    arrays, refs = refs[: 2 * sources], refs[2 * sources :]
    if small:
        small_own, small_other, refs = refs[0], refs[1], refs[2:]
    away, mine, refs = refs[0], refs[1], refs[2:]
    if small:
        small_ref, refs = refs[0], refs[1:]
    kept_buf, arrived_buf, away_buf, mine_buf, kept_sems, arrived_sems, away_sems, mine_sems = refs
    which = which_ref[0]
    ins, outs = [], []
    for k, (source, low, at, width) in enumerate(pieces):
        cols, here = pl.ds(low, width), pl.ds(at, width)
        ins.append(pltpu.make_async_copy(arrays[2 * source].at[:, cols], kept_buf.at[:, here], kept_sems.at[k]))
        ins.append(pltpu.make_async_copy(arrays[2 * source + 1].at[:, cols], arrived_buf.at[:, here], arrived_sems.at[k]))
        ins[-2].start()
        ins[-1].start()
    if small:
        small_ref[...] = small_own[...] + small_other[...]
    for k, (source, low, at, width) in enumerate(pieces):
        ins[2 * k].wait()
        ins[2 * k + 1].wait()
        here = pl.ds(at, width)
        for out, target, sems, side in ((away_buf, away, away_sems, 1 - which), (mine_buf, mine, mine_sems, which)):
            for i in range(kept_buf.shape[0] // (2 * block)):
                rows = pl.ds(pl.multiple_of((2 * i + side) * block, block), block)
                total = kept_buf[rows, at : at + width].astype(f32) + arrived_buf[rows, at : at + width].astype(f32)
                out[i * block : (i + 1) * block, at : at + width] = total.astype(bf16)
            outs.append(pltpu.make_async_copy(out.at[:, here], target.at[:, here], sems.at[k]))
            outs[-1].start()
    for copy in outs:
        copy.wait()


def step_call(which, sources, block, after, small=()):
    rows = sources[0][0].shape[0]
    pieces, at = [], 0
    for i, (kept, _) in enumerate(sources):
        for low, high in pieces_of(kept.shape[1], 512):
            pieces.append((i, low, at + low, high - low))
        at += kept.shape[1]
    args = [a for pair in sources for a in pair]

    def wrapped(which_ref, *refs):
        used = len(args) + len(small)
        step_kernel(pieces, len(sources), block, bool(small), which_ref, *refs[:used], *refs[used + len(after) :])

    half = (rows // 2, at)
    anywhere = pl.BlockSpec(memory_space=pltpu.HBM)
    inside = pl.BlockSpec(memory_space=pltpu.VMEM)
    return pl.pallas_call(
        wrapped,
        out_shape=[jax.ShapeDtypeStruct(half, bf16)] * 2 + [jax.ShapeDtypeStruct(a.shape, f32) for a in small[:1]],
        in_specs=[pl.BlockSpec(memory_space=pltpu.SMEM)] + [anywhere] * len(args) + [inside] * len(small)
        + [anywhere] * len(after),
        out_specs=[anywhere] * 2 + [inside] * len(small[:1]),
        scratch_shapes=[pltpu.VMEM((rows, at), bf16)] * 2
        + [pltpu.VMEM(half, bf16)] * 2
        + [pltpu.SemaphoreType.DMA((len(pieces),))] * 4,
        **plain_params(),
    )(which, *args, *small, *after)


def shared_kernel(wp, own_ref, other_ref, out_ref):
    row = lax.broadcasted_iota(jnp.int32, own_ref.shape, 0)
    lane = lax.broadcasted_iota(jnp.int32, own_ref.shape, 1)
    shared = (row < 2) | ((row < 6) & (lane >= wp) & (lane < wp + 256))
    out_ref[...] = own_ref[...] + jnp.where(shared, other_ref[...], 0.0)


class Fetched:
    def __init__(self, source, held, sem):
        self.held, self.copy, self.ready = held, pltpu.make_async_copy(source, held, sem), False
        self.shape, self.dtype = held.shape, held.dtype
        self.copy.start()

    def __getitem__(self, key):
        if not self.ready:
            self.copy.wait()
            self.ready = True
        return self.held[key]


class Stored:
    def __init__(self, held, target, sem):
        self.held, self.copy, self.sent = held, pltpu.make_async_copy(held, target, sem), False
        self.shape, self.dtype = held.shape, held.dtype

    def __getitem__(self, key):
        return self.held[key]

    def __setitem__(self, key, value):
        self.held[key] = value

    def finish(self):
        if not self.sent:
            self.copy.start()
            self.sent = True


LARGE = 1 << 16
COST_US = 1100000000


def finish(*refs):
    for ref in refs:
        if isinstance(ref, Stored):
            ref.finish()


def call(kernel, outs, scratch, args, scalars=0, after=(), flops=1000):
    count = len(args)
    large_in = [i >= scalars and a.size * a.dtype.itemsize >= LARGE for i, a in enumerate(args)]
    large_out = [s[0] * s[1] * jnp.dtype(t).itemsize >= LARGE for s, t in outs]
    buffers = [pltpu.VMEM(a.shape, a.dtype) for a, big in zip(args, large_in) if big]
    buffers += [pltpu.VMEM(s, t) for (s, t), big in zip(outs, large_out) if big]
    copies = len(buffers)

    def wrapped(*refs):
        ins, rest = list(refs[:count]), refs[count + len(after) :]
        results, rest = list(rest[: len(outs)]), rest[len(outs) :]
        held, sems, inner = rest[:copies], rest[copies], rest[copies + 1 :]
        slot = 0
        for i, big in enumerate(large_in):
            if big:
                ins[i] = Fetched(ins[i], held[slot], sems.at[slot])
                slot += 1
        for i, big in enumerate(large_out):
            if big:
                results[i] = Stored(held[slot], results[i], sems.at[slot])
                slot += 1
        kernel(*ins, *results, *inner)
        finish(*results)
        for ref in ins:
            if isinstance(ref, Fetched) and not ref.ready:
                ref.copy.wait()
        for ref in results:
            if isinstance(ref, Stored):
                ref.copy.wait()

    spaces = [pltpu.SMEM] * scalars + [pltpu.HBM if big else pltpu.VMEM for big in large_in[scalars:]] + [pltpu.HBM] * len(after)
    return pl.pallas_call(
        wrapped,
        out_shape=[jax.ShapeDtypeStruct(s, t) for s, t in outs],
        in_specs=[pl.BlockSpec(memory_space=space) for space in spaces],
        out_specs=[pl.BlockSpec(memory_space=pltpu.HBM if big else pltpu.VMEM) for big in large_out],
        scratch_shapes=buffers + [pltpu.SemaphoreType.DMA((max(copies, 1),))] + [pltpu.VMEM(s, t) for s, t in scratch],
        **plain_params(flops),
    )(*args, *after)


def swap(values):
    return lax.ppermute(values, "tensor", [(0, 1), (1, 0)])


def gather_rows(values, me, count):
    if count != 2:
        return lax.all_gather(values, "tensor", axis=0, tiled=True)
    other = swap(values)
    first = jnp.where(me == 0, values, other)
    return jnp.concatenate([first, jnp.where(me == 0, other, values)], axis=0)


def both_parts(part, count):
    if count != 2:
        return (lax.psum(part, "tensor"), jnp.zeros_like(part))
    return (part, swap(part))


def scatter_rows(part, me, count):
    if count != 2:
        return lax.psum_scatter(part, "tensor", scatter_dimension=0, tiled=True).astype(f32)
    halves = part.reshape(2, part.shape[0] // 2, part.shape[1])
    arrived = swap(lax.dynamic_index_in_dim(halves, 1 - me, 0, keepdims=False))
    return lax.dynamic_index_in_dim(halves, me, 0, keepdims=False).astype(f32) + arrived.astype(f32)


def partners(count, bit):
    return [(i, i ^ bit) for i in range(count)]


def exchange(sent, count, bit):
    return lax.ppermute(sent, "dp", partners(count, bit))


class Reduction:
    def __init__(self, parts, index, count, block, bit=1, small=None):
        self.parts, self.index, self.count, self.block, self.bit = parts, index, count, block, bit
        self.small = small
        self.small_arrived = None if small is None else exchange(small, count, bit)

    def done(self):
        return self.bit * 2 >= self.count

    def step(self, after=()):
        if self.done():
            return after
        self.bit *= 2
        which = ((self.index // self.bit) % 2).astype(jnp.int32).reshape(1)
        small = () if self.small is None else (self.small, self.small_arrived)
        sent, kept, *small = step_call(which, self.parts, self.block, after, small)
        self.parts = [(kept, exchange(sent, self.count, self.bit))]
        if small:
            self.small = small[0]
            self.small_arrived = exchange(self.small, self.count, self.bit)
        return (sent,)

    def total(self, after):
        totals = []
        for kept, arrived in self.parts:
            if self.bit > 1:
                arrived = lax.optimization_barrier((arrived, after[0]))[0]
            totals.append(kept.astype(f32) + arrived.astype(f32))
        return totals[0] if len(totals) == 1 else jnp.concatenate(totals, axis=1)


def segments(lengths, row_count):
    seq_ends = jnp.cumsum(lengths)
    places = jnp.arange(row_count, dtype=jnp.int32)
    passed = places[:, None] >= seq_ends[None, :]
    seq_ids = jnp.sum(passed.astype(jnp.int32), axis=1)
    starts = jnp.max(jnp.where(passed, seq_ends[None, :], 0), axis=1)
    is_live = (places < seq_ends[-1]).astype(f32)
    return (seq_ids, places - starts, is_live)


def body(
    dp_count, tensor_count, tokens, cotangent, seq_lengths, norm1_gain, norm2_gain, mixer_in, state_in, step_in,
    conv_inner, conv_state, step_bias, decay_log, skip_gain, mixer_out, query_in, key_value, attend_out, gate_up,
    down_out,
):
    share, model = tokens.shape
    rows = share * tensor_count
    me = lax.axis_index("tensor")
    index = lax.axis_index("dp")
    inner = mixer_in.shape[2]
    heads = step_in.shape[1]
    query_width = query_in.shape[1]
    qheads = query_width // HD
    wp, qwp = padded(inner), padded(query_width)
    span = min(LANES, rows)
    dims = (heads, qheads, wp, qwp, span)

    if tensor_count == 2:
        x_own, x_other = tokens, swap(tokens)
    else:
        x_own = x_other = gather_rows(tokens, me, tensor_count)
    place = jnp.stack([me, lax.rem(me + 1, tensor_count)]).astype(jnp.int32)
    seq_ids, positions, is_live = segments(seq_lengths[0], rows)
    live_share = lax.dynamic_slice_in_dim(is_live, me * share, share, 0)[:, None]
    dout_rows = gather_rows(lax.optimization_barrier((cotangent, x_other))[0], me, tensor_count)
    dout_rows = dout_rows * is_live[:, None].astype(bf16)

    seq_col = seq_ids.astype(f32)[:, None]
    seq_row = seq_ids.astype(f32)[None, :]
    shifts = jnp.minimum(jnp.arange(LANES, dtype=jnp.int32), 4)[None, :]
    masks = (positions[:, None] >= shifts).astype(f32)
    lane = jnp.arange(LANES)
    frequency = rope_base ** (-2.0 * (lane % (HD // 2)).astype(f32) / HD)
    angles = positions.astype(f32)[:, None] * frequency[None, :]
    cosine = jnp.cos(angles)
    sine = jnp.sin(angles) * jnp.where(lane % HD < HD // 2, -1.0, 1.0)[None, :]

    key_index = me * qheads // (QH // KVH)
    pair_local = lax.dynamic_slice_in_dim(key_value, key_index * HD, HD, 2).reshape(model, 2 * HD)
    if inner == wp:
        wzx = mixer_in.reshape(model, 2 * inner)
    else:
        wzx = pad_to(mixer_in, wp).reshape(model, 2 * wp)
    wsp = jnp.concatenate([pad_to(step_in, LANES), pair_local], axis=1)
    wq, wmix, watt = pad_to(query_in, qwp), pad_to(mixer_out, wp), pad_to(attend_out, qwp)
    taps = pad_to(conv_inner, wp)
    bias = pad_to(step_bias[None], LANES)
    rate = pad_to(jnp.exp(decay_log)[None], LANES)
    skip = pad_to(jnp.repeat(skip_gain, HD)[None], wp)
    gain1, gain2 = norm1_gain[None], norm2_gain[None]

    x_rows, act, pa, pb, y, cat, part = call(
        functools.partial(front_kernel, dims),
        [
            ((rows, model), bf16), ((rows, model), bf16), ((rows, wp + qwp + LANES), f32), ((rows, wp + 384), f32),
            ((rows, wp), f32), ((rows, wp + qwp), bf16), ((rows, model), bf16),
        ],
        [((rows, rows), f32), ((rows, rows), f32), ((rows, LANES), bf16)],
        (
            place, x_own, x_other, state_in, wsp, wzx, wq, wmix, watt, gain1, seq_col, seq_row, masks, cosine, sine, taps,
            conv_state, bias, rate, skip,
        ),
        1, (), 10 * COST_US,
    )
    own, other = both_parts(part, tensor_count)
    wgu = lax.optimization_barrier((gate_up, part))[0].reshape(model, -1)
    dhidden = mm(dout_rows, down_out)
    ff2 = wgu.shape[1]
    h1, n2, hidden, dgu, ffn_part, dn2_part = call(
        middle_kernel,
        [
            ((rows, model), f32), ((rows, model), bf16), ((rows, ff2 // 2), bf16), ((rows, ff2), bf16),
            ((rows, model), bf16), ((rows, model), bf16),
        ],
        [],
        (x_rows, own, other, gain2, wgu, down_out, dhidden),
    )
    dn2_own, dn2_other = both_parts(dn2_part, tensor_count)

    bit = (index % 2).astype(jnp.int32).reshape(1)
    block = model // dp_count

    def reduction(pairs, most, after=(), small=None):
        sent, kept = weight_halves(pairs, bit, block, most, after)
        parts = [(stay, exchange(go, dp_count, 1)) for go, stay in zip(sent, kept)]
        return Reduction(parts, index, dp_count, block, 1, small)

    most = max(LANES, ff2 * 5 // 16 // LANES * LANES)
    cut = ff2 - ff2 // 4
    ffn = reduction([(dout_rows, hidden, 0, ff2 // 2), (n2, dgu, 0, cut)], most)
    order = ffn.step()

    dh1_share, ffn_send, dmix, dy, da, gn2 = call(
        functools.partial(attend_back_kernel, dims, share),
        [
            ((share, model), f32), ((share, model), bf16), ((rows, model), bf16), ((rows, wp), f32),
            ((rows, wp + qwp + LANES), bf16), ((1, model), f32),
        ],
        [((rows, rows), f32), ((rows, model), f32), ((rows, qwp), bf16), ((rows, LANES), f32), ((rows, LANES), f32)],
        (
            place, dn2_own, dn2_other, ffn_part, h1, dout_rows, gain2, wmix, watt, seq_col, seq_row, cosine, sine, pa, y,
        ),
        1, order, 40 * COST_US,
    )
    mix_out = reduction([(dmix, cat, 0, wp + qwp), (n2, dgu, cut, ff2)], 512)
    mix_a = reduction([(act, da, 0, wp + qwp + LANES)], 2048, (mix_out.parts[0][0],))
    order = ffn.step((mix_a.parts[0][0],))
    order = mix_out.step(order)
    ffn_arrived = swap(ffn_send) if tensor_count == 2 else ffn_send

    dxb, dact, dact_send, small = call(
        functools.partial(mixer_back_kernel, dims, share),
        [((rows, wp + 384), bf16), ((rows, model), bf16), ((share, model), bf16), ((8, model), f32)],
        [
            ((rows, rows), f32), ((rows, rows), f32), ((rows, rows), f32), ((rows, wp), f32), ((rows, wp), f32),
        ],
        (
            place, pb, dy, y, wzx, state_in, wsp, da, wq, x_rows, seq_col, seq_row, masks, taps, conv_state, bias, rate,
            skip, gn2,
        ),
        1, order + (ffn_arrived,), 40 * COST_US,
    )
    if tensor_count == 2:
        summed = swap(small)
    else:
        summed = lax.psum(small, "tensor") - small
    small = call(functools.partial(shared_kernel, wp), [((8, model), f32)], [], (small, summed))[0]
    order = ffn.step((dxb,))
    mix_b = reduction([(act, dxb, 0, wp + 384)], 384, order, small)
    order = mix_a.step((mix_b.parts[0][0],))
    order = mix_out.step(order)
    order = mix_b.step(order)
    ffn_total = ffn.total(order) if ffn.done() else None
    order = mix_a.step(order if ffn_total is None else order + (ffn_total,))
    order = mix_out.step(order)
    if tensor_count == 2:
        dact_mine = lax.dynamic_slice_in_dim(dact, me * share, share, 0).astype(f32)
        dact_share = dact_mine + lax.optimization_barrier((swap(dact_send), order[0]))[0].astype(f32)
    else:
        dact_share = scatter_rows(dact, me, tensor_count)
    for r in [mix_b, mix_a] + 4 * [ffn, mix_out, mix_a]:
        order = r.step(order)
    out_total = mix_out.total(order)
    while not mix_b.done():
        order = mix_b.step(order)
    if ffn_total is None:
        ffn_total = ffn.total(order)
    first_total = mix_a.total(order)
    down_total = ffn_total[:, : ff2 // 2]
    up_total = jnp.concatenate([ffn_total[:, ff2 // 2 :], out_total[:, wp + qwp :]], axis=1)
    mix_b, minor = mix_b.total(order), mix_b.small + mix_b.small_arrived
    second_total, state_total = mix_b[:, :wp], mix_b[:, wp : wp + 256]
    step_total = mix_b[:, wp + 256 :]

    if tensor_count == 2:
        ffn_mine = lax.dynamic_slice_in_dim(ffn_part, me * share, share, 0).astype(f32)
        ffn_share = ffn_mine + ffn_arrived.astype(f32)
    else:
        ffn_share = scatter_rows(ffn_part, me, tensor_count)
    h1_share = lax.dynamic_slice_in_dim(h1, me * share, share, 0)
    block_out = ((h1_share + ffn_share) * live_share).astype(bf16)

    x_share = tokens.astype(f32)
    r1 = lax.rsqrt(jnp.mean(x_share * x_share, axis=-1, keepdims=True) + norm_eps)
    u = dact_share * gain1
    token_grad = dh1_share + r1 * u - x_share * (r1 * r1 * r1 * jnp.mean(u * x_share, axis=-1, keepdims=True))

    g_norm1, g_norm2, g_conv_state = minor[0], minor[1], minor[2:6, wp : wp + 256]
    g_conv_inner = minor[2:6, :inner]
    g_skip = jnp.sum(minor[6, :wp].reshape(-1, HD), axis=1)[:heads]
    g_bias = minor[6, wp : wp + heads]
    g_decay = minor[6, wp + LANES : wp + LANES + heads]

    both = jnp.concatenate([state_total, first_total[:, wp + qwp :]], axis=1).astype(bf16)
    placed = lambda pair: lax.dynamic_update_slice_in_dim(
        jnp.zeros((block,) + key_value.shape[1:], f32), pair.astype(f32).reshape(block, 2, HD), key_index * HD, 2
    )
    if tensor_count == 2:
        arrived = swap(both)
        g_state = both[:, :256].astype(f32) + arrived[:, :256].astype(f32)
        mine = both[:, 256:].reshape(block, 2, HD)
        theirs = arrived[:, 256:].reshape(block, 2, HD)
        g_pair = jnp.concatenate(
            [jnp.where(me == 0, mine, theirs), jnp.where(me == 0, theirs, mine)], axis=2
        ).astype(f32)
    else:
        g_state = lax.psum(both[:, :256], "tensor").astype(f32)
        g_pair = lax.psum(placed(both[:, 256:]).astype(bf16), "tensor").astype(f32)

    g_mixer_in = jnp.stack([first_total[:, :inner], second_total[:, :inner]], axis=1)
    return (
        block_out,
        token_grad.astype(bf16),
        g_norm1,
        g_norm2,
        g_mixer_in,
        g_state,
        step_total[:, :heads],
        g_conv_inner,
        g_conv_state,
        g_bias,
        g_decay,
        g_skip,
        out_total[:, :inner],
        first_total[:, wp : wp + query_width],
        g_pair,
        out_total[:, wp : wp + query_width],
        up_total.reshape(block, 2, ff2 // 2),
        down_total,
    )


def solution(mesh):
    return jax.shard_map(
        functools.partial(body, mesh.shape["dp"], mesh.shape["tensor"]),
        mesh=mesh,
        in_specs=(
            P(("dp", "tensor"), None),
            P(("dp", "tensor"), None),
            P("dp", None),
            P(),
            P(),
            P(None, None, "tensor"),
            P(),
            P(None, "tensor"),
            P(None, "tensor"),
            P(),
            P("tensor"),
            P("tensor"),
            P("tensor"),
            P(None, "tensor"),
            P(None, "tensor"),
            P(),
            P(None, "tensor"),
            P(None, None, "tensor"),
            P(None, "tensor"),
        ),
        out_specs=(
            P(("dp", "tensor"), None),
            P(("dp", "tensor"), None),
            P(),
            P(),
            P("dp", None, "tensor"),
            P("dp", None),
            P("dp", "tensor"),
            P(None, "tensor"),
            P(),
            P("tensor"),
            P("tensor"),
            P("tensor"),
            P("dp", "tensor"),
            P("dp", "tensor"),
            P("dp", None, None),
            P("dp", "tensor"),
            P("dp", None, "tensor"),
            P("dp", "tensor"),
        ),
        check_vma=False,
    )
```
